32 devices in a mesh: dp: 16 (over z, x, core), mp: 2 (over y).
Axes of the slice: x: 2, y: 2, z: 4, core: 2. Of those that a mesh axis runs over, the one named last changes fastest.
Arguments:
- hidden_in: bfloat16 [16, 1024, 768], P('dp'), may hold values from -6 to 6, as said below
- segment_ids: int32 [16, 1024], P('dp'), may hold values from 0 to 7, as said below
- time_mask: int32 [16, 1024], P('dp'), may hold values 0 or 1
- mask_embed: bfloat16 [768], replicated, may hold values from -4 to 4
- conv_weight: bfloat16 [6144, 768], P('dp', 'mp'), may hold values from -0.078125 to 0.078125
- conv_bias: bfloat16 [768], P('mp'), may hold values from -3 to 3
- query_weight: bfloat16 [768, 768], P('dp', 'mp'), may hold values from -0.21875 to 0.21875
- key_weight: bfloat16 [768, 768], P('dp', 'mp'), may hold values from -0.21875 to 0.21875
- value_weight: bfloat16 [768, 768], P('dp', 'mp'), may hold values from -0.21875 to 0.21875
- query_bias: bfloat16 [768], P('mp'), may hold values from -3 to 3
- value_bias: bfloat16 [768], P('mp'), may hold values from -3 to 3
- out_weight: bfloat16 [768, 768], P('mp', 'dp'), may hold values from -1.75 to 1.75
- out_bias: bfloat16 [768], replicated, may hold values from -3 to 3
- first_gain: bfloat16 [768], replicated, may hold values from 0.099609375 to 1.8984375
- first_shift: bfloat16 [768], replicated, may hold values from -3 to 3
- up_weight: bfloat16 [768, 3072], P('dp', 'mp'), may hold values from -0.21875 to 0.21875
- up_bias: bfloat16 [3072], P('mp'), may hold values from -3 to 3
- down_weight: bfloat16 [3072, 768], P('mp', 'dp'), may hold values from -0.109375 to 0.109375
- down_bias: bfloat16 [768], replicated, may hold values from -3 to 3
- second_gain: bfloat16 [768], replicated, may hold values from 0.099609375 to 1.8984375
- second_shift: bfloat16 [768], replicated, may hold values from -3 to 3
- cotangent: bfloat16 [16, 1024, 768], P('dp'), may hold values from -6 to 6
Outputs:
- layer_out: bfloat16 [16, 1024, 768], P('dp')
- input_grad: float32 [16, 1024, 768], P('dp', None, 'mp')
- mask_grad: float32 [768], P('mp')
- conv_grad: float32 [6144, 768], P('dp', 'mp')
- conv_bias_grad: float32 [768], P('mp')
- query_grad: float32 [768, 768], P('dp', 'mp')
- key_grad: float32 [768, 768], P('dp', 'mp')
- value_grad: float32 [768, 768], P('dp', 'mp')
- query_bias_grad: float32 [768], P('mp')
- value_bias_grad: float32 [768], P('mp')
- out_grad: float32 [768, 768], P('mp', 'dp')
- out_bias_grad: float32 [768], replicated
- first_gain_grad: float32 [768], replicated
- first_shift_grad: float32 [768], replicated
- up_grad: float32 [768, 3072], P('dp', 'mp')
- up_bias_grad: float32 [3072], P('mp')
- down_grad: float32 [3072, 768], P('mp', 'dp')
- down_bias_grad: float32 [768], replicated
- second_gain_grad: float32 [768], replicated
- second_shift_grad: float32 [768], replicated
- stream_rms: float32 [4], replicated
The draws below stay inside these ranges and needn't reach their ends.
Inputs may be any that keep to these rules, and one draw needn't show every extreme that they name: `hidden_in`: scaled by a factor per packed row; rows later in the array are larger. `segment_ids`: along a row the ids never fall until the padding (id 0), which fills the end of the row; a row starts with id 1 and holds fewer than 512 padding frames.
All inputs are finite; a program needn't handle non-finite values. No bound on the sum of `time_mask` on one device may be relied on, other than what follows from the above.
Results may differ from the reference program's by a relative error of at most 0.02.
Values may be sent and summed in bfloat16 or wider, within the bound.
A program may use at most 192 MiB of HBM per device.

```python
import jax
import jax.numpy as jnp
from jax import lax

D = 768
HEADS = 12
HD = 64
FF = 3072
KW = 128
GROUPS = 16
CG = 48
LEN = 1024
SEQS = 16
N_MP = 2


def draw_hidden_in(key, part):
    key_one = jax.random.fold_in(jax.random.fold_in(key, 11), 0)
    row_ramp = 0.5 + jnp.arange(SEQS, dtype=jnp.float32) / max(SEQS - 1, 1)
    values = jnp.clip(jax.random.normal(key_one, (SEQS, LEN, D), jnp.float32), -4.0, 4.0)
    return (values * row_ramp[:, None, None]).astype(jnp.bfloat16)


def draw_segment_ids(key, part):
    key_one, key_two = jax.random.split(jax.random.fold_in(key, 23))
    cut_points = jax.random.randint(key_one, (SEQS, 6), 1, LEN)
    pad_count = jax.random.randint(key_two, (SEQS, 1), 0, LEN // 2)
    position = jnp.arange(LEN, dtype=jnp.int32)
    segment = 1 + jnp.sum((position[None, None, :] >= cut_points[:, :, None]).astype(jnp.int32), axis=1)
    return jnp.where(position[None, :] >= LEN - pad_count, 0, segment).astype(jnp.int32)


def with_ends(result, own_key, smallest, largest):
    place = [jax.random.randint(jax.random.fold_in(own_key, axis), (), 0, length) for axis, length in enumerate(result.shape)]
    longest = result.shape.index(max(result.shape))
    beside = place[:longest] + [(place[longest] + 1) % result.shape[longest]] + place[longest + 1:]
    return result.at[tuple(place)].set(smallest).at[tuple(beside)].set(largest)


def block_levels(key, shape, pieces, low, top_value):
    loudness = 1.0
    for axis_at, blocks in pieces:
        draws = jax.random.uniform(jax.random.fold_in(jax.random.fold_in(key, 6), axis_at), (blocks,), jnp.float32, low / len(pieces), top_value / len(pieces))
        loudness = loudness * jnp.repeat(jnp.exp(draws), shape[axis_at] // blocks).reshape((-1,) + (1,) * (len(shape) - 1 - axis_at))
    return loudness


def scatter_about(rng, shape, scale, most, shards=(), kind=jnp.bfloat16):
    loudness = block_levels(rng, shape, shards, -0.22, 0.18) if shards else 1.0
    drawn = jax.random.normal(rng, shape, jnp.float32) * scale * loudness
    return jnp.minimum(jnp.maximum(drawn, -most), most).astype(kind)


def setup_inputs(seed: int = 0) -> dict:
    key_list = jax.random.split(jax.random.key(seed), 23)
    hidden_in = draw_hidden_in(jax.random.fold_in(key_list[22], 71), 0)
    segment_ids = draw_segment_ids(jax.random.fold_in(key_list[22], 71), 0)
    time_mask = with_ends((jax.random.randint(key_list[2], (SEQS, LEN), 0, 2) < 1).astype(jnp.int32), jax.random.fold_in(key_list[2], 1), 0, 1)
    mask_embed = scatter_about(key_list[3], (D,), 1.0, 4.0)
    conv_weight = scatter_about(key_list[4], (KW * CG, D), (KW * CG) ** -0.5, 0.078125, ((0, 16), (1, 2)))
    conv_bias = scatter_about(key_list[5], (D,), 0.5, 3.0, ((0, 2),))
    query_weight = scatter_about(key_list[6], (D, D), D ** -0.5, 0.21875, ((0, 16), (1, 2)))
    key_weight = scatter_about(key_list[7], (D, D), D ** -0.5, 0.21875, ((0, 16), (1, 2)))
    value_weight = scatter_about(key_list[8], (D, D), D ** -0.5, 0.21875, ((0, 16), (1, 2)))
    query_bias = scatter_about(key_list[9], (D,), 0.5, 3.0, ((0, 2),))
    value_bias = scatter_about(key_list[10], (D,), 0.5, 3.0, ((0, 2),))
    out_weight = scatter_about(key_list[11], (D, D), (D // 64) ** -0.5, 1.75, ((0, 2), (1, 16)))
    out_bias = scatter_about(key_list[12], (D,), 0.5, 3.0)
    first_gain = jnp.clip(1.0 + 0.18 * jax.random.normal(key_list[13], (D,), jnp.float32), 0.099609375, 1.8984375).astype(jnp.bfloat16)
    first_shift = scatter_about(key_list[14], (D,), 0.5, 3.0)
    up_weight = scatter_about(key_list[15], (D, FF), D ** -0.5, 0.21875, ((0, 16), (1, 2)))
    up_bias = scatter_about(key_list[16], (FF,), 0.5, 3.0, ((0, 2),))
    down_weight = scatter_about(key_list[17], (FF, D), FF ** -0.5, 0.109375, ((0, 2), (1, 16)))
    down_bias = scatter_about(key_list[18], (D,), 0.5, 3.0)
    second_gain = jnp.clip(1.0 + 0.18 * jax.random.normal(key_list[19], (D,), jnp.float32), 0.099609375, 1.8984375).astype(jnp.bfloat16)
    second_shift = scatter_about(key_list[20], (D,), 0.5, 3.0)
    cotangent = scatter_about(key_list[21], (SEQS, LEN, D), 1.0, 6.0, ((0, 16),))
    return dict(hidden_in=hidden_in, segment_ids=segment_ids, time_mask=time_mask, mask_embed=mask_embed, conv_weight=conv_weight, conv_bias=conv_bias, query_weight=query_weight, key_weight=key_weight, value_weight=value_weight, query_bias=query_bias, value_bias=value_bias, out_weight=out_weight, out_bias=out_bias, first_gain=first_gain, first_shift=first_shift, up_weight=up_weight, up_bias=up_bias, down_weight=down_weight, down_bias=down_bias, second_gain=second_gain, second_shift=second_shift, cotangent=cotangent)


highest = lax.Precision.HIGHEST
norm_eps = 1e-05

@jax.custom_vjp
def low(v):
    return lax.optimization_barrier(v.astype(jnp.bfloat16)).astype(jnp.float32)

@jax.custom_vjp
def low_back(v):
    return v

def low_keep(v):
    return (low(v), None)

def low_pass(kept, grad):
    return (grad,)

def back_keep(v):
    return (v, None)

def back_low(kept, grad):
    return (low(grad),)
low.defvjp(low_keep, low_pass)
low_back.defvjp(back_keep, back_low)

def exact_gelu(values):
    return jax.nn.gelu(values, approximate=False)

def layer_norm(rows, gain, shift):
    centre = rows - lax.optimization_barrier(jnp.mean(rows, axis=-1, keepdims=True))
    spread = lax.optimization_barrier(jnp.mean(centre * centre, axis=-1, keepdims=True))
    return centre * lax.rsqrt(spread + norm_eps) * gain + shift

def matmul(left, right):
    return jnp.dot(left, right, precision=highest)

def masked_conv(start_low, seg_row, kernel_flat):
    kernel = kernel_flat.reshape(KW, CG, GROUPS, CG)
    grouped = start_low.reshape(LEN, GROUPS, CG)
    half_kernel = KW // 2
    padded = jnp.pad(grouped, ((half_kernel, half_kernel), (0, 0), (0, 0)))
    seg_pad = jnp.pad(seg_row, (half_kernel, half_kernel), constant_values=-1)

    def one_tap(total, tap_index):
        window = lax.dynamic_slice_in_dim(padded, tap_index, LEN, 0)
        neighbour = lax.dynamic_slice_in_dim(seg_pad, tap_index, LEN, 0)
        keep_mask = (neighbour == seg_row).astype(window.dtype)
        taps_now = lax.dynamic_index_in_dim(kernel, tap_index, 0, keepdims=False)
        total = total + jnp.einsum('tgi,igo->tgo', window * keep_mask[:, None, None], taps_now, precision=highest)
        return (total, None)
    total, _ = lax.scan(one_tap, jnp.zeros((LEN, GROUPS, CG), start_low.dtype), jnp.arange(KW, dtype=jnp.int32))
    return total.reshape(LEN, D)

def split_product(left, right, inner):
    part_width = inner // N_MP
    total = jnp.zeros((left.shape[0], right.shape[1]), left.dtype)
    for piece in range(N_MP):
        total = total + low(matmul(left[:, piece * part_width:(piece + 1) * part_width], right[piece * part_width:(piece + 1) * part_width]))
    return total

def row_forward(params, row_in, seg_row, mask_row):
    mask_embed, conv_weight, conv_bias, query_weight, key_weight, value_weight, query_bias, value_bias, out_weight, out_bias, first_gain, first_shift, up_weight, up_bias, down_weight, down_bias, second_gain, second_shift = params
    valid = (seg_row != 0).astype(row_in.dtype)[:, None]
    masked = mask_row.astype(row_in.dtype)[:, None]
    start_in = row_in + masked * (mask_embed - row_in)
    start_low = low(start_in)
    conv_pre = low_back(masked_conv(start_low, seg_row, conv_weight) + conv_bias)
    branch_conv = low(valid * exact_gelu(conv_pre))
    mixed = start_in + branch_conv
    mixed_low = low(mixed)
    queries = low(low_back(matmul(mixed_low, query_weight) + query_bias)).reshape(LEN, HEADS, HD)
    keys_all = low(low_back(matmul(mixed_low, key_weight))).reshape(LEN, HEADS, HD)
    values_all = low(low_back(matmul(mixed_low, value_weight) + value_bias)).reshape(LEN, HEADS, HD)
    scores = low_back(jnp.einsum('qhd,khd->hqk', queries, keys_all, precision=highest) * HD ** (-0.5))
    allowed = (seg_row[:, None] == seg_row[None, :])[None]
    scores = jnp.where(allowed, scores, -1000000000.0)
    probs = low(jax.nn.softmax(scores, axis=-1))
    context = jnp.einsum('hqk,khd->qhd', probs, values_all, precision=highest).reshape(LEN, D)
    context = low(low_back(valid * context))
    attn_out = low_back(out_bias + split_product(context, out_weight, D))
    normed_one = layer_norm(mixed + attn_out, first_gain, first_shift)
    normed_low = low(normed_one)
    hidden_pre = low_back(matmul(normed_low, up_weight) + up_bias)
    hidden = low(exact_gelu(hidden_pre))
    ffn_out = low_back(down_bias + split_product(hidden, down_weight, FF))
    normed_two = layer_norm(normed_one + ffn_out, second_gain, second_shift)
    final = valid * normed_two
    stats = jnp.stack([jnp.sum(valid * branch_conv * branch_conv), jnp.sum(valid * attn_out * attn_out), jnp.sum(valid * ffn_out * ffn_out), jnp.sum(final * final)])
    return (final, stats)

def reference(hidden_in, segment_ids, time_mask, mask_embed, conv_weight, conv_bias, query_weight, key_weight, value_weight, query_bias, value_bias, out_weight, out_bias, first_gain, first_shift, up_weight, up_bias, down_weight, down_bias, second_gain, second_shift, cotangent):
    params = tuple((item.astype(jnp.float32) for item in (mask_embed, conv_weight, conv_bias, query_weight, key_weight, value_weight, query_bias, value_bias, out_weight, out_bias, first_gain, first_shift, up_weight, up_bias, down_weight, down_bias, second_gain, second_shift)))
    inputs = hidden_in.astype(jnp.float32)

    def forward(frames, weights):

        def one_row(total, row_items):
            out_row, stats = jax.checkpoint(row_forward)(weights, row_items[0], row_items[1], row_items[2])
            return (total + stats, out_row)
        total, outs = lax.scan(one_row, jnp.zeros((4,), frames.dtype), (frames, segment_ids, time_mask))
        return (outs, total)
    (outs, total), pullback = jax.vjp(forward, inputs, params)
    input_grad, grads = pullback((cotangent.astype(jnp.float32), jnp.zeros_like(total)))
    count = jnp.sum((segment_ids != 0).astype(total.dtype))
    stream_rms = jnp.sqrt(total / (count * D))
    return (outs.astype(jnp.bfloat16), input_grad, grads[0], grads[1], grads[2], grads[3], grads[4], grads[5], grads[6], grads[7], grads[8], grads[9], grads[10], grads[11], grads[12], grads[13], grads[14], grads[15], grads[16], grads[17], stream_rms)
```

```python
import functools

import jax
import jax.numpy as jnp
from jax import lax
from jax.experimental import pallas as pl
from jax.experimental.pallas import tpu as pltpu
from jax.sharding import PartitionSpec as P

HD = 64
KW = 128
CG = 48
TAPS = 8
EPS = 1e-05
F32 = jnp.float32
BF16 = jnp.bfloat16
NN = (((1,), (0,)), ((), ()))
NT = (((1,), (1,)), ((), ()))
TN = (((0,), (0,)), ((), ()))
BOTH = ("dp", "mp")


def dg(a, b, dims):
    return lax.dot_general(a, b, dims, preferred_element_type=F32)


def gelu_parts(v):
    t = 1.0 / (1.0 + (0.3275911 * 0.7071067811865476) * jnp.abs(v))
    e = jnp.exp(-0.5 * v * v)
    poly = t * (0.254829592 + t * (-0.284496736 + t * (1.421413741 + t * (-1.453152027 + t * 1.061405429))))
    tail = 0.5 * poly * e
    return jnp.where(v >= 0, 1.0 - tail, tail), e


def gelu_and_slope(v):
    phi, e = gelu_parts(v)
    return v * phi, phi + v * e * 0.3989422804014327


def params(mb=56):
    return pltpu.CompilerParams(vmem_limit_bytes=mb * 2**20)


def vspec():
    return pl.BlockSpec(memory_space=pltpu.VMEM)


def call(kernel, outs, scratch, *args):
    return pl.pallas_call(
        kernel,
        out_shape=[jax.ShapeDtypeStruct(s, d) for s, d in outs],
        in_specs=[vspec()] * len(args),
        out_specs=[vspec()] * len(outs),
        scratch_shapes=[pltpu.VMEM(s, d) for s, d in scratch],
        compiler_params=params(),
    )(*args)


def split_low(v):
    hi = v.astype(BF16)
    return hi, (v - hi.astype(F32)).astype(BF16)


def spread_matrix(seg, length, width):
    rank = jnp.where(seg == 0, 7, seg - 1)
    pos = lax.broadcasted_iota(jnp.int32, (length, 1), 0) + 64 * rank + 8
    hit = pos == lax.broadcasted_iota(jnp.int32, (length, width), 1)
    return hit.astype(F32).astype(BF16)


def rolled(x, left):
    width = x.shape[1]
    left = left % width
    return x if left == 0 else pltpu.roll(x, width - left, 1)


def tap_patches(xg):
    return jnp.concatenate([rolled(xg, r) for r in range(TAPS)], axis=0)


def conv_fwd_kernel(seg_ref, x_ref, w_ref, b_ref, low_ref, slope_ref, spread, xq, y_ref, ot):
    length, width = spread.shape
    blocks = w_ref.shape[0]
    spread[...] = spread_matrix(seg_ref[...], length, width)
    xq[...] = dg(x_ref[...], spread[...], TN).astype(BF16)

    def body(g, carry):
        at = pl.ds(pl.multiple_of(g * CG, 16), CG)
        y_ref[...] = dg(w_ref[:, at, :].reshape(blocks * CG, TAPS * CG), tap_patches(xq[at, :]), NN)
        acc = rolled(y_ref[0:CG, :], -64)
        for b in range(1, blocks):
            acc = acc + rolled(y_ref[b * CG:(b + 1) * CG, :], TAPS * b - 64)
        ot[at, :] = acc
        return carry

    lax.fori_loop(0, x_ref.shape[1] // CG, body, 0)
    hi, lo = split_low(ot[...])
    pre = dg(spread[...], hi, NT) + dg(spread[...], lo, NT) + b_ref[...]
    valid = (seg_ref[...] != 0).astype(F32)
    value, slope = gelu_and_slope(pre)
    low_ref[...] = (valid * value).astype(BF16)
    slope_ref[...] = valid * slope


def conv_bwd_kernel(seg_ref, x_ref, w_ref, slope_ref, gm_ref, mask_ref, dw_ref, in_ref, db_ref, dm_ref,
                    spread, xq, dq, d_ref, gq):
    length, width = spread.shape
    blocks = w_ref.shape[0]
    spread[...] = spread_matrix(seg_ref[...], length, width)
    xq[...] = dg(x_ref[...], spread[...], TN).astype(BF16)
    dpre = (slope_ref[...] * gm_ref[...].astype(F32)).astype(BF16)
    db_ref[...] = jnp.sum(dpre.astype(F32), axis=0, keepdims=True)
    dq[...] = dg(dpre, spread[...], TN).astype(BF16)

    def body(g, carry):
        at = pl.ds(pl.multiple_of(g * CG, 16), CG)
        dqg = dq[at, :]
        for b in range(blocks):
            d_ref[b * CG:(b + 1) * CG, :] = rolled(dqg, 64 - TAPS * b)
        dmat = d_ref[...]
        dw = dg(dmat, tap_patches(xq[at, :]), NT)
        dw_ref[:, at, :] = dw.astype(dw_ref.dtype).reshape(blocks, CG, TAPS * CG)
        v = dg(w_ref[:, at, :].reshape(blocks * CG, TAPS * CG), dmat, TN)
        acc = v[0:CG, :]
        for r in range(1, TAPS):
            acc = acc + rolled(v[r * CG:(r + 1) * CG, :], -r)
        gq[at, :] = acc
        return carry

    lax.fori_loop(0, x_ref.shape[1] // CG, body, 0)
    hi, lo = split_low(gq[...])
    grad = dg(spread[...], hi, NT) + dg(spread[...], lo, NT) + gm_ref[...].astype(F32)
    masked = mask_ref[...].astype(F32)
    dm_ref[...] = jnp.sum(masked * grad, axis=0, keepdims=True)
    in_ref[...] = (1.0 - masked) * grad


def attn_fwd_kernel(hid_ref, c0_ref, c1_ref, mask_ref, segc_ref, segr_ref, emb_ref, w_ref, qb_ref, vb_ref,
                    mixed_ref, mlow_ref, qkv_ref, ctx_ref, lse_ref, part_ref, stat_ref, qt, vt, ot):
    rows, width = hid_ref.shape
    half = c0_ref.shape[1]
    heads = half // HD
    step = 256
    stat = jnp.zeros((1, half), F32)
    for i in range(rows // step):
        at = pl.ds(i * step, step)
        conv = jnp.concatenate([c0_ref[at, :].astype(F32), c1_ref[at, :].astype(F32)], axis=1)
        hid = hid_ref[at, :].astype(F32)
        masked = mask_ref[at, :].astype(F32)
        mixed = hid + masked * (emb_ref[...] - hid) + conv
        low = mixed.astype(BF16)
        mixed_ref[at, :] = mixed
        mlow_ref[at, :] = low
        stat = stat + jnp.sum(conv[:, :half] * conv[:, :half] + conv[:, half:] * conv[:, half:], axis=0, keepdims=True)
        qkv = dg(low, w_ref[:, :3 * half], NN)
        qkv_ref[at, 0:half] = (qkv[:, :half] + qb_ref[...]).astype(BF16)
        qkv_ref[at, half:2 * half] = qkv[:, half:2 * half].astype(BF16)
        qkv_ref[at, 2 * half:] = (qkv[:, 2 * half:] + vb_ref[...]).astype(BF16)
    stat_ref[...] = stat
    qt[...] = (qkv_ref[:, 0:half] * jnp.asarray(HD ** -0.5, BF16)).T
    vt[...] = qkv_ref[:, 2 * half:].T

    def pair_body(p, carry):
        lanes = pl.ds(pl.multiple_of(half + p * 128, 128), 128)
        k_pair = qkv_ref[:, lanes]
        for j in range(2):
            head_at = pl.ds(pl.multiple_of(p * 128 + j * HD, HD), HD)
            qh = qt[head_at, :]
            vh = vt[head_at, :]
            zero = jnp.zeros_like(qh)
            qz = jnp.concatenate([qh, zero] if j == 0 else [zero, qh], axis=0)
            for i in range(rows // step):
                at = slice(i * step, (i + 1) * step)
                s = dg(k_pair, qz[:, at], NN)
                s = jnp.where(segc_ref[...] == segr_ref[:, at], s, -1000000000.0)
                top = jnp.max(s, axis=0, keepdims=True)
                e = jnp.exp(s - top)
                den = jnp.sum(e, axis=0, keepdims=True)
                o = dg(vh, e.astype(BF16), NN) / den
                ot[head_at, at] = jnp.where(segr_ref[:, at] != 0, o, 0.0).astype(BF16)
                lse_ref[pl.ds(2 * p + j, 1), at] = top + jnp.log(den)
        return carry

    lax.fori_loop(0, heads // 2, pair_body, 0)
    ctx_ref[...] = ot[...].T
    part_ref[...] = dg(ctx_ref[...], w_ref[:, 3 * half:], NT).astype(BF16)


def norm_stats(x):
    centre = x - jnp.mean(x, axis=-1, keepdims=True)
    r = lax.rsqrt(jnp.mean(centre * centre, axis=-1, keepdims=True) + EPS)
    return centre * r, r


def ffn_fwd_kernel(mixed_ref, p0_ref, p1_ref, seg_ref, ob_ref, g1_ref, s1_ref, up_ref, ub_ref, dt_ref,
                   n1_ref, r1_ref, low_ref, hid_ref, slope_ref, part_ref, stat_ref):
    rows, width = mixed_ref.shape
    step = 256
    stat_ref[...] = jnp.zeros_like(stat_ref)

    def body(i, carry):
        at = pl.ds(pl.multiple_of(i * step, step), step)
        attn = ob_ref[...] + (p0_ref[at, :].astype(F32) + p1_ref[at, :].astype(F32))
        valid = (seg_ref[at, :] != 0).astype(F32)
        stat_ref[...] += jnp.sum(valid * attn * attn, axis=0, keepdims=True)
        n1, r1 = norm_stats(mixed_ref[at, :] + attn)
        n1_ref[at, :] = n1
        r1_ref[at, :] = r1
        low = (n1 * g1_ref[...] + s1_ref[...]).astype(BF16)
        low_ref[at, :] = low
        pre = dg(low, up_ref[...], NN) + ub_ref[...]
        value, slope = gelu_and_slope(pre)
        hidden = value.astype(BF16)
        hid_ref[at, :] = hidden
        slope_ref[at, :] = slope.astype(BF16)
        part_ref[at, :] = dg(hidden, dt_ref[...], NT).astype(BF16)
        return carry

    lax.fori_loop(0, rows // step, body, 0)


def norm_back(gn, n, r):
    return r * (gn - jnp.mean(gn, axis=-1, keepdims=True) - n * jnp.mean(gn * n, axis=-1, keepdims=True))


def ffn_bwd_kernel(n1_ref, g1_ref, s1_ref, p0_ref, p1_ref, seg_ref, db_ref, g2_ref, s2_ref, cot_ref, low_ref,
                   hid_ref, slope_ref, up_ref, dt_ref,
                   out_ref, gr2_ref, part_ref, ddt_ref, dup_ref, sums_ref, dub_ref, fg, hg):
    rows, width = n1_ref.shape
    step = 256
    sums_ref[...] = jnp.zeros_like(sums_ref)
    dub_ref[...] = jnp.zeros_like(dub_ref)

    def body(i, carry):
        at = pl.ds(pl.multiple_of(i * step, step), step)
        ffn = db_ref[...] + (p0_ref[at, :].astype(F32) + p1_ref[at, :].astype(F32))
        valid = (seg_ref[at, :] != 0).astype(F32)
        resid = n1_ref[at, :] * g1_ref[...] + s1_ref[...] + ffn
        n2, r2 = norm_stats(resid)
        final = valid * (n2 * g2_ref[...] + s2_ref[...])
        out_ref[at, :] = final.astype(BF16)
        gf = valid * cot_ref[at, :].astype(F32)
        gr2 = norm_back(gf * g2_ref[...], n2, r2)
        gr2_ref[at, :] = gr2
        ffn_grad = gr2.astype(BF16)
        fg[at, :] = ffn_grad
        row_sum = lambda v: jnp.sum(v, axis=0, keepdims=True)
        sums_ref[...] += jnp.concatenate(
            [row_sum(valid * ffn * ffn), row_sum(final * final), row_sum(gf * n2), row_sum(gf), row_sum(ffn_grad.astype(F32))], axis=0)
        gh = dg(ffn_grad, dt_ref[...], NN)
        hidden_grad = (slope_ref[at, :].astype(F32) * gh).astype(BF16)
        hg[at, :] = hidden_grad
        dub_ref[...] += row_sum(hidden_grad.astype(F32))
        part_ref[at, :] = dg(hidden_grad, up_ref[...], NT).astype(BF16)
        return carry

    lax.fori_loop(0, rows // step, body, 0)
    ddt_ref[...] = dg(fg[...], hid_ref[...], TN).astype(ddt_ref.dtype)
    dup_ref[...] = dg(low_ref[...], hg[...], TN).astype(dup_ref.dtype)


def attn_bwd_kernel(gr2_ref, p0_ref, p1_ref, n1_ref, r1_ref, g1_ref, segc_ref, segr_ref, ctx_ref, qkv_ref, lse_ref,
                    mlow_ref, w_ref,
                    own_ref, send_ref, dw_ref, sums_ref, dqkvb_ref, gr1, cg, qt, kt, ct, dqt, dk, dv, gqkv):
    rows, width = gr2_ref.shape
    half = ctx_ref.shape[1]
    heads = half // HD
    step = 256
    core = lax.rem(lax.axis_index("dp"), 2)
    sums_ref[...] = jnp.zeros_like(sums_ref)
    row_sum = lambda v: jnp.sum(v, axis=0, keepdims=True)

    def norm_body(i, carry):
        at = pl.ds(pl.multiple_of(i * step, step), step)
        gn1 = gr2_ref[at, :] + (p0_ref[at, :].astype(F32) + p1_ref[at, :].astype(F32))
        n1 = n1_ref[at, :]
        g = norm_back(gn1 * g1_ref[...], n1, r1_ref[at, :])
        gr1[at, :] = g
        attn_grad = g.astype(BF16)
        sums_ref[...] += jnp.concatenate([row_sum(gn1 * n1), row_sum(gn1), row_sum(attn_grad.astype(F32))], axis=0)
        back = dg(attn_grad, w_ref[:, 3 * half:], NN)
        cg[at, :] = jnp.where(segc_ref[at, :] != 0, back, 0.0).astype(BF16)
        return carry

    lax.fori_loop(0, rows // step, norm_body, 0)
    dw_ref[:, 3 * half:] = dg(gr1[...].astype(BF16), ctx_ref[...], TN).astype(dw_ref.dtype)
    scale = jnp.asarray(HD ** -0.5, BF16)
    qt[...] = (qkv_ref[:, 0:half] * scale).T
    kt[...] = qkv_ref[:, half:2 * half].T
    ct[...] = cg[...].T
    lane = lax.broadcasted_iota(jnp.int32, (1, 128), 1)

    def pair_body(p, carry):
        base = pl.multiple_of(p * 128, 128)
        k_at = pl.ds(pl.multiple_of(half + base, 128), 128)
        v_at = pl.ds(pl.multiple_of(2 * half + base, 128), 128)
        q_pair = qkv_ref[:, pl.ds(base, 128)] * scale
        o_pair = cg[:, pl.ds(base, 128)]
        dk[...] = jnp.zeros_like(dk)
        dv[...] = jnp.zeros_like(dv)
        for j in range(2):
            head_at = pl.ds(pl.multiple_of(base + j * HD, HD), HD)
            zero = jnp.zeros((HD, rows), BF16)
            put = lambda a: jnp.concatenate([a, zero] if j == 0 else [zero, a], axis=0)
            qz, cz, kh = put(qt[head_at, :]), put(ct[head_at, :]), kt[head_at, :]
            keep = (lane < HD) if j == 0 else (lane >= HD)
            for i in range(rows // step):
                at = slice(i * step, (i + 1) * step)
                s = dg(qkv_ref[:, k_at], qz[:, at], NN)
                pr = jnp.exp(s - lse_ref[pl.ds(2 * p + j, 1), at])
                pr = jnp.where(segc_ref[...] == segr_ref[:, at], pr, 0.0)
                gp = dg(qkv_ref[:, v_at], cz[:, at], NN)
                delta = jnp.sum(pr * gp, axis=0, keepdims=True)
                ds = (pr * (gp - delta)).astype(BF16)
                dv[...] += dg(pr.astype(BF16), jnp.where(keep, o_pair[at, :], jnp.zeros_like(o_pair[at, :])), NN)
                dk[...] += dg(ds, jnp.where(keep, q_pair[at, :], jnp.zeros_like(q_pair[at, :])), NN)
                dqt[head_at, at] = (dg(kh, ds, NN) * (HD ** -0.5)).astype(BF16)
        gqkv[:, k_at] = dk[...].astype(BF16)
        gqkv[:, v_at] = dv[...].astype(BF16)
        return carry

    lax.fori_loop(0, heads // 2, pair_body, 0)
    gqkv[:, 0:half] = dqt[...].T
    dqkvb_ref[...] = row_sum(gqkv[...].astype(F32))
    dw_ref[:, :3 * half] = dg(mlow_ref[...], gqkv[...], TN).astype(dw_ref.dtype)
    mine = pl.ds(pl.multiple_of(core * half, 128), half)
    other = pl.ds(pl.multiple_of((1 - core) * half, 128), half)
    own_ref[...] = gr1[:, mine] + dg(gqkv[...], w_ref[mine, 0:3 * half], NT)
    send_ref[...] = dg(gqkv[...], w_ref[other, 0:3 * half], NT).astype(BF16)


def local(n_dp, hidden_in, segment_ids, time_mask, mask_embed, conv_weight, conv_bias, query_weight, key_weight,
          value_weight, query_bias, value_bias, out_weight, out_bias, first_gain, first_shift, up_weight, up_bias,
          down_weight, down_bias, second_gain, second_shift, cotangent):
    _, rows, width = hidden_in.shape
    half = width // 2
    ff = up_weight.shape[1]
    spread_width = -(-(rows + 7 * 64 + 64) // 128) * 128
    blocks = KW // TAPS
    part = lax.axis_index("mp")
    core = lax.rem(lax.axis_index("dp"), 2)
    n_all = 2 * n_dp
    turn = [(f, f // 4 * 4 + (f % 2) * 2 + (f // 2) % 2) for f in range(n_all)]
    sibling = [(f, f ^ 2) for f in range(n_all)]
    core_groups = [[f for f in range(n_all) if (f // 2) % 2 == c] for c in range(2)]
    swap = lambda v: lax.ppermute(v, BOTH, sibling)
    turned = lambda v: lax.ppermute(v, BOTH, turn)
    mine = part == core

    if conv_weight.shape[0] == TAPS * CG:
        conv_full = lax.all_gather(conv_weight.T, "dp", axis=0, tiled=True)
        conv_full = conv_full.reshape(blocks, half, TAPS * CG)
    else:
        conv_full = lax.all_gather(conv_weight, "dp", axis=0, tiled=True)
        conv_full = conv_full.reshape(blocks, TAPS * CG, half).swapaxes(1, 2)
    wall = jnp.concatenate([query_weight, key_weight, value_weight, out_weight.T, up_weight, down_weight.T], axis=1)
    wall = lax.all_gather(turned(wall), BOTH, axis=0, tiled=True, axis_index_groups=core_groups)
    w_qkvo, w_up, w_down = wall[:, :4 * half], wall[:, 4 * half:4 * half + ff], wall[:, 4 * half + ff:]
    bias = turned(jnp.concatenate([query_bias, value_bias, up_bias])[None])
    qb, vb, ub = (b.astype(F32) for b in (bias[:, :half], bias[:, half:2 * half], bias[:, 2 * half:]))
    row = lambda v: v.astype(F32)[None]

    hid, cot = hidden_in[0], cotangent[0]
    small = jnp.concatenate([segment_ids, time_mask], axis=0)
    hid_s = jnp.where(mine, hid, swap(hid))
    cot_s = jnp.where(mine, cot, swap(cot))
    small_s = jnp.where(mine, small, swap(small))
    seg_c, mask_c = segment_ids.reshape(rows, 1), time_mask.reshape(rows, 1)
    seg_sr, seg_sc, mask_sc = small_s[0:1], small_s[0].reshape(rows, 1), small_s[1].reshape(rows, 1)

    masked = mask_c.astype(F32)
    hid_half = lax.dynamic_slice_in_dim(hid, part * half, half, 1).astype(F32)
    emb_half = lax.dynamic_slice_in_dim(mask_embed, part * half, half, 0).astype(F32)
    start_half = (hid_half + masked * (emb_half - hid_half)).astype(BF16)
    conv_low, conv_slope = call(
        conv_fwd_kernel, [((rows, half), BF16), ((rows, half), F32)],
        [((rows, spread_width), BF16), ((half, spread_width), BF16), ((blocks * CG, spread_width), F32), ((half, spread_width), F32)],
        seg_c, start_half, conv_full, row(conv_bias))
    conv_s = turned(conv_low)
    conv_o = swap(conv_s)
    c0, c1 = jnp.where(core == 0, conv_s, conv_o), jnp.where(core == 0, conv_o, conv_s)

    heads = half // HD
    mixed, mlow, qkv, ctx, lse, part1, stat_conv = call(
        attn_fwd_kernel,
        [((rows, width), F32), ((rows, width), BF16), ((rows, 3 * half), BF16), ((rows, half), BF16), ((heads, rows), F32), ((rows, width), BF16), ((1, half), F32)],
        [((half, rows), BF16)] * 3,
        hid_s, c0, c1, mask_sc, seg_sc, seg_sr, row(mask_embed), w_qkvo, qb, vb)
    n1, r1, nlow, hidden, slope, part2, stat_attn = call(
        ffn_fwd_kernel,
        [((rows, width), F32), ((rows, 1), F32), ((rows, width), BF16), ((rows, ff), BF16), ((rows, ff), BF16), ((rows, width), BF16), ((1, width), F32)],
        [],
        mixed, part1, swap(part1), seg_sc, row(out_bias), row(first_gain), row(first_shift), w_up, ub, w_down)
    out_s, gr2, part3, d_down, d_up, sums2, d_ub = call(
        ffn_bwd_kernel,
        [((rows, width), BF16), ((rows, width), F32), ((rows, width), BF16), ((width, ff), BF16), ((width, ff), BF16), ((5, width), F32), ((1, ff), F32)],
        [((rows, width), BF16), ((rows, ff), BF16)],
        n1, row(first_gain), row(first_shift), part2, swap(part2), seg_sc, row(down_bias), row(second_gain), row(second_shift), cot_s, nlow,
        hidden, slope, w_up, w_down)
    other_out = lax.ppermute(out_s, "mp", [(0, 1), (1, 0)])
    layer_out = jnp.where(mine, out_s, other_out)[None]
    own, send, d_qkvo, sums1, d_qkvb = call(
        attn_bwd_kernel,
        [((rows, half), F32), ((rows, half), BF16), ((width, 4 * half), BF16), ((3, width), F32), ((1, 3 * half), F32)],
        [((rows, width), F32), ((rows, half), BF16), ((half, rows), BF16), ((half, rows), BF16), ((half, rows), BF16), ((half, rows), BF16),
         ((rows, 128), F32), ((rows, 128), F32), ((rows, 3 * half), BF16)],
        gr2, part3, swap(part3), n1, r1, row(first_gain), seg_sc, seg_sr, ctx, qkv, lse, mlow, w_qkvo)
    gm_half = turned((own + swap(send).astype(F32)).astype(BF16))
    d_conv, input_grad, d_cb, d_me = call(
        conv_bwd_kernel,
        [((blocks, half, TAPS * CG), BF16), ((rows, half), F32), ((1, half), F32), ((1, half), F32)],
        [((rows, spread_width), BF16), ((half, spread_width), BF16), ((half, spread_width), BF16), ((blocks * CG, spread_width), BF16), ((half, spread_width), F32)],
        seg_c, start_half, conv_full, conv_slope, gm_half, mask_c)

    d_wall = jnp.concatenate([d_qkvo, d_up, d_down], axis=1)
    d_wall = turned(lax.psum_scatter(d_wall, BOTH, scatter_dimension=0, tiled=True, axis_index_groups=core_groups)).astype(F32)
    if conv_weight.shape[0] == TAPS * CG:
        d_conv = lax.psum_scatter(d_conv.reshape(blocks * half, TAPS * CG), "dp", scatter_dimension=0, tiled=True).T.astype(F32)
    else:
        d_conv = lax.psum_scatter(d_conv.swapaxes(1, 2).reshape(blocks * TAPS * CG, half), "dp", scatter_dimension=0, tiled=True).astype(F32)
    once = (jnp.arange(width) // half == core).astype(F32)[None]
    put = lambda v, which: lax.dynamic_update_slice(jnp.zeros((1, 2 * v.shape[1]), F32), v, (0, which * v.shape[1]))
    full = jnp.concatenate([sums2, sums1, stat_attn], axis=0) * once
    pieces = [put(d_me, part), put(d_cb, part), put(d_qkvb[:, :half], core), put(d_qkvb[:, 2 * half:], core), put(d_ub, core)]
    stats = jnp.stack([jnp.sum(stat_conv) * 0.5, jnp.sum(full[8]), jnp.sum(full[0]), jnp.sum(full[1]), jnp.sum((seg_c != 0).astype(F32)) * 0.5])
    flat = jnp.concatenate([jnp.concatenate(pieces, axis=1)[0], full[2:8].reshape(-1), stats])
    flat = lax.psum(flat, BOTH)
    at = 0
    sections = []
    for size in (width, width, width, width, 2 * ff) + (width,) * 6 + (5,):
        sections.append(flat[at:at + size])
        at += size
    me, cb, dqb, dvb, dub, g2, s2, db, g1, s1, ob, st = sections
    half_of = lambda v: lax.dynamic_slice_in_dim(v, part * (v.shape[0] // 2), v.shape[0] // 2, 0)
    stream_rms = jnp.sqrt(st[:4] / (st[4] * width))
    q_, k_, v_, o_, u_, d_ = jnp.split(d_wall, [half, 2 * half, 3 * half, 4 * half, 4 * half + ff], axis=1)
    return (layer_out, input_grad[None], half_of(me), d_conv, half_of(cb), q_, k_, v_, half_of(dqb), half_of(dvb), o_.T, ob, g1, s1,
            u_, half_of(dub), d_.T, db, g2, s2, stream_rms)


def solution(mesh):
    split, half, turn = P("dp", "mp"), P("mp"), P("mp", "dp")
    whole = P()
    rows = P("dp", None, None)
    return jax.shard_map(
        functools.partial(local, mesh.shape["dp"]),
        mesh=mesh,
        in_specs=(rows, P("dp", None), P("dp", None), whole, split, half, split, split, split, half, half, turn, whole, whole, whole,
                  split, half, turn, whole, whole, whole, rows),
        out_specs=(rows, P("dp", None, "mp"), half, split, half, split, split, split, half, half, turn, whole, whole, whole,
                   split, half, turn, whole, whole, whole, whole),
        check_vma=False,
    )
```

```python
import functools

import jax
import jax.numpy as jnp
from jax import lax
from jax.experimental import pallas as pl
from jax.experimental.pallas import tpu as pltpu
from jax.sharding import PartitionSpec as P

HD = 64
KW = 128
CG = 48
TAPS = 8
EPS = 1e-05
F32 = jnp.float32
BF16 = jnp.bfloat16
NN = (((1,), (0,)), ((), ()))
NT = (((1,), (1,)), ((), ()))
TN = (((0,), (0,)), ((), ()))
BOTH = ("dp", "mp")


def dg(a, b, dims):
    return lax.dot_general(a, b, dims, preferred_element_type=F32)


def gelu_parts(v):
    t = 1.0 / (1.0 + (0.3275911 * 0.7071067811865476) * jnp.abs(v))
    e = jnp.exp(-0.5 * v * v)
    poly = t * (0.254829592 + t * (-0.284496736 + t * (1.421413741 + t * (-1.453152027 + t * 1.061405429))))
    tail = 0.5 * poly * e
    return jnp.where(v >= 0, 1.0 - tail, tail), e


def gelu_and_slope(v):
    phi, e = gelu_parts(v)
    return v * phi, phi + v * e * 0.3989422804014327


def call(kernel, outs, scratch, *args, hbm_in=(), hbm_out=(), sems=(), meeting=None):
    space = lambda here: pl.BlockSpec(memory_space=pl.ANY if here else pltpu.VMEM)
    return pl.pallas_call(
        kernel,
        out_shape=[jax.ShapeDtypeStruct(s, d) for s, d in outs],
        in_specs=[space(i in hbm_in) for i in range(len(args))],
        out_specs=[space(i in hbm_out) for i in range(len(outs))],
        scratch_shapes=[pltpu.VMEM(s, d) for s, d in scratch] + [pltpu.SemaphoreType.DMA(s) for s in sems],
        compiler_params=pltpu.CompilerParams(vmem_limit_bytes=60 * 2**20, has_side_effects=bool(sems), collective_id=meeting),
    )(*args)


def split_low(v):
    hi = v.astype(BF16)
    return hi, (v - hi.astype(F32)).astype(BF16)


def spread_matrix(seg, length, width):
    rank = jnp.where(seg == 0, 7, seg - 1)
    pos = lax.broadcasted_iota(jnp.int32, (length, 1), 0) + 64 * rank + 8
    hit = pos == lax.broadcasted_iota(jnp.int32, (length, width), 1)
    return hit.astype(F32).astype(BF16)


def rolled(x, left):
    width = x.shape[1]
    left = left % width
    return x if left == 0 else pltpu.roll(x, width - left, 1)


def tap_patches(xg):
    return jnp.concatenate([rolled(xg, r) for r in range(TAPS)], axis=0)


def nothing(*_):
    pass


def block_rows(w_ref, at):
    w = w_ref[(slice(None),) * (len(w_ref.shape) - 2) + (at, slice(None))]
    return w.reshape(-1, w.shape[-1])


def conv_fwd_kernel(seg_ref, x_ref, w_ref, b_ref, low_ref, slope_ref, spread, xq, y_ref, ot, ready=nothing, beside=nothing):
    length, width = spread.shape
    blocks = KW // TAPS
    spread[...] = spread_matrix(seg_ref[...], length, width)
    xq[...] = dg(x_ref[...], spread[...], TN).astype(BF16)
    ready()

    def body(g, carry):
        beside(g)
        at = pl.ds(pl.multiple_of(g * CG, 16), CG)
        y_ref[...] = dg(block_rows(w_ref, at), tap_patches(xq[at, :]), NN)
        acc = rolled(y_ref[0:CG, :], -64)
        for b in range(1, blocks):
            acc = acc + rolled(y_ref[b * CG:(b + 1) * CG, :], TAPS * b - 64)
        ot[at, :] = acc
        return carry

    lax.fori_loop(0, x_ref.shape[1] // CG, body, 0)
    hi, lo = split_low(ot[...])
    pre = dg(spread[...], hi, NT) + dg(spread[...], lo, NT) + b_ref[...]
    valid = (seg_ref[...] != 0).astype(F32)
    value, slope = gelu_and_slope(pre)
    low_ref[...] = (valid * value).astype(BF16)
    slope_ref[...] = valid * slope


def conv_bwd_kernel(seg_ref, xq, w_ref, slope_ref, gm_ref, mask_ref, dw_ref, in_ref, db_ref, dm_ref,
                    spread, dq, d_ref, gq, extra=0, beside=nothing, store=None):
    length, width = spread.shape
    blocks = KW // TAPS
    groups = xq.shape[0] // CG
    spread[...] = spread_matrix(seg_ref[...], length, width)
    dpre = (slope_ref[...] * gm_ref[...].astype(F32)).astype(BF16)
    db_ref[...] = jnp.sum(dpre.astype(F32), axis=0, keepdims=True)
    dq[...] = dg(dpre, spread[...], TN).astype(BF16)

    def group(g):
        at = pl.ds(pl.multiple_of(g * CG, 16), CG)
        dqg = dq[at, :]
        for b in range(blocks):
            d_ref[b * CG:(b + 1) * CG, :] = rolled(dqg, 64 - TAPS * b)
        dmat = d_ref[...]
        dw = dg(dmat, tap_patches(xq[at, :]), NT).astype(BF16).reshape(blocks, CG, TAPS * CG)
        if store is None:
            dw_ref[:, at, :] = dw
        else:
            store(g, dw)
        v = dg(block_rows(w_ref, at), dmat, TN)
        acc = v[0:CG, :]
        for r in range(1, TAPS):
            acc = acc + rolled(v[r * CG:(r + 1) * CG, :], -r)
        gq[at, :] = acc

    def body(g, carry):
        if extra:
            pl.when(g < groups)(lambda: group(g))
        else:
            group(g)
        beside(g)
        return carry

    lax.fori_loop(0, groups + extra, body, 0)
    hi, lo = split_low(gq[...])
    grad = dg(spread[...], hi, NT) + dg(spread[...], lo, NT) + gm_ref[...].astype(F32)
    masked = mask_ref[...].astype(F32)
    dm_ref[...] = jnp.sum(masked * grad, axis=0, keepdims=True)
    in_ref[...] = (1.0 - masked) * grad


class Place:
    def __init__(self):
        self.dp, self.y = lax.axis_index("dp"), lax.axis_index("mp")
        self.z, self.x, self.core = self.dp // 4, lax.rem(self.dp // 2, 2), lax.rem(self.dp, 2)

    def at(self, z=None, x=None, core=None, y=None):
        pick = lambda new, old: old if new is None else new
        dp = pick(z, self.z) * 4 + pick(x, self.x) * 2 + pick(core, self.core)
        return {"dp": dp, "mp": pick(y, self.y)}


def push(src, dst, sems, index, device):
    send, recv = sems if isinstance(sems, tuple) else (sems.at[0], sems.at[1])
    return pltpu.make_async_remote_copy(
        src_ref=src, dst_ref=dst, send_sem=send.at[index], recv_sem=recv.at[index],
        device_id=device, device_id_type=pl.DeviceIdType.MESH)


def meet(devices):
    here = pltpu.get_barrier_semaphore()
    for device in devices:
        pl.semaphore_signal(here, inc=1, device_id=device, device_id_type=pl.DeviceIdType.MESH)
    pl.semaphore_wait(here, len(devices))


def partners(p):
    return [p.at(z=lax.rem(p.z + o, 4)) for o in (1, 2, 3)] + [p.at(x=1 - p.x), p.at(core=1 - p.core), p.at(y=1 - p.y)]


def meet_all(p):
    crooked = p.core != p.y
    pl.when(crooked)(lambda: meet(partners(p) + [p.at(core=p.y, y=p.core)]))
    pl.when(jnp.logical_not(crooked))(lambda: meet(partners(p)))


class LineGather:
    UP, DOWN, ACROSS, LAST = range(4)

    def __init__(self, place, own, buf, send, recv, k, third, x_first=True):
        p = self.p = place
        self.own, self.buf, self.send, self.recv, self.k, self.x_first = own, buf, send, recv, k, x_first
        self.t = p.core if third == "core" else p.y
        over_x, over_t = p.at(x=1 - p.x), p.at(**{third: 1 - self.t})
        self.to = [p.at(z=jnp.minimum(p.z + 1, 3)), p.at(z=jnp.maximum(p.z - 1, 0))] + ([over_x, over_t] if x_first else [over_t, over_x])

    def slot(self, z, across=False, last=False):
        flip = lambda v, yes: 1 - v if yes else v
        x, t = (across, last) if self.x_first else (last, across)
        return (z, flip(self.p.x, x), flip(self.t, t))

    def copy(self, way, slot, src=None):
        at = (self.k,) + slot
        return pltpu.make_async_remote_copy(
            src_ref=self.buf.at[slot] if src is None else src, dst_ref=self.buf.at[slot], send_sem=self.send.at[(way,) + at],
            recv_sem=self.recv.at[at], device_id=self.to[way], device_id_type=pl.DeviceIdType.MESH)

    def walk(self, d, start, finish):
        p = self.p
        if d == 0:
            mine = self.slot(p.z)
            pl.when(p.z < 3)(lambda: start(self.UP, mine, True))
            pl.when(p.z > 0)(lambda: start(self.DOWN, mine, True))
            start(self.ACROSS, mine, True)
            start(self.LAST, mine, True)
            return

        def passing(z, way, further):
            slot = self.slot(z)
            finish(slot)
            pl.when(further)(lambda: start(way, slot, False))
            start(self.ACROSS, slot, False)
            start(self.LAST, slot, False)

        def crossed(z):
            slot = self.slot(z, across=True)
            finish(slot)
            start(self.LAST, slot, False)

        if d < 4:
            pl.when(p.z >= d)(lambda: passing(p.z - d, self.UP, p.z < 3))
            pl.when(p.z + d <= 3)(lambda: passing(p.z + d, self.DOWN, p.z > 0))
        if d == 1:
            crossed(p.z)
        else:
            pl.when(p.z >= d - 1)(lambda: crossed(p.z - d + 1))
            pl.when(p.z + d - 1 <= 3)(lambda: crossed(p.z + d - 1))

    def begin(self, way, slot, own):
        self.copy(way, slot, self.own if own else None).start()

    def round(self, d):
        self.walk(d, self.begin, lambda slot: self.copy(0, slot).wait_recv())

    def drain(self):
        for z in range(4):
            for across in (False, True):
                self.copy(0, self.slot(z, across, True)).wait_recv()
        for d in range(5):
            self.walk(d, lambda way, slot, own: self.copy(way, slot, self.own if own else None).wait_send(), nothing)


class Fold:
    def __init__(self, kind, place, grad, sems, k, first, across, out1, cur, mid, last, out):
        self.kind, self.p, self.d, self.first, self.across, self.out1 = kind, place, grad, first, across, out1
        self.cur, self.mid, self.last, self.out = cur, mid, last, out
        p = place
        self.straight = p.core == p.y
        copy = lambda src, dst, n, dev: push(src, dst, sems, (k, n), dev)
        home, partner, sibling = p.at(y=p.core), p.at(x=1 - p.x), p.at(core=1 - p.core)
        away = grad.at[:, 1 - p.x]
        if kind == 0:
            self.over_y = copy(grad, first, 0, home)
            self.to_sibling = copy(out1, cur, 1, sibling)
            self.over_x = copy(cur.at[:, 1 - p.x], across, 2, partner)
        else:
            self.over_x = copy(away, across, 2, partner)
            self.over_y = copy(mid, first, 0, home)
            self.to_sibling = copy(out1, cur, 1, sibling)
        held = mid if kind == 0 else cur
        self.along = [copy(held.at[lax.rem(p.z + o, 4)], last.at[o - 1], 2 + o, p.at(z=lax.rem(p.z + o, 4))) for o in (1, 2, 3)]
        self.held = held

    def one_way(self, copy, sends, wait):
        pl.when(sends)(copy.wait_send if wait else copy.start)
        if wait:
            pl.when(jnp.logical_not(sends))(copy.wait_recv)

    def start(self, n):
        p, wide = self.p, lambda ref: ref.astype(F32)
        crooked = jnp.logical_not(self.straight)
        if n == 0:
            if self.kind == 0:
                self.one_way(self.over_y, crooked, False)
            else:
                self.over_x.start()
        elif n == 1:
            if self.kind == 0:
                @pl.when(self.straight)
                def _():
                    for z in range(4):
                        for x in range(2):
                            self.cur[z, x] = (wide(self.d[z, x, p.core]) + wide(self.first[z, x, p.core])).astype(BF16)
                            self.out1[z, x] = (wide(self.d[z, x, 1 - p.core]) + wide(self.first[z, x, 1 - p.core])).astype(BF16)
                    self.to_sibling.start()
            else:
                for z in range(4):
                    for c in range(2):
                        self.mid[z, c] = (wide(self.d[z, p.x, c]) + wide(self.across[z, c])).astype(BF16)
                self.one_way(self.over_y, crooked, False)
        elif n == 2:
            if self.kind == 0:
                self.over_x.start()
            else:
                @pl.when(self.straight)
                def _():
                    for z in range(4):
                        self.cur[z] = (wide(self.mid[z, p.core]) + wide(self.first[z, p.core])).astype(BF16)
                        self.out1[z] = (wide(self.mid[z, 1 - p.core]) + wide(self.first[z, 1 - p.core])).astype(BF16)
                    self.to_sibling.start()
        elif n == 3:
            if self.kind == 0:
                for z in range(4):
                    self.mid[z] = (wide(self.cur[z, p.x]) + wide(self.across[z])).astype(BF16)
            for c in self.along:
                c.start()
        else:
            self.out[...] = wide(self.held[p.z]) + wide(self.last[0]) + wide(self.last[1]) + wide(self.last[2])

    def wait(self, n):
        crooked = jnp.logical_not(self.straight)
        if n == 3:
            for c in self.along:
                c.wait()
        elif (self.kind, n) in ((0, 0), (1, 1)):
            self.one_way(self.over_y, crooked, True)
        elif (self.kind, n) in ((0, 1), (1, 2)):
            self.one_way(self.to_sibling, self.straight, True)
        else:
            self.over_x.wait()


def fold_scratch(kind, n):
    wide = (4, 2, 48, n)
    if kind == 0:
        shapes = ((4, 2, 2, 48, n), (4, 48, n), wide, wide, (4, 48, n), (3, 48, n))
    else:
        shapes = (wide, wide, (4, 48, n), (4, 48, n), wide, (3, 48, n))
    return [(s, BF16) for s in shapes]


def columns(rows_ref):
    return rows_ref[...].astype(F32).T


def conv_gather_kernel(*refs):
    (small_ref, hid_ref, cot_ref, emb_ref, shard_ref, b_ref, qk, vo, ul, ur,
     xq, slope_ref, conv_t, hid_s, cot_s, small_s, w_out, wqk, wvo, wul, wur,
     spread, y_ref, ot, low, w_ref, own_t, seg, x_ref, local, turn, send_c, recv_c, send_w, recv_w) = refs
    p = Place()
    straight = p.core == p.y
    crooked = jnp.logical_not(straight)
    meet_all(p)
    shards = (qk, vo, ul, ur)
    walls = (wqk, wvo, wul, wur)
    conv = LineGather(p, shard_ref, w_ref, send_c, recv_c, 0, "core")
    gathers = [LineGather(p, own_t.at[k], walls[k], send_w, recv_w, k, "y", k < 3) for k in range(4)]
    own_w = pltpu.make_async_copy(shard_ref, w_ref.at[p.z, p.x, p.core], local.at[0])
    save_w = pltpu.make_async_copy(w_ref, w_out, local.at[1])
    keep = [pltpu.make_async_copy(own_t.at[k], walls[k].at[p.z, p.x, p.y], local.at[2 + k]) for k in range(4)]
    turned = [push(shards[k], own_t.at[k], turn, (k,), p.at(core=p.y, y=p.core)) for k in range(4)]
    pairs = ((hid_ref, hid_s), (cot_ref, cot_s), (small_ref, small_s))
    keep_rows = [pltpu.make_async_copy(a, b, local.at[6 + k]) for k, (a, b) in enumerate(pairs)]
    push_rows = [push(a, b, turn, (4 + k,), p.at(core=1 - p.core)) for k, (a, b) in enumerate(pairs)]
    turn_conv = push(low, conv_t, turn, (7,), p.at(core=p.y, y=p.core))

    own_w.start()
    conv.round(0)

    @pl.when(straight)
    def _():
        for k in range(4):
            own_t[k] = shards[k][...]
        for c in keep_rows + push_rows:
            c.start()

    @pl.when(crooked)
    def _():
        for c in turned:
            c.start()

    cols = columns(small_ref)
    seg[...] = cols[:, 0:1].astype(jnp.int32)
    mine = pl.ds(pl.multiple_of(p.y * x_ref.shape[1], 128), x_ref.shape[1])
    hid = hid_ref[:, mine].astype(F32)
    x_ref[...] = (hid + cols[:, 1:2] * (emb_ref[:, mine] - hid)).astype(BF16)

    def ready():
        for d in (1, 2, 3):
            conv.round(d)

        @pl.when(crooked)
        def _():
            for c in turned:
                c.wait()

        for g in gathers:
            g.round(0)
        for c in keep:
            c.start()
        conv.round(4)
        conv.drain()
        own_w.wait()
        save_w.start()

    def beside(g):
        for at, d in ((1, 1), (3, 2), (5, 3), (7, 4)):
            @pl.when(g == at)
            def _(d=d):
                for gather in gathers:
                    gather.round(d)

    conv_fwd_kernel(seg, x_ref, w_ref, b_ref, low, slope_ref, spread, xq, y_ref, ot, ready, beside)

    @pl.when(straight)
    def _():
        conv_t[...] = low[...]
        for c in keep_rows:
            c.wait()
        for c in push_rows:
            c.wait_send()

    @pl.when(crooked)
    def _():
        turn_conv.start()
        for c in push_rows:
            c.wait_recv()

    for g in gathers:
        g.drain()
    for c in keep:
        c.wait()
    save_w.wait()
    pl.when(crooked)(turn_conv.wait)


def attn_gather_kernel(*refs):
    (hid_ref, conv_t, small_ref, emb_ref, wqk_ref, wvo_ref, qb_ref, vb_ref, dl, dr,
     mixed_ref, mlow_ref, qkv_ref, ctx_ref, lse_ref, part_ref, other_ref, stat_ref, wdl, wdr,
     qt, vt, ot, both, own_t, segc, mask, local, turn, send_w, recv_w, send_p, recv_p) = refs
    p = Place()
    crooked = p.core != p.y
    sibling = p.at(core=1 - p.core)
    meet_all(p)
    shards, walls = (dl, dr), (wdl, wdr)
    gathers = [LineGather(p, own_t.at[k], walls[k], send_w, recv_w, k, "y", k == 0) for k in range(2)]
    keep = [pltpu.make_async_copy(own_t.at[k], walls[k].at[p.z, p.x, p.y], local.at[k]) for k in range(2)]
    turned = [push(shards[k], own_t.at[k], turn, (k,), p.at(core=p.y, y=p.core)) for k in range(2)]
    give = push(conv_t, both.at[p.core], turn, (2,), sibling)
    give.start()

    @pl.when(crooked)
    def _():
        for c in turned:
            c.start()

    @pl.when(jnp.logical_not(crooked))
    def _():
        for k in range(2):
            own_t[k] = shards[k][...]

    both[p.core] = conv_t[...]
    cols = columns(small_ref)
    segc[...] = cols[:, 0:1].astype(jnp.int32)
    mask[...] = cols[:, 1:2].astype(jnp.int32)

    @pl.when(crooked)
    def _():
        for c in turned:
            c.wait()

    for g in gathers:
        g.round(0)
    for c in keep:
        c.start()
    give.wait()

    def beside(n):
        for at, d in ((-1, 1), (0, 2), (1, 3), (2, 4)):
            if isinstance(n, int):
                if n == at:
                    for g in gathers:
                        g.round(d)
            elif at >= 0:
                @pl.when(n == at)
                def _(d=d):
                    for g in gathers:
                        g.round(d)

    def sent(i, at):
        c = push(part_ref.at[at], other_ref.at[at], (send_p, recv_p), (i,), sibling)
        c.start()
        return c

    copies = attn_fwd_kernel(hid_ref, both.at[0], both.at[1], mask, segc, small_ref.at[0:1], emb_ref, (wqk_ref, wvo_ref), qb_ref, vb_ref,
                             mixed_ref, mlow_ref, qkv_ref, ctx_ref, lse_ref, part_ref, stat_ref, qt, vt, ot, beside, sent)
    for g in gathers:
        g.drain()
    for c in keep + copies:
        c.wait()


def attn_fwd_kernel(hid_ref, c0_ref, c1_ref, mask_ref, segc_ref, segr_ref, emb_ref, w_refs, qb_ref, vb_ref,
                    mixed_ref, mlow_ref, qkv_ref, ctx_ref, lse_ref, part_ref, stat_ref, qt, vt, ot, beside=nothing, sent=nothing):
    wqk_ref, wvo_ref = w_refs
    rows, width = hid_ref.shape
    half = c0_ref.shape[1]
    heads = half // HD
    step = 256
    stat = jnp.zeros((1, half), F32)
    for i in range(rows // step):
        at = pl.ds(i * step, step)
        conv = jnp.concatenate([c0_ref[at, :].astype(F32), c1_ref[at, :].astype(F32)], axis=1)
        hid = hid_ref[at, :].astype(F32)
        masked = mask_ref[at, :].astype(F32)
        mixed = hid + masked * (emb_ref[...] - hid) + conv
        low = mixed.astype(BF16)
        mixed_ref[at, :] = mixed
        mlow_ref[at, :] = low
        stat = stat + jnp.sum(conv[:, :half] * conv[:, :half] + conv[:, half:] * conv[:, half:], axis=0, keepdims=True)
        qk = dg(low, wqk_ref[...], NN)
        qkv_ref[at, 0:half] = (qk[:, :half] + qb_ref[...]).astype(BF16)
        qkv_ref[at, half:2 * half] = qk[:, half:].astype(BF16)
        qkv_ref[at, 2 * half:] = (dg(low, wvo_ref[:, :half], NN) + vb_ref[...]).astype(BF16)
    stat_ref[...] = stat
    beside(-1)
    qt[...] = (qkv_ref[:, 0:half] * jnp.asarray(HD ** -0.5, BF16)).T
    vt[...] = qkv_ref[:, 2 * half:].T

    def pair_body(p, carry):
        beside(p)
        lanes = pl.ds(pl.multiple_of(half + p * 128, 128), 128)
        k_pair = qkv_ref[:, lanes]
        for j in range(2):
            head_at = pl.ds(pl.multiple_of(p * 128 + j * HD, HD), HD)
            qh = qt[head_at, :]
            vh = vt[head_at, :]
            zero = jnp.zeros_like(qh)
            qz = jnp.concatenate([qh, zero] if j == 0 else [zero, qh], axis=0)
            for i in range(rows // step):
                at = slice(i * step, (i + 1) * step)
                s = dg(k_pair, qz[:, at], NN)
                s = jnp.where(segc_ref[...] == segr_ref[:, at], s, -1000000000.0)
                top = jnp.max(s, axis=0, keepdims=True)
                e = jnp.exp(s - top)
                den = jnp.sum(e, axis=0, keepdims=True)
                o = dg(vh, e.astype(BF16), NN) / den
                ot[head_at, at] = jnp.where(segr_ref[:, at] != 0, o, 0.0).astype(BF16)
                lse_ref[pl.ds(2 * p + j, 1), at] = top + jnp.log(den)
        return carry

    lax.fori_loop(0, heads // 2, pair_body, 0)
    ctx_ref[...] = ot[...].T
    copies = []
    for i in range(rows // step):
        at = pl.ds(i * step, step)
        part_ref[at, :] = dg(ctx_ref[at, :], wvo_ref[:, half:], NT).astype(BF16)
        copies.append(sent(i, at))
    return copies


def norm_stats(x):
    centre = x - jnp.mean(x, axis=-1, keepdims=True)
    r = lax.rsqrt(jnp.mean(centre * centre, axis=-1, keepdims=True) + EPS)
    return centre * r, r


def ffn_fwd_kernel(mixed_ref, p0_ref, p1_ref, seg_ref, ob_ref, g1_ref, s1_ref, ul_ref, ur_ref, ub_ref, dl_ref, dr_ref,
                   n1_ref, r1_ref, low_ref, hid_ref, slope_ref, part_ref, stat_ref, sent=nothing):
    rows, width = mixed_ref.shape
    ff = ul_ref.shape[1]
    step = 256
    stat_ref[...] = jnp.zeros_like(stat_ref)

    def body(i, carry):
        at = pl.ds(pl.multiple_of(i * step, step), step)
        attn = ob_ref[...] + (p0_ref[at, :].astype(F32) + p1_ref[at, :].astype(F32))
        valid = (seg_ref[at, :] != 0).astype(F32)
        stat_ref[...] += jnp.sum(valid * attn * attn, axis=0, keepdims=True)
        n1, r1 = norm_stats(mixed_ref[at, :] + attn)
        n1_ref[at, :] = n1
        r1_ref[at, :] = r1
        low = (n1 * g1_ref[...] + s1_ref[...]).astype(BF16)
        low_ref[at, :] = low
        part = 0.0
        for k, (up, down) in enumerate(((ul_ref, dl_ref), (ur_ref, dr_ref))):
            cols = slice(k * ff, (k + 1) * ff)
            value, slope = gelu_and_slope(dg(low, up[...], NN) + ub_ref[:, cols])
            hidden = value.astype(BF16)
            hid_ref[at, cols] = hidden
            slope_ref[at, cols] = slope.astype(BF16)
            part = part + dg(hidden, down[...], NT)
        part_ref[at, :] = part.astype(BF16)
        sent(i, at)
        return carry

    lax.fori_loop(0, rows // step, body, 0)


class Give:
    def __init__(self, place, part, other, sems):
        self.make = lambda i, at: push(part.at[at], other.at[at], sems, (i,), place.at(core=1 - place.core))

    def __call__(self, i, at):
        self.make(i, at).start()

    def wait(self, parts, step):
        for i in range(parts):
            self.make(i, pl.ds(i * step, step)).wait()


def ffn_fwd_give_kernel(*refs):
    ins, outs, other, seg, sems = refs[:12], refs[12:19], refs[19], refs[20], refs[21]
    p = Place()
    meet([p.at(core=1 - p.core)])
    seg[...] = columns(ins[3])[:, 0:1].astype(jnp.int32)
    give = Give(p, outs[5], other, sems)
    ffn_fwd_kernel(*ins[:3], seg, *ins[4:], *outs, give)
    give.wait(4, 256)


def norm_back(gn, n, r):
    return r * (gn - jnp.mean(gn, axis=-1, keepdims=True) - n * jnp.mean(gn * n, axis=-1, keepdims=True))


def ffn_bwd_kernel(n1_ref, g1_ref, s1_ref, p0_ref, p1_ref, seg_ref, db_ref, g2_ref, s2_ref, cot_ref, low_ref,
                   hid_ref, slope_ref, ul_ref, ur_ref, dl_ref, dr_ref,
                   out_ref, gr2_ref, part_ref, ddl_ref, ddr_ref, dul_ref, dur_ref, sums_ref, dub_ref, fg, hg,
                   done=None, down_done=nothing, sent=nothing):
    rows, width = n1_ref.shape
    ff = ul_ref.shape[1]
    step = 256
    sums_ref[...] = jnp.zeros_like(sums_ref)
    dub_ref[...] = jnp.zeros_like(dub_ref)
    row_sum = lambda v: jnp.sum(v, axis=0, keepdims=True)
    store = lambda ref, v: ref.__setitem__(Ellipsis, v.astype(ref.dtype).reshape(ref.shape))

    def norm_body(i, carry):
        at = pl.ds(pl.multiple_of(i * step, step), step)
        ffn = db_ref[...] + (p0_ref[at, :].astype(F32) + p1_ref[at, :].astype(F32))
        valid = (seg_ref[at, :] != 0).astype(F32)
        n2, r2 = norm_stats(n1_ref[at, :] * g1_ref[...] + s1_ref[...] + ffn)
        final = valid * (n2 * g2_ref[...] + s2_ref[...])
        if done is None:
            out_ref[at, :] = final.astype(BF16)
        else:
            done(i, at, final.astype(BF16))
        gf = valid * cot_ref[at, :].astype(F32)
        gr2 = norm_back(gf * g2_ref[...], n2, r2)
        gr2_ref[at, :] = gr2
        ffn_grad = gr2.astype(BF16)
        fg[at, :] = ffn_grad
        sums_ref[...] += jnp.concatenate(
            [row_sum(valid * ffn * ffn), row_sum(final * final), row_sum(gf * n2), row_sum(gf), row_sum(ffn_grad.astype(F32))], axis=0)
        return carry

    lax.fori_loop(0, rows // step, norm_body, 0)
    store(ddl_ref, dg(fg[...], hid_ref[:, :ff], TN))
    store(ddr_ref, dg(fg[...], hid_ref[:, ff:], TN))
    down_done()

    def body(i, carry):
        at = pl.ds(pl.multiple_of(i * step, step), step)
        part = 0.0
        for k, (up, down) in enumerate(((ul_ref, dl_ref), (ur_ref, dr_ref))):
            cols = slice(k * ff, (k + 1) * ff)
            hidden_grad = (slope_ref[at, cols].astype(F32) * dg(fg[at, :], down[...], NN)).astype(BF16)
            hg[at, cols] = hidden_grad
            dub_ref[:, cols] += row_sum(hidden_grad.astype(F32))
            part = part + dg(hidden_grad, up[...], NT)
        part_ref[at, :] = part.astype(BF16)
        sent(i, at)
        return carry

    lax.fori_loop(0, rows // step, body, 0)
    store(dul_ref, dg(low_ref[...], hg[:, :ff], TN))
    store(dur_ref, dg(low_ref[...], hg[:, ff:], TN))


def ffn_bwd_fold_kernel(*refs):
    ins, outs, (other, first_l, across_r), (fg, hg, seg), (sem_p, sem_o, sem_f) = refs[:17], refs[17:26], refs[26:29], refs[29:32], refs[32:]
    p = Place()
    straight = p.core == p.y
    home = p.at(y=p.core)
    meet([p.at(core=1 - p.core), p.at(x=1 - p.x), p.at(y=1 - p.y)])
    seg[...] = columns(ins[5])[:, 0:1].astype(jnp.int32)
    give = Give(p, outs[2], other, sem_p)
    out_ref, ddl, ddr = outs[0], outs[3], outs[4]
    show = lambda i: push(out_ref.at[pl.ds(i * 256, 256)], out_ref.at[pl.ds(i * 256, 256)], sem_o, (i,), p.at(y=1 - p.y))
    over_y = push(ddl, first_l, sem_f, (0,), home)
    over_x = push(ddr.at[:, 1 - p.x], across_r, sem_f, (1,), p.at(x=1 - p.x))

    def done(i, at, value):
        @pl.when(straight)
        def _():
            out_ref[at, :] = value
            push(out_ref.at[at], out_ref.at[at], sem_o, (i,), p.at(y=1 - p.y)).start()

    def down_done():
        pl.when(jnp.logical_not(straight))(over_y.start)
        over_x.start()

    ffn_bwd_kernel(*ins[:5], seg, *ins[6:], *outs, fg, hg, done, down_done, give)
    give.wait(4, 256)
    over_x.wait()

    @pl.when(straight)
    def _():
        over_y.wait_recv()
        for i in range(4):
            show(i).wait_send()

    @pl.when(jnp.logical_not(straight))
    def _():
        over_y.wait_send()
        for i in range(4):
            show(i).wait_recv()


def attn_bwd_kernel(gr2_ref, p0_ref, p1_ref, n1_ref, r1_ref, g1_ref, segc_ref, segr_ref, ctx_ref, qkv_ref, lse_ref,
                    mlow_ref, wqk_ref, wvo_ref,
                    dqk_ref, dvo_ref, sums_ref, dqkvb_ref, gr1, cg, qt, kt, ct, dqt, dk, dv, gqkv, finish, beside=nothing):
    rows, width = gr2_ref.shape
    half = ctx_ref.shape[1]
    heads = half // HD
    step = 256
    core = lax.rem(lax.axis_index("dp"), 2)
    sums_ref[...] = jnp.zeros_like(sums_ref)
    row_sum = lambda v: jnp.sum(v, axis=0, keepdims=True)

    def norm_body(i, carry):
        at = pl.ds(pl.multiple_of(i * step, step), step)
        gn1 = gr2_ref[at, :] + (p0_ref[at, :].astype(F32) + p1_ref[at, :].astype(F32))
        n1 = n1_ref[at, :]
        g = norm_back(gn1 * g1_ref[...], n1, r1_ref[at, :])
        gr1[at, :] = g
        attn_grad = g.astype(BF16)
        sums_ref[...] += jnp.concatenate([row_sum(gn1 * n1), row_sum(gn1), row_sum(attn_grad.astype(F32))], axis=0)
        back = dg(attn_grad, wvo_ref[:, half:], NN)
        cg[at, :] = jnp.where(segc_ref[at, :] != 0, back, 0.0).astype(BF16)
        return carry

    lax.fori_loop(0, rows // step, norm_body, 0)
    store = lambda ref, cols, v: ref.__setitem__((Ellipsis, cols), v.astype(BF16).reshape(ref.shape[:-1] + (v.shape[-1],)))
    store(dvo_ref, slice(half, 2 * half), dg(gr1[...].astype(BF16), ctx_ref[...], TN))
    scale = jnp.asarray(HD ** -0.5, BF16)
    qt[...] = (qkv_ref[:, 0:half] * scale).T
    kt[...] = qkv_ref[:, half:2 * half].T
    ct[...] = cg[...].T
    lane = lax.broadcasted_iota(jnp.int32, (1, 128), 1)

    def pair_body(p, carry):
        beside(p)
        base = pl.multiple_of(p * 128, 128)
        k_at = pl.ds(pl.multiple_of(half + base, 128), 128)
        v_at = pl.ds(pl.multiple_of(2 * half + base, 128), 128)
        q_pair = qkv_ref[:, pl.ds(base, 128)] * scale
        o_pair = cg[:, pl.ds(base, 128)]
        dk[...] = jnp.zeros_like(dk)
        dv[...] = jnp.zeros_like(dv)
        for j in range(2):
            head_at = pl.ds(pl.multiple_of(base + j * HD, HD), HD)
            zero = jnp.zeros((HD, rows), BF16)
            put = lambda a: jnp.concatenate([a, zero] if j == 0 else [zero, a], axis=0)
            qz, cz, kh = put(qt[head_at, :]), put(ct[head_at, :]), kt[head_at, :]
            keep = (lane < HD) if j == 0 else (lane >= HD)
            for i in range(rows // step):
                at = slice(i * step, (i + 1) * step)
                s = dg(qkv_ref[:, k_at], qz[:, at], NN)
                pr = jnp.exp(s - lse_ref[pl.ds(2 * p + j, 1), at])
                pr = jnp.where(segc_ref[...] == segr_ref[:, at], pr, 0.0)
                gp = dg(qkv_ref[:, v_at], cz[:, at], NN)
                delta = jnp.sum(pr * gp, axis=0, keepdims=True)
                ds = (pr * (gp - delta)).astype(BF16)
                dv[...] += dg(pr.astype(BF16), jnp.where(keep, o_pair[at, :], jnp.zeros_like(o_pair[at, :])), NN)
                dk[...] += dg(ds, jnp.where(keep, q_pair[at, :], jnp.zeros_like(q_pair[at, :])), NN)
                dqt[head_at, at] = (dg(kh, ds, NN) * (HD ** -0.5)).astype(BF16)
        gqkv[:, k_at] = dk[...].astype(BF16)
        gqkv[:, v_at] = dv[...].astype(BF16)
        return carry

    lax.fori_loop(0, heads // 2, pair_body, 0)
    gqkv[:, 0:half] = dqt[...].T
    mine = pl.ds(pl.multiple_of(core * half, 128), half)
    other = pl.ds(pl.multiple_of((1 - core) * half, 128), half)
    to_mixed = lambda at: (dg(gqkv[:, :2 * half], wqk_ref[at, :], NT) + dg(gqkv[:, 2 * half:], wvo_ref[at, 0:half], NT))
    finish(lambda: to_mixed(other).astype(BF16), lambda: gr1[:, mine] + to_mixed(mine))
    dqkvb_ref[...] = row_sum(gqkv[...].astype(F32))
    dqk_ref[...] = dg(mlow_ref[...], gqkv[:, :2 * half], TN).astype(BF16).reshape(dqk_ref.shape)
    store(dvo_ref, slice(0, half), dg(mlow_ref[...], gqkv[:, 2 * half:], TN))


def attn_bwd_plain_kernel(*refs):
    ins, outs, scratch = refs[:14], refs[14:20], refs[20:]
    own_ref, send_ref = outs[:2]

    def finish(send, own):
        send_ref[...] = send()
        own_ref[...] = own()

    attn_bwd_kernel(*ins, *outs[2:], *scratch, finish)


def attn_bwd_fold_kernel(*refs):
    ins, (ddl, ddr, dul, dur, first_l, across_r) = refs[:13], refs[13:19]
    outs, (gm_out, out_dl, out_dr, out_ul, out_ur) = refs[19:23], refs[23:28]
    scratch, (segc, send, got, gm), bufs, (sem_f, sem_g) = refs[28:37], refs[37:41], refs[41:63], refs[63:]
    p = Place()
    straight = p.core == p.y
    meet_all(p)
    segc[...] = columns(ins[6])[:, 0:1].astype(jnp.int32)
    early = [Fold(0, p, ddl, sem_f, 0, first_l, *bufs[0:5], out_dl), Fold(1, p, ddr, sem_f, 1, bufs[5], across_r, *bufs[6:10], out_dr)]
    late = [Fold(0, p, dul, sem_f, 2, *bufs[10:16], out_ul), Fold(1, p, dur, sem_f, 3, *bufs[16:22], out_ur)]

    def step(folds, n, wait=True):
        for f in folds:
            if wait:
                f.wait(n - 1)
            f.start(n)

    step(late, 0, False)
    step(early, 1, False)

    def beside(pair):
        @pl.when(pair == 0)
        def _():
            step(early, 2)

        @pl.when(pair == 1)
        def _():
            step(early, 3)
            step(late, 1)

        @pl.when(pair == 2)
        def _():
            step(late, 2)
            step(early, 4)

    to_sibling = push(send, got, sem_g, (0,), p.at(core=1 - p.core))
    turn = push(gm, gm_out, sem_g, (1,), p.at(core=p.y, y=p.core))

    def finish(give, own):
        send[...] = give()
        to_sibling.start()
        step(late, 3)
        mine = own()
        to_sibling.wait()
        value = (mine + got[...].astype(F32)).astype(BF16)

        @pl.when(straight)
        def _():
            gm_out[...] = value

        @pl.when(jnp.logical_not(straight))
        def _():
            gm[...] = value
            turn.start()

    attn_bwd_kernel(*ins[:6], segc, ins[6].at[0:1], *ins[7:], *outs, *scratch, finish, beside)
    step(late, 4)
    pl.when(jnp.logical_not(straight))(turn.wait)


def share_and_add(vec, got, sems, p):
    hops = [p.at(core=1 - p.core), p.at(y=1 - p.y), p.at(x=1 - p.x)]
    for n, device in enumerate(hops):
        c = push(vec.at[n], got.at[n], sems, (n,), device)
        c.start()
        c.wait()
        vec[n + 1] = vec[n] + got[n]
    along = [push(vec.at[3], got.at[2 + o], sems, (2 + o,), p.at(z=lax.rem(p.z + o, 4))) for o in (1, 2, 3)]
    for c in along:
        c.start()
    for c in along:
        c.wait()
    return vec[3] + got[3] + got[4] + got[5]


def conv_fold_kernel(*refs):
    (small_ref, xq, w_ref, slope_ref, gm_ref, dqk, dvo, sums2, sums1, dqkvb, dub, stat_conv, stat_attn,
     in_ref, dconv_ref, out_qk, out_vo, vec_out, ub_out, rms_out, spread, dq, d_ref, gq) = refs[:24]
    seg_ref, mask_ref, db_ref, dm_ref, d_all, got_c, sum_c, got_x, sum_x, got_z, vec, got_v = refs[24:36]
    folds_bufs, (sem_c, sem_x, sem_z, sem_fold, sem_vec) = refs[36:48], refs[48:]
    p = Place()
    meet(partners(p))
    cols = columns(small_ref)
    seg_ref[...] = cols[:, 0:1].astype(jnp.int32)
    mask_ref[...] = cols[:, 1:2].astype(jnp.int32)
    groups = 8
    folds = [Fold(0, p, dqk, sem_fold, 0, *folds_bufs[:6], out_qk), Fold(0, p, dvo, sem_fold, 1, *folds_bufs[6:], out_vo)]
    for f in folds:
        f.start(0)

    def store(g, dw):
        d_all[g] = dw.reshape(d_all.shape[1:])

    to_c = lambda g: push(d_all.at[g, :, :, 1 - p.core], got_c.at[g], sem_c, (g,), p.at(core=1 - p.core))
    to_x = lambda g: push(sum_c.at[g, :, 1 - p.x], got_x.at[g], sem_x, (g,), p.at(x=1 - p.x))
    to_z = lambda g: [push(sum_x.at[g, lax.rem(p.z + o, 4)], got_z.at[g, o - 1], sem_z, (g, o - 1), p.at(z=lax.rem(p.z + o, 4)))
                      for o in (1, 2, 3)]
    wide = lambda v: v.astype(F32)

    def beside(g):
        @pl.when(g < groups)
        def _():
            to_c(g).start()

        @pl.when(jnp.logical_and(g >= 1, g <= groups))
        def _():
            k = g - 1
            to_c(k).wait()
            for z in range(4):
                for x in range(2):
                    sum_c[k, z, x] = (wide(d_all[k, z, x, p.core]) + wide(got_c[k, z, x])).astype(BF16)
            to_x(k).start()

        @pl.when(jnp.logical_and(g >= 2, g <= groups + 1))
        def _():
            k = g - 2
            to_x(k).wait()
            for z in range(4):
                sum_x[k, z] = (wide(sum_c[k, z, p.x]) + wide(got_x[k, z])).astype(BF16)
            for c in to_z(k):
                c.start()

        for n, turn in ((1, 3), (2, 4), (3, 6)):
            @pl.when(g == turn)
            def _(n=n):
                for f in folds:
                    f.wait(n - 1)
                for f in folds:
                    f.start(n)

    conv_bwd_kernel(seg_ref, xq, w_ref, slope_ref, gm_ref, mask_ref, None, in_ref, db_ref, dm_ref,
                    spread, dq, d_ref, gq, 2, beside, store)
    width = vec.shape[2]
    half = width // 2
    by_core = (lax.broadcasted_iota(jnp.int32, (1, width), 1) // half == p.core).astype(F32)
    by_y = (lax.broadcasted_iota(jnp.int32, (1, width), 1) // half == p.y).astype(F32)
    twice = lambda v: jnp.concatenate([v, v], axis=1)
    is_core = lambda c: (p.core == c).astype(F32)
    frames = jnp.sum(wide(seg_ref[...] != 0), axis=0, keepdims=True)
    rows = [twice(dm_ref[...]) * by_y, twice(db_ref[...]) * by_y, twice(dqkvb[:, :half]) * by_core, twice(dqkvb[:, 2 * half:]) * by_core,
            sums1[2:3] * by_core, sums1[0:1] * by_core, sums1[1:2] * by_core, sums2[4:5] * by_core, sums2[2:3] * by_core, sums2[3:4] * by_core,
            dub[:, :width] * is_core(0), dub[:, width:] * is_core(0), dub[:, :width] * is_core(1), dub[:, width:] * is_core(1),
            twice(stat_conv[...]) * by_core * 0.5, stat_attn[...] * by_core, sums2[0:1] * by_core, sums2[1:2] * by_core,
            jnp.broadcast_to(frames * 0.5, (1, width))]
    rows.append(jnp.zeros((24 - len(rows), width), F32))
    vec[0] = jnp.concatenate(rows, axis=0)
    total = share_and_add(vec, got_v, sem_vec, p)
    vec_out[...] = total[:16]
    ub_out[...] = jnp.where(p.y == 0, total[10:12], total[12:14])
    powers = jnp.sum(total[14:18], axis=1, keepdims=True)
    rms_out[...] = jnp.broadcast_to(jnp.sqrt(powers / (total[18:19, 0:1] * width)), (4, 128))
    for f in folds:
        f.wait(3)
        f.start(4)
    for k in range(groups):
        for c in to_z(k):
            c.wait()
        piece = wide(sum_x[k, p.z]) + wide(got_z[k, 0]) + wide(got_z[k, 1]) + wide(got_z[k, 2])
        dq_at = slice(k * CG, (k + 1) * CG)
        gq[dq_at, 0:TAPS * CG] = piece
    dconv_ref[...] = gq[:, 0:TAPS * CG].T


def one_row(v):
    return v.astype(F32)[None]


def flat_turn(n_all):
    return [(f, f // 4 * 4 + (f % 2) * 2 + (f // 2) % 2) for f in range(n_all)]


def shapes(rows, width, ff):
    half = width // 2
    heads = half // HD
    spread_width = -(-(rows + 7 * 64 + 64) // 128) * 128
    blocks = KW // TAPS
    low, wide = lambda *s: (s, BF16), lambda *s: (s, F32)
    return dict(
        half=half, spread_width=spread_width, blocks=blocks,
        attn_out=[wide(rows, width), low(rows, width), low(rows, 3 * half), low(rows, half), wide(heads, rows), low(rows, width)],
        attn_scratch=[low(half, rows)] * 3,
        ffn_out=[wide(rows, width), wide(rows, 1), low(rows, width), low(rows, ff), low(rows, ff), low(rows, width), wide(1, width)],
        back_scratch=[wide(rows, width), low(rows, half), low(half, rows), low(half, rows), low(half, rows), low(half, rows),
                      wide(rows, 128), wide(rows, 128), low(rows, 3 * half)],
    )


def local_close(hidden_in, segment_ids, time_mask, mask_embed, conv_weight, conv_bias, query_weight, key_weight,
                value_weight, query_bias, value_bias, out_weight, out_bias, first_gain, first_shift, up_weight, up_bias,
                down_weight, down_bias, second_gain, second_shift, cotangent):
    _, rows, width = hidden_in.shape
    ff = up_weight.shape[1]
    n = ff // 2
    sh = shapes(rows, width, ff)
    half, sw, blocks = sh["half"], sh["spread_width"], sh["blocks"]
    low, wide = lambda *s: (s, BF16), lambda *s: (s, F32)
    down_t = down_weight.T
    shards = [jnp.concatenate([query_weight, key_weight], axis=1), jnp.concatenate([value_weight, out_weight.T], axis=1),
              up_weight[:, :n], up_weight[:, n:], down_t[:, :n], down_t[:, n:]]
    bias = lax.ppermute(jnp.concatenate([query_bias, value_bias, up_bias])[None], BOTH, flat_turn(32)).astype(F32)
    qb, vb, ub = bias[:, :half], bias[:, half:2 * half], bias[:, 2 * half:]
    small = jnp.concatenate([segment_ids, time_mask, jnp.zeros((6, rows), jnp.int32)], axis=0)
    emb, g1, s1 = one_row(mask_embed), one_row(first_gain), one_row(first_shift)
    seats = (4, 2, 2)
    wall = [low(*seats, 48, n)]

    xq, slope, conv_t, hid_s, cot_s, small_s, conv_full, w_qk, w_vo, w_ul, w_ur = call(
        conv_gather_kernel,
        [low(half, sw), wide(rows, half), low(rows, half), low(rows, width), low(rows, width), ((8, rows), jnp.int32),
         low(*seats, half, TAPS * CG)] + wall * 4,
        [low(rows, sw), wide(blocks * CG, sw), wide(half, sw), low(rows, half), low(*seats, half, TAPS * CG), low(4, 48, n),
         ((rows, 1), jnp.int32), low(rows, half)],
        small, hidden_in[0], cotangent[0], emb, conv_weight.T, one_row(conv_bias), *shards[:4],
        hbm_in=(4,), hbm_out=(3, 4, 5, 6, 7, 8, 9, 10),
        sems=((9,), (2, 8), (4, 1) + seats, (1,) + seats, (4, 4) + seats, (4,) + seats), meeting=1)
    flat = lambda w: w.reshape(width, n)
    w_qk, w_vo, w_ul, w_ur = flat(w_qk), flat(w_vo), flat(w_ul), flat(w_ur)
    mixed, mlow, qkv, ctx, lse, part1, other1, stat_conv, w_dl, w_dr = call(
        attn_gather_kernel, sh["attn_out"] + [low(rows, width), wide(1, half)] + wall * 2,
        sh["attn_scratch"] + [low(2, rows, half), low(2, 48, n), ((rows, 1), jnp.int32), ((rows, 1), jnp.int32)],
        hid_s, conv_t, small_s, emb, w_qk, w_vo, qb, vb, *shards[4:],
        hbm_out=(8, 9), sems=((2,), (2, 3), (4, 2) + seats, (2,) + seats, (4,), (4,)), meeting=2)
    w_dl, w_dr = flat(w_dl), flat(w_dr)
    n1, r1, nlow, hidden, hslope, part2, stat_attn, other2 = call(
        ffn_fwd_give_kernel, sh["ffn_out"] + [low(rows, width)], [((rows, 1), jnp.int32)],
        mixed, part1, other1, small_s, one_row(out_bias), g1, s1, w_ul, w_ur, ub, w_dl, w_dr, sems=((2, 4),), meeting=3)
    grad = low(*seats, 48, n)
    layer_out, gr2, part3, ddl, ddr, dul, dur, sums2, d_ub, other3, first_l, across_r = call(
        ffn_bwd_fold_kernel,
        [low(rows, width), wide(rows, width), low(rows, width)] + [grad] * 4 + [wide(5, width), wide(1, ff), low(rows, width), grad, low(4, 2, 48, n)],
        [low(rows, width), low(rows, ff), ((rows, 1), jnp.int32)],
        n1, g1, s1, part2, other2, small_s, one_row(down_bias), one_row(second_gain), one_row(second_shift), cot_s, nlow,
        hidden, hslope, w_ul, w_ur, w_dl, w_dr, sems=((2, 4), (2, 4), (2, 2)), meeting=4)
    own = [wide(48, n)]
    kinds = [fold_scratch(0, n)[1:], fold_scratch(1, n)[:1] + fold_scratch(1, n)[2:], fold_scratch(0, n), fold_scratch(1, n)]
    dqk, dvo, sums1, d_qkvb, gm, o_dl, o_dr, o_ul, o_ur = call(
        attn_bwd_fold_kernel,
        [grad, grad, wide(3, width), wide(1, 3 * half), low(rows, half)] + own * 4,
        sh["back_scratch"] + [((rows, 1), jnp.int32), low(rows, half), low(rows, half), low(rows, half)] + sum(kinds, []),
        gr2, part3, other3, n1, r1, g1, small_s, ctx, qkv, lse, mlow, w_qk, w_vo, ddl, ddr, dul, dur, first_l, across_r,
        sems=((2, 4, 6), (2, 2)), meeting=5)
    input_grad, d_conv, o_qk, o_vo, vec, d_ub, rms = call(
        conv_fold_kernel,
        [wide(rows, half), wide(TAPS * CG, half)] + own * 2 + [wide(16, width), wide(2, width), wide(4, 128)],
        [low(rows, sw), low(half, sw), low(blocks * CG, sw), wide(half, sw), ((rows, 1), jnp.int32), ((rows, 1), jnp.int32), wide(1, half), wide(1, half),
         low(8, *seats, CG, TAPS * CG), low(8, 4, 2, CG, TAPS * CG), low(8, 4, 2, CG, TAPS * CG), low(8, 4, CG, TAPS * CG),
         low(8, 4, CG, TAPS * CG), low(8, 3, CG, TAPS * CG), wide(4, 24, width), wide(6, 24, width)] + fold_scratch(0, n) * 2,
        small, xq, conv_full, slope, gm, dqk, dvo, sums2, sums1, d_qkvb, d_ub, stat_conv, stat_attn,
        sems=((2, 8), (2, 8), (2, 8, 3), (2, 2, 6), (2, 6)), meeting=6)
    y = lax.axis_index("mp")
    mine = lambda r: lax.dynamic_slice_in_dim(vec[r], y * half, half, 0)
    return (layer_out[None], input_grad[None], mine(0), d_conv, mine(1), o_qk[:, :half], o_qk[:, half:], o_vo[:, :half], mine(2), mine(3),
            o_vo[:, half:].T, vec[4], vec[5], vec[6], jnp.concatenate([o_ul, o_ur], axis=1), d_ub.reshape(ff),
            jnp.concatenate([o_dl, o_dr], axis=1).T, vec[7], vec[8], vec[9], rms[:, 0])


def local_any(n_dp, hidden_in, segment_ids, time_mask, mask_embed, conv_weight, conv_bias, query_weight, key_weight,
          value_weight, query_bias, value_bias, out_weight, out_bias, first_gain, first_shift, up_weight, up_bias,
          down_weight, down_bias, second_gain, second_shift, cotangent):
    _, rows, width = hidden_in.shape
    ff = up_weight.shape[1]
    n = ff // 2
    sh = shapes(rows, width, ff)
    half, spread_width, blocks = sh["half"], sh["spread_width"], sh["blocks"]
    part = lax.axis_index("mp")
    core = lax.rem(lax.axis_index("dp"), 2)
    n_all = 2 * n_dp
    turn = flat_turn(n_all)
    sibling = [(f, f ^ 2) for f in range(n_all)]
    core_groups = [[f for f in range(n_all) if (f // 2) % 2 == c] for c in range(2)]
    swap = lambda v: lax.ppermute(v, BOTH, sibling)
    turned = lambda v: lax.ppermute(v, BOTH, turn)
    mine = part == core

    down_t = down_weight.T
    w_shards = [jnp.concatenate([query_weight, key_weight], axis=1), jnp.concatenate([value_weight, out_weight.T], axis=1),
                up_weight[:, :n], up_weight[:, n:], down_t[:, :n], down_t[:, n:]]
    conv_full = lax.all_gather(conv_weight, "dp", axis=0, tiled=True)
    conv_full = conv_full.reshape(blocks, TAPS * CG, half).swapaxes(1, 2)
    w_qk, w_vo, w_ul, w_ur, w_dl, w_dr = (
        lax.all_gather(turned(w), BOTH, axis=0, tiled=True, axis_index_groups=core_groups) for w in w_shards)
    bias = turned(jnp.concatenate([query_bias, value_bias, up_bias])[None])
    qb, vb, ub = (b.astype(F32) for b in (bias[:, :half], bias[:, half:2 * half], bias[:, 2 * half:]))
    row = one_row

    hid, cot = hidden_in[0], cotangent[0]
    small = jnp.concatenate([segment_ids, time_mask], axis=0)
    hid_s = jnp.where(mine, hid, swap(hid))
    cot_s = jnp.where(mine, cot, swap(cot))
    small_s = jnp.where(mine, small, swap(small))
    seg_c, mask_c = segment_ids.reshape(rows, 1), time_mask.reshape(rows, 1)
    seg_sr, seg_sc, mask_sc = small_s[0:1], small_s[0].reshape(rows, 1), small_s[1].reshape(rows, 1)

    masked = mask_c.astype(F32)
    hid_half = lax.dynamic_slice_in_dim(hid, part * half, half, 1).astype(F32)
    emb_half = lax.dynamic_slice_in_dim(mask_embed, part * half, half, 0).astype(F32)
    start_half = (hid_half + masked * (emb_half - hid_half)).astype(BF16)
    low, wide = lambda *s: (s, BF16), lambda *s: (s, F32)
    def conv_kernel(seg_ref, x_ref, w_ref, b_ref, low_ref, slope_ref, xq, spread, y_ref, ot):
        conv_fwd_kernel(seg_ref, x_ref, w_ref, b_ref, low_ref, slope_ref, spread, xq, y_ref, ot)

    conv_low, conv_slope, xq = call(
        conv_kernel, [low(rows, half), wide(rows, half), low(half, spread_width)],
        [low(rows, spread_width), wide(blocks * CG, spread_width), wide(half, spread_width)],
        seg_c, start_half, conv_full, row(conv_bias))
    conv_s = turned(conv_low)
    conv_o = swap(conv_s)
    c0, c1 = jnp.where(core == 0, conv_s, conv_o), jnp.where(core == 0, conv_o, conv_s)

    def attn_kernel(*refs):
        attn_fwd_kernel(*refs[:7], refs[7:9], *refs[9:])

    mixed, mlow, qkv, ctx, lse, part1, stat_conv = call(
        attn_kernel, sh["attn_out"] + [wide(1, half)], sh["attn_scratch"],
        hid_s, c0, c1, mask_sc, seg_sc, seg_sr, row(mask_embed), w_qk, w_vo, qb, vb)
    n1, r1, nlow, hidden, slope, part2, stat_attn = call(
        ffn_fwd_kernel, sh["ffn_out"], [],
        mixed, part1, swap(part1), seg_sc, row(out_bias), row(first_gain), row(first_shift), w_ul, w_ur, ub, w_dl, w_dr)
    out_s, gr2, part3, ddl, ddr, dul, dur, sums2, d_ub = call(
        ffn_bwd_kernel,
        [low(rows, width), wide(rows, width), low(rows, width)] + [low(width, n)] * 4 + [wide(5, width), wide(1, ff)],
        [low(rows, width), low(rows, ff)],
        n1, row(first_gain), row(first_shift), part2, swap(part2), seg_sc, row(down_bias), row(second_gain), row(second_shift), cot_s, nlow,
        hidden, slope, w_ul, w_ur, w_dl, w_dr)
    other_out = lax.ppermute(out_s, "mp", [(0, 1), (1, 0)])
    layer_out = jnp.where(mine, out_s, other_out)[None]
    own, send, dqk, dvo, sums1, d_qkvb = call(
        attn_bwd_plain_kernel,
        [wide(rows, half), low(rows, half), low(width, 2 * half), low(width, 2 * half), wide(3, width), wide(1, 3 * half)], sh["back_scratch"],
        gr2, part3, swap(part3), n1, r1, row(first_gain), seg_sc, seg_sr, ctx, qkv, lse, mlow, w_qk, w_vo)
    gm_half = turned((own + swap(send).astype(F32)).astype(BF16))
    d_conv, input_grad, d_cb, d_me = call(
        conv_bwd_kernel,
        [low(blocks, half, TAPS * CG), wide(rows, half), wide(1, half), wide(1, half)],
        [low(rows, spread_width), low(half, spread_width), low(blocks * CG, spread_width), wide(half, spread_width)],
        seg_c, xq, conv_full, conv_slope, gm_half, mask_c)

    d_wall = jnp.concatenate([dqk, dvo, dul, dur, ddl, ddr], axis=1)
    d_wall = turned(lax.psum_scatter(d_wall, BOTH, scatter_dimension=0, tiled=True, axis_index_groups=core_groups)).astype(F32)
    d_conv = lax.psum_scatter(d_conv.swapaxes(1, 2).reshape(blocks * TAPS * CG, half), "dp", scatter_dimension=0, tiled=True).astype(F32)
    once = (jnp.arange(width) // half == core).astype(F32)[None]
    put = lambda v, which: lax.dynamic_update_slice(jnp.zeros((1, 2 * v.shape[1]), F32), v, (0, which * v.shape[1]))
    full = jnp.concatenate([sums2, sums1, stat_attn], axis=0) * once
    pieces = [put(d_me, part), put(d_cb, part), put(d_qkvb[:, :half], core), put(d_qkvb[:, 2 * half:], core), put(d_ub, core)]
    stats = jnp.stack([jnp.sum(stat_conv) * 0.5, jnp.sum(full[8]), jnp.sum(full[0]), jnp.sum(full[1]), jnp.sum((seg_c != 0).astype(F32)) * 0.5])
    flat = jnp.concatenate([jnp.concatenate(pieces, axis=1)[0], full[2:8].reshape(-1), stats])
    flat = lax.psum(flat, BOTH)
    at = 0
    sections = []
    for size in (width, width, width, width, 2 * ff) + (width,) * 6 + (5,):
        sections.append(flat[at:at + size])
        at += size
    me, cb, dqb, dvb, dub, g2, s2, db, g1, s1, ob, st = sections
    half_of = lambda v: lax.dynamic_slice_in_dim(v, part * (v.shape[0] // 2), v.shape[0] // 2, 0)
    stream_rms = jnp.sqrt(st[:4] / (st[4] * width))
    q_, k_, v_, o_, u_, d_ = jnp.split(d_wall, [half, 2 * half, 3 * half, 4 * half, 4 * half + ff], axis=1)
    return (layer_out, input_grad[None], half_of(me), d_conv, half_of(cb), q_, k_, v_, half_of(dqb), half_of(dvb), o_.T, ob, g1, s1,
            u_, half_of(dub), d_.T, db, g2, s2, stream_rms)


def solution(mesh):
    split, half, turn = P("dp", "mp"), P("mp"), P("mp", "dp")
    whole = P()
    rows = P("dp", None, None)
    return jax.shard_map(
        local_close if mesh.shape["dp"] == 16 else functools.partial(local_any, mesh.shape["dp"]),
        mesh=mesh,
        in_specs=(rows, P("dp", None), P("dp", None), whole, split, half, split, split, split, half, half, turn, whole, whole, whole,
                  split, half, turn, whole, whole, whole, rows),
        out_specs=(rows, P("dp", None, "mp"), half, split, half, split, split, split, half, half, turn, whole, whole, whole,
                   split, half, turn, whole, whole, whole, whole),
        check_vma=False,
    )
```

```python
import functools

import jax
import jax.numpy as jnp
from jax import lax
from jax.experimental import pallas as pl
from jax.experimental.pallas import tpu as pltpu
from jax.sharding import PartitionSpec as P

HD = 64
KW = 128
CG = 48
TAPS = 8
EPS = 1e-05
F32 = jnp.float32
BF16 = jnp.bfloat16
NN = (((1,), (0,)), ((), ()))
NT = (((1,), (1,)), ((), ()))
TN = (((0,), (0,)), ((), ()))
BOTH = ("dp", "mp")
CROSS_AT = (3, 5, 6, 8, 9, 11, 13, 15)
FOLD_AT = (8, 11, 13)
TOTAL_AT = (2, 4, 6)
SHOW_AT = 10
FOLD_KINDS = (0, 1)


def dg(a, b, dims):
    return lax.dot_general(a, b, dims, preferred_element_type=F32)


def gelu_parts(v):
    t = 1.0 / (1.0 + (0.3275911 * 0.7071067811865476) * jnp.abs(v))
    e = jnp.exp(-0.5 * v * v)
    poly = t * (0.254829592 + t * (-0.284496736 + t * (1.421413741 + t * (-1.453152027 + t * 1.061405429))))
    tail = 0.5 * poly * e
    return jnp.where(v >= 0, 1.0 - tail, tail), e


def gelu_and_slope(v):
    phi, e = gelu_parts(v)
    return v * phi, phi + v * e * 0.3989422804014327


def call(kernel, outs, scratch, *args, hbm_in=(), hbm_out=(), sems=(), meeting=None):
    space = lambda here: pl.BlockSpec(memory_space=pl.ANY if here else pltpu.VMEM)
    return pl.pallas_call(
        kernel,
        out_shape=[jax.ShapeDtypeStruct(s, d) for s, d in outs],
        in_specs=[space(i in hbm_in) for i in range(len(args))],
        out_specs=[space(i in hbm_out) for i in range(len(outs))],
        scratch_shapes=[pltpu.VMEM(s, d) for s, d in scratch] + [pltpu.SemaphoreType.DMA(s) for s in sems],
        compiler_params=pltpu.CompilerParams(vmem_limit_bytes=60 * 2**20, has_side_effects=bool(sems), collective_id=meeting),
    )(*args)


def split_low(v):
    hi = v.astype(BF16)
    return hi, (v - hi.astype(F32)).astype(BF16)


def spread_matrix(seg, length, width):
    rank = jnp.where(seg == 0, 7, seg - 1)
    pos = lax.broadcasted_iota(jnp.int32, (length, 1), 0) + 64 * rank + 8
    hit = pos == lax.broadcasted_iota(jnp.int32, (length, width), 1)
    return hit.astype(F32).astype(BF16)


def rolled(x, left):
    width = x.shape[1]
    left = left % width
    return x if left == 0 else pltpu.roll(x, width - left, 1)


def tap_patches(xg):
    return jnp.concatenate([rolled(xg, r) for r in range(TAPS)], axis=0)


def nothing(*_):
    pass


def block_rows(w_ref, at):
    w = w_ref[(slice(None),) * (len(w_ref.shape) - 2) + (at, slice(None))]
    return w.reshape(-1, w.shape[-1])


def conv_plane(w_ref, patches, ot, plane, first):
    rows = w_ref.shape[0] * w_ref.shape[1]
    per = rows * TAPS

    def body(g, carry):
        at = pl.ds(pl.multiple_of(g * CG, 16), CG)
        y = dg(block_rows(w_ref, at), patches[g], NN)
        acc = y[0:CG, :]
        for j in range(1, rows):
            acc = acc + rolled(y[j * CG:(j + 1) * CG, :], TAPS * j)
        width = acc.shape[1]
        acc = pltpu.roll(acc, lax.rem(width + 64 - per * plane, width), 1)
        if first:
            ot[at, :] = acc
        else:
            ot[at, :] += acc
        return carry

    lax.fori_loop(0, ot.shape[0] // CG, body, 0)


def conv_prepare(seg_ref, x_ref, spread, xq, patches):
    length, width = spread.shape
    spread[...] = spread_matrix(seg_ref[...], length, width)
    xq[...] = dg(x_ref[...], spread[...], TN).astype(BF16)

    def body(g, carry):
        patches[g] = tap_patches(xq[pl.ds(pl.multiple_of(g * CG, 16), CG), :])
        return carry

    lax.fori_loop(0, xq.shape[0] // CG, body, 0)


def conv_finish(seg_ref, b_ref, spread, ot, low_ref, slope_ref, cols):
    hi, lo = split_low(ot[cols, :])
    pre = dg(spread[...], hi, NT) + dg(spread[...], lo, NT) + b_ref[:, cols]
    valid = (seg_ref[...] != 0).astype(F32)
    value, slope = gelu_and_slope(pre)
    low_ref[:, cols] = (valid * value).astype(BF16)
    slope_ref[:, cols] = valid * slope


def conv_fwd_kernel(seg_ref, x_ref, w_ref, b_ref, low_ref, slope_ref, xq, spread, patches, ot):
    conv_prepare(seg_ref, x_ref, spread, xq, patches)
    for plane in range(w_ref.shape[0]):
        conv_plane(w_ref.at[plane], patches, ot, plane, plane == 0)
    conv_finish(seg_ref, b_ref, spread, ot, low_ref, slope_ref, slice(0, x_ref.shape[1]))


def conv_bwd_kernel(seg_ref, xq, w_ref, slope_ref, gm_ref, mask_ref, dw_ref, in_ref, db_ref, dm_ref,
                    spread, dq, d_ref, gq, ready=nothing, beside=nothing, store=None, summed=nothing):
    length, width = spread.shape
    blocks = KW // TAPS
    groups = xq.shape[0] // CG
    spread[...] = spread_matrix(seg_ref[...], length, width)
    dpre = (slope_ref[...] * gm_ref[...].astype(F32)).astype(BF16)
    db_ref[...] = jnp.sum(dpre.astype(F32), axis=0, keepdims=True)
    ready()
    dq[...] = dg(dpre, spread[...], TN).astype(BF16)
    place = lambda g: pl.ds(pl.multiple_of(g * CG, 16), CG)

    def shifts(g):
        dqg = dq[place(g), :]
        for b in range(blocks):
            d_ref[b * CG:(b + 1) * CG, :] = rolled(dqg, 64 - TAPS * b)
        return d_ref[...]

    def weight_body(g, carry):
        dw = dg(shifts(g), tap_patches(xq[place(g), :]), NT).astype(BF16).reshape(blocks, CG, TAPS * CG)
        if store is None:
            dw_ref[:, place(g), :] = dw
        else:
            store(g, dw)
        beside(g)
        return carry

    def input_body(g, carry):
        v = dg(block_rows(w_ref, place(g)), shifts(g), TN)
        acc = v[0:CG, :]
        for r in range(1, TAPS):
            acc = acc + rolled(v[r * CG:(r + 1) * CG, :], -r)
        gq[place(g), :] = acc
        beside(groups + g)
        return carry

    lax.fori_loop(0, groups, weight_body, 0)
    lax.fori_loop(0, groups, input_body, 0)
    hi, lo = split_low(gq[...])
    grad = dg(spread[...], hi, NT) + dg(spread[...], lo, NT) + gm_ref[...].astype(F32)
    masked = mask_ref[...].astype(F32)
    dm_ref[...] = jnp.sum(masked * grad, axis=0, keepdims=True)
    summed()
    in_ref[...] = (1.0 - masked) * grad


class Place:
    def __init__(self):
        self.dp, self.y = lax.axis_index("dp"), lax.axis_index("mp")
        self.z, self.x, self.core = self.dp // 4, lax.rem(self.dp // 2, 2), lax.rem(self.dp, 2)

    def at(self, z=None, x=None, core=None, y=None):
        pick = lambda new, old: old if new is None else new
        dp = pick(z, self.z) * 4 + pick(x, self.x) * 2 + pick(core, self.core)
        return {"dp": dp, "mp": pick(y, self.y)}


def push(src, dst, sems, index, device):
    send, recv = sems if isinstance(sems, tuple) else (sems.at[0], sems.at[1])
    return pltpu.make_async_remote_copy(
        src_ref=src, dst_ref=dst, send_sem=send.at[index], recv_sem=recv.at[index],
        device_id=device, device_id_type=pl.DeviceIdType.MESH)


def meet(devices):
    here = pltpu.get_barrier_semaphore()
    for device in devices:
        pl.semaphore_signal(here, inc=1, device_id=device, device_id_type=pl.DeviceIdType.MESH)
    pl.semaphore_wait(here, len(devices))


def partners(p):
    return [p.at(z=lax.rem(p.z + o, 4)) for o in (1, 2, 3)] + [p.at(x=1 - p.x), p.at(core=1 - p.core), p.at(y=1 - p.y)]


def meet_all(p):
    crooked = p.core != p.y
    pl.when(crooked)(lambda: meet(partners(p) + [p.at(core=p.y, y=p.core)]))
    pl.when(jnp.logical_not(crooked))(lambda: meet(partners(p)))


class LineGather:
    UP, DOWN, ACROSS, LAST = range(4)

    def __init__(self, place, own, buf, send, recv, k, third, x_first=True):
        p = self.p = place
        self.own, self.buf, self.send, self.recv, self.k, self.x_first = own, buf, send, recv, k, x_first
        self.t = p.core if third == "core" else p.y
        over_x, over_t = p.at(x=1 - p.x), p.at(**{third: 1 - self.t})
        self.to = [p.at(z=jnp.minimum(p.z + 1, 3)), p.at(z=jnp.maximum(p.z - 1, 0))] + ([over_x, over_t] if x_first else [over_t, over_x])

    def slot(self, z, across=False, last=False):
        flip = lambda v, yes: 1 - v if yes else v
        x, t = (across, last) if self.x_first else (last, across)
        return (z, flip(self.p.x, x), flip(self.t, t))

    def copy(self, way, slot, src=None):
        at = (self.k,) + slot
        return pltpu.make_async_remote_copy(
            src_ref=self.buf.at[slot] if src is None else src, dst_ref=self.buf.at[slot], send_sem=self.send.at[(way,) + at],
            recv_sem=self.recv.at[at], device_id=self.to[way], device_id_type=pl.DeviceIdType.MESH)

    def walk(self, d, start, finish):
        p = self.p
        if d == 0:
            mine = self.slot(p.z)
            pl.when(p.z < 3)(lambda: start(self.UP, mine, True))
            pl.when(p.z > 0)(lambda: start(self.DOWN, mine, True))
            start(self.ACROSS, mine, True)
            start(self.LAST, mine, True)
            return

        def passing(z, way, further):
            slot = self.slot(z)
            finish(slot)
            pl.when(further)(lambda: start(way, slot, False))
            start(self.ACROSS, slot, False)
            start(self.LAST, slot, False)

        def crossed(z):
            slot = self.slot(z, across=True)
            finish(slot)
            start(self.LAST, slot, False)

        if d < 4:
            pl.when(p.z >= d)(lambda: passing(p.z - d, self.UP, p.z < 3))
            pl.when(p.z + d <= 3)(lambda: passing(p.z + d, self.DOWN, p.z > 0))
        if d == 1:
            crossed(p.z)
        else:
            pl.when(p.z >= d - 1)(lambda: crossed(p.z - d + 1))
            pl.when(p.z + d - 1 <= 3)(lambda: crossed(p.z + d - 1))

    def begin(self, way, slot, own):
        self.copy(way, slot, self.own if own else None).start()

    def round(self, d):
        self.walk(d, self.begin, lambda slot: self.copy(0, slot).wait_recv())

    def drain(self):
        for z in range(4):
            for across in (False, True):
                self.copy(0, self.slot(z, across, True)).wait_recv()
        self.sent()

    def sent(self):
        for d in range(5):
            self.walk(d, lambda way, slot, own: self.copy(way, slot, self.own if own else None).wait_send(), nothing)


class Fold:
    def __init__(self, kind, place, grad, sems, k, first, across, out1, cur, mid, last, out):
        self.kind, self.p, self.d, self.first, self.across, self.out1 = kind, place, grad, first, across, out1
        self.cur, self.mid, self.last, self.out = cur, mid, last, out
        p = place
        self.straight = p.core == p.y
        copy = lambda src, dst, n, dev: push(src, dst, sems, (k, n), dev)
        home, partner, sibling = p.at(y=p.core), p.at(x=1 - p.x), p.at(core=1 - p.core)
        away = grad.at[:, 1 - p.x]
        if kind == 0:
            self.over_y = copy(grad, first, 0, home)
            self.to_sibling = copy(out1, cur, 1, sibling)
            self.over_x = copy(cur.at[:, 1 - p.x], across, 2, partner)
        else:
            self.over_x = copy(away, across, 2, partner)
            self.over_y = copy(mid, first, 0, home)
            self.to_sibling = copy(out1, cur, 1, sibling)
        held = mid if kind == 0 else cur
        self.along = [copy(held.at[lax.rem(p.z + o, 4)], last.at[o - 1], 2 + o, p.at(z=lax.rem(p.z + o, 4))) for o in (1, 2, 3)]
        self.held = held

    def one_way(self, copy, sends, wait):
        pl.when(sends)(copy.wait_send if wait else copy.start)
        if wait:
            pl.when(jnp.logical_not(sends))(copy.wait_recv)

    def start(self, n):
        p, wide = self.p, lambda ref: ref.astype(F32)
        crooked = jnp.logical_not(self.straight)
        if n == 0:
            if self.kind == 0:
                self.one_way(self.over_y, crooked, False)
            else:
                self.over_x.start()
        elif n == 1:
            if self.kind == 0:
                @pl.when(self.straight)
                def _():
                    for z in range(4):
                        for x in range(2):
                            self.cur[z, x] = (wide(self.d[z, x, p.core]) + wide(self.first[z, x, p.core])).astype(BF16)
                            self.out1[z, x] = (wide(self.d[z, x, 1 - p.core]) + wide(self.first[z, x, 1 - p.core])).astype(BF16)
                    self.to_sibling.start()
            else:
                for z in range(4):
                    for c in range(2):
                        self.mid[z, c] = (wide(self.d[z, p.x, c]) + wide(self.across[z, c])).astype(BF16)
                self.one_way(self.over_y, crooked, False)
        elif n == 2:
            if self.kind == 0:
                self.over_x.start()
            else:
                @pl.when(self.straight)
                def _():
                    for z in range(4):
                        self.cur[z] = (wide(self.mid[z, p.core]) + wide(self.first[z, p.core])).astype(BF16)
                        self.out1[z] = (wide(self.mid[z, 1 - p.core]) + wide(self.first[z, 1 - p.core])).astype(BF16)
                    self.to_sibling.start()
        elif n == 3:
            if self.kind == 0:
                for z in range(4):
                    self.mid[z] = (wide(self.cur[z, p.x]) + wide(self.across[z])).astype(BF16)
            for c in self.along:
                c.start()
        else:
            self.out[...] = wide(self.held[p.z]) + wide(self.last[0]) + wide(self.last[1]) + wide(self.last[2])

    def wait(self, n):
        crooked = jnp.logical_not(self.straight)
        if n == 3:
            for c in self.along:
                c.wait()
        elif (self.kind, n) in ((0, 0), (1, 1)):
            self.one_way(self.over_y, crooked, True)
        elif (self.kind, n) in ((0, 1), (1, 2)):
            self.one_way(self.to_sibling, self.straight, True)
        else:
            self.over_x.wait()


def fold_scratch(kind, n):
    wide = (4, 2, 48, n)
    if kind == 0:
        shapes = ((4, 2, 2, 48, n), (4, 48, n), wide, wide, (4, 48, n), (3, 48, n))
    else:
        shapes = (wide, wide, (4, 48, n), (4, 48, n), wide, (3, 48, n))
    return [(s, BF16) for s in shapes]


def columns(rows_ref):
    return rows_ref[...].astype(F32).T


VECS = dict(embed=(0, 6), out_bias=(6, 6), gain1=(12, 6), shift1=(18, 6), down_bias=(24, 6), gain2=(30, 6), shift2=(36, 6),
            query_bias=(42, 3), value_bias=(45, 3), up_bias=(48, 12), conv_bias=(60, 3))


def lay_out(rows_ref, block_ref, *names):
    for k, name in enumerate(names):
        start, count = VECS[name]
        for j in range(count):
            rows_ref[k:k + 1, j * 128:(j + 1) * 128] = block_ref[start + j:start + j + 1, :]
    return [rows_ref.at[k:k + 1, 0:VECS[name][1] * 128] for k, name in enumerate(names)]


class Flow:
    def __init__(self, sems, *pairs):
        self.copies = [pltpu.make_async_copy(a, b, sems.at[k]) for k, (a, b) in enumerate(pairs)]

    def start(self, *which):
        for k in which or range(len(self.copies)):
            self.copies[k].start()

    def wait(self, *which):
        for k in which or range(len(self.copies)):
            self.copies[k].wait()


def transposed(x):
    a = x.shape[0]
    x = x.astype(F32)
    pad = -a % 128
    if pad:
        x = jnp.concatenate([x, jnp.zeros((pad, x.shape[1]), F32)], axis=0)
    return x.T[:, :a]


def conv_gather_kernel(*refs):
    vectors, refs = refs[:len(VECS)], refs[len(VECS):]
    (seg_row, mask_row, hid_ref, cot_ref, conv_ref, q_ref, k_ref, v_ref, o_ref, up_ref, dn_ref,
     xq, slope_ref, conv_t, hid_s, cot_s, small_s, vecs_t, own_late, w_out, wqk, wvo,
     spread, patches, ot, low, w_ref, shard, staged, own_t, seg, x_ref, small_ref, rows_ref, vecs_ref,
     local, turn, send_c, recv_c, send_w, recv_w) = refs
    p = Place()
    straight = p.core == p.y
    crooked = jnp.logical_not(straight)
    half, n = x_ref.shape[1], staged.shape[2]
    shard[...] = conv_ref[...].T
    meet_all(p)
    conv = LineGather(p, shard, w_ref, send_c, recv_c, 0, "core")
    conv.round(0)
    vecs_ref[...] = jnp.zeros_like(vecs_ref)
    for ref, (start, count) in zip(vectors, VECS.values()):
        line = ref[...].astype(F32).reshape(1, count * 128)
        for j in range(count):
            vecs_ref[start + j:start + j + 1, :] = line[:, j * 128:(j + 1) * 128]
    small_ref[...] = jnp.zeros_like(small_ref)
    small_ref[0:1, :] = seg_row[...]
    small_ref[1:2, :] = mask_row[...]
    w_ref[p.z, p.x, p.core] = shard[...]
    save_w = pltpu.make_async_copy(w_ref, w_out, local.at[0])
    walls = (wqk, wvo)
    lines = [LineGather(p, own_t.at[k], walls[k], send_w, recv_w, k, "y", k == 0) for k in range(2)]
    keep = [pltpu.make_async_copy(own_t.at[k], walls[k].at[p.z, p.x, p.y], local.at[1 + k]) for k in range(2)]
    twin = p.at(core=p.y, y=p.core)
    turned = [push(staged.at[0:2], own_t, turn, (0,), twin), push(staged.at[2:6], own_late, turn, (1,), twin), push(vecs_ref, vecs_t, turn, (2,), twin)]
    pairs = ((hid_ref, hid_s), (cot_ref, cot_s), (small_ref, small_s))
    keep_rows = [pltpu.make_async_copy(a, b, local.at[3 + k]) for k, (a, b) in enumerate(pairs)]
    push_rows = [push(a, b, turn, (3 + k,), p.at(core=1 - p.core)) for k, (a, b) in enumerate(pairs)]

    staged[0, :, :half] = q_ref[...]
    staged[0, :, half:] = k_ref[...]
    staged[1, :, :half] = v_ref[...]
    staged[1, :, half:] = o_ref[...]
    staged[2] = up_ref[:, :n]
    staged[3] = up_ref[:, n:]
    staged[4] = dn_ref[:, :n]
    staged[5] = dn_ref[:, n:]

    @pl.when(straight)
    def _():
        own_t[...] = staged[0:2]
        own_late[...] = staged[2:6]
        vecs_t[...] = vecs_ref[...]
        for c in keep_rows + push_rows:
            c.start()

    @pl.when(crooked)
    def _():
        for c in turned:
            c.start()

    cols = columns(small_ref)
    seg[...] = cols[:, 0:1].astype(jnp.int32)
    mine = pl.ds(pl.multiple_of(p.y * half, 128), half)
    hid = hid_ref[:, mine].astype(F32)
    embed, conv_bias = lay_out(rows_ref, vecs_ref, "embed", "conv_bias")
    x_ref[...] = (hid + cols[:, 1:2] * (rows_ref[0:1, mine] - hid)).astype(BF16)
    conv_prepare(seg, x_ref, spread, xq, patches)

    @pl.when(crooked)
    def _():
        for c in turned:
            c.wait()

    for c in keep:
        c.start()

    def nearest(n):
        pick = lambda *v: jnp.where(p.z == 0, v[0], jnp.where(p.z == 1, v[1], jnp.where(p.z == 2, v[2], v[3])))
        return (p.z, pick(1, 0, 1, 2), pick(2, 2, 3, 1), pick(3, 3, 0, 0))[n]

    def compute(n):
        z = nearest(n)
        for across in (False, True):
            conv.copy(0, conv.slot(z, across, True)).wait_recv()
        conv_plane(w_ref.at[z], patches, ot, z, n == 0)

    conv.round(1)
    compute(0)
    conv.round(2)
    compute(1)
    conv.round(3)
    for g in lines:
        g.round(0)
    compute(2)
    conv.round(4)
    for g in lines:
        g.round(1)
    compute(3)
    conv.sent()
    save_w.start()
    for g in lines:
        g.round(2)
    tile = 128
    turn_conv = [push(low.at[:, j * tile:(j + 1) * tile], conv_t.at[:, j * tile:(j + 1) * tile], turn, (6 + j,), twin) for j in range(half // tile)]
    for j in range(half // tile):
        conv_finish(seg, conv_bias, spread, ot, low, slope_ref, slice(j * tile, (j + 1) * tile))
        pl.when(crooked)(turn_conv[j].start)
        if j == 0:
            for g in lines:
                g.round(3)

    for g in lines:
        g.round(4)

    @pl.when(straight)
    def _():
        conv_t[...] = low[...]
        for c in keep_rows:
            c.wait()
        for c in push_rows:
            c.wait_send()

    @pl.when(crooked)
    def _():
        for c in push_rows:
            c.wait_recv()

    for g in lines:
        g.drain()
    for c in keep:
        c.wait()
    save_w.wait()

    @pl.when(crooked)
    def _():
        for c in turn_conv:
            c.wait()


def attn_gather_kernel(*refs):
    (hid_ref, conv_t, small_ref, vecs_ref, wqk_ref, wvo_ref, own_t,
     mixed_out, mlow_out, qkv_out, ctx_ref, lse_ref, part_ref, stat_ref, other_ref, wul, wur,
     qt, vt, ot, both, segc, mask, rows_ref, mixed_ref, mlow_ref, qkv_ref, local, flow, turn, send_w, recv_w, send_p, recv_p) = refs
    p = Place()
    half = conv_t.shape[1]
    sibling = p.at(core=1 - p.core)
    meet(partners(p))
    walls = (wul, wur)
    lines = [LineGather(p, own_t.at[k], walls[k], send_w, recv_w, k, "y", k == 0) for k in range(2)]
    keep = [pltpu.make_async_copy(own_t.at[k], walls[k].at[p.z, p.x, p.y], local.at[k]) for k in range(2)]
    give = push(conv_t, both.at[p.core], turn, (0,), sibling)
    give.start()
    for c in keep:
        c.start()
    for g in lines:
        g.round(0)
    embed, query_bias, value_bias = lay_out(rows_ref, vecs_ref, "embed", "query_bias", "value_bias")
    save = Flow(flow, (mixed_ref, mixed_out), (mlow_ref, mlow_out), (qkv_ref, qkv_out))
    both[p.core] = conv_t[...]
    cols = columns(small_ref)
    segc[...] = cols[:, 0:1].astype(jnp.int32)
    mask[...] = cols[:, 1:2].astype(jnp.int32)
    give.wait()

    def rounds(d):
        for g in lines:
            g.round(d)

    def beside(n):
        if isinstance(n, int):
            if n in (-3, -1):
                rounds((n + 5) // 2)
            if n == -1:
                save.start()
        else:
            for at in (0, 1):
                pl.when(n == at)(functools.partial(rounds, 3 + at))

    def sent(i, at):
        c = push(part_ref.at[at], other_ref.at[at], (send_p, recv_p), (i,), sibling)
        c.start()
        return c

    copies = attn_fwd_kernel(hid_ref, both.at[0], both.at[1], mask, segc, small_ref.at[0:1], embed, (wqk_ref, wvo_ref), query_bias, value_bias,
                             mixed_ref, mlow_ref, qkv_ref, ctx_ref, lse_ref, part_ref, stat_ref, qt, vt, ot, beside, sent)
    for g in lines:
        g.drain()
    for c in keep + copies:
        c.wait()
    save.wait()


def attn_fwd_kernel(hid_ref, c0_ref, c1_ref, mask_ref, segc_ref, segr_ref, emb_ref, w_refs, qb_ref, vb_ref,
                    mixed_ref, mlow_ref, qkv_ref, ctx_ref, lse_ref, part_ref, stat_ref, qt, vt, ot, beside=nothing, sent=nothing):
    wqk_ref, wvo_ref = w_refs
    rows, width = hid_ref.shape
    half = c0_ref.shape[1]
    heads = half // HD
    step = 256
    stat = jnp.zeros((1, half), F32)
    for i in range(rows // step):
        at = pl.ds(i * step, step)
        conv = jnp.concatenate([c0_ref[at, :].astype(F32), c1_ref[at, :].astype(F32)], axis=1)
        hid = hid_ref[at, :].astype(F32)
        masked = mask_ref[at, :].astype(F32)
        mixed = hid + masked * (emb_ref[...] - hid) + conv
        low = mixed.astype(BF16)
        mixed_ref[at, :] = mixed
        mlow_ref[at, :] = low
        stat = stat + jnp.sum(conv[:, :half] * conv[:, :half] + conv[:, half:] * conv[:, half:], axis=0, keepdims=True)
        qk = dg(low, wqk_ref[...], NN)
        qkv_ref[at, 0:half] = (qk[:, :half] + qb_ref[...]).astype(BF16)
        qkv_ref[at, half:2 * half] = qk[:, half:].astype(BF16)
        qkv_ref[at, 2 * half:] = (dg(low, wvo_ref[:, :half], NN) + vb_ref[...]).astype(BF16)
        beside(i - 4)
    stat_ref[...] = stat
    qt[...] = (qkv_ref[:, 0:half] * jnp.asarray(HD ** -0.5, BF16)).T
    vt[...] = qkv_ref[:, 2 * half:].T

    def pair_body(p, carry):
        beside(p)
        lanes = pl.ds(pl.multiple_of(half + p * 128, 128), 128)
        k_pair = qkv_ref[:, lanes]
        for j in range(2):
            head_at = pl.ds(pl.multiple_of(p * 128 + j * HD, HD), HD)
            qh = qt[head_at, :]
            vh = vt[head_at, :]
            zero = jnp.zeros_like(qh)
            qz = jnp.concatenate([qh, zero] if j == 0 else [zero, qh], axis=0)
            for i in range(rows // step):
                at = slice(i * step, (i + 1) * step)
                s = dg(k_pair, qz[:, at], NN)
                s = jnp.where(segc_ref[...] == segr_ref[:, at], s, -1000000000.0)
                top = jnp.max(s, axis=0, keepdims=True)
                e = jnp.exp(s - top)
                den = jnp.sum(e, axis=0, keepdims=True)
                o = dg(vh, e.astype(BF16), NN) / den
                ot[head_at, at] = jnp.where(segr_ref[:, at] != 0, o, 0.0).astype(BF16)
                lse_ref[pl.ds(2 * p + j, 1), at] = top + jnp.log(den)
        return carry

    lax.fori_loop(0, heads // 2, pair_body, 0)
    ctx_ref[...] = ot[...].T
    copies = []
    for i in range(rows // step):
        at = pl.ds(i * step, step)
        part_ref[at, :] = dg(ctx_ref[at, :], wvo_ref[:, half:], NT).astype(BF16)
        copies.append(sent(i, at))
    return copies


def norm_stats(x):
    centre = x - jnp.mean(x, axis=-1, keepdims=True)
    r = lax.rsqrt(jnp.mean(centre * centre, axis=-1, keepdims=True) + EPS)
    return centre * r, r


def matrix(ref):
    w = ref[...]
    return w if len(w.shape) == 2 else w.reshape(-1, w.shape[-1])


def ffn_fwd_kernel(mixed_ref, p0_ref, p1_ref, seg_ref, ob_ref, g1_ref, s1_ref, ul_ref, ur_ref, ub_ref, dl_ref, dr_ref,
                   n1_ref, r1_ref, low_ref, hid_ref, slope_ref, part_ref, stat_ref, beside=nothing, before_down=nothing, sent=nothing):
    rows, width = mixed_ref.shape
    ff = ul_ref.shape[-1]
    step = 256
    stat_ref[...] = jnp.zeros_like(stat_ref)

    def up_body(i, carry):
        at = pl.ds(pl.multiple_of(i * step, step), step)
        attn = ob_ref[...] + (p0_ref[at, :].astype(F32) + p1_ref[at, :].astype(F32))
        valid = (seg_ref[at, :] != 0).astype(F32)
        stat_ref[...] += jnp.sum(valid * attn * attn, axis=0, keepdims=True)
        n1, r1 = norm_stats(mixed_ref[at, :] + attn)
        n1_ref[at, :] = n1
        r1_ref[at, :] = r1
        low = (n1 * g1_ref[...] + s1_ref[...]).astype(BF16)
        low_ref[at, :] = low
        for k, up in enumerate((ul_ref, ur_ref)):
            cols = slice(k * ff, (k + 1) * ff)
            value, slope = gelu_and_slope(dg(low, matrix(up), NN) + ub_ref[:, cols])
            hid_ref[at, cols] = value.astype(BF16)
            slope_ref[at, cols] = slope.astype(BF16)
        beside(i)
        return carry

    def down_body(i, carry):
        at = pl.ds(pl.multiple_of(i * step, step), step)
        part_ref[at, :] = (dg(hid_ref[at, :ff], matrix(dl_ref), NT) + dg(hid_ref[at, ff:], matrix(dr_ref), NT)).astype(BF16)
        sent(i, at)
        return carry

    lax.fori_loop(0, rows // step, up_body, 0)
    before_down()
    lax.fori_loop(0, rows // step, down_body, 0)


class Give:
    def __init__(self, place, part, other, sems):
        self.make = lambda i, at: push(part.at[at], other.at[at], sems, (i,), place.at(core=1 - place.core))

    def __call__(self, i, at):
        self.make(i, at).start()

    def arrived(self, i, at):
        self.make(i, at).wait()

    def wait(self, parts, step):
        for i in range(parts):
            self.make(i, pl.ds(i * step, step)).wait()


def norm_back(gn, n, r):
    return r * (gn - jnp.mean(gn, axis=-1, keepdims=True) - n * jnp.mean(gn * n, axis=-1, keepdims=True))


def ffn_bwd_kernel(n1_ref, g1_ref, s1_ref, p0_ref, p1_ref, seg_ref, db_ref, g2_ref, s2_ref, cot_ref, low_ref,
                   hid_ref, slope_ref, ul_ref, ur_ref, dl_ref, dr_ref,
                   out_ref, gr2_ref, part_ref, ddl_ref, ddr_ref, dul_ref, dur_ref, sums_ref, dub_ref, fg, hg,
                   here=nothing, down_done=nothing, sent=nothing):
    rows, width = n1_ref.shape
    ff = ul_ref.shape[-1]
    step = 256
    sums_ref[...] = jnp.zeros_like(sums_ref)
    dub_ref[...] = jnp.zeros_like(dub_ref)
    row_sum = lambda v: jnp.sum(v, axis=0, keepdims=True)
    store = lambda ref, v: ref.__setitem__(Ellipsis, v.astype(ref.dtype).reshape(ref.shape))

    def norm_body(i, carry):
        at = pl.ds(pl.multiple_of(i * step, step), step)
        here(i, at)
        ffn = db_ref[...] + (p0_ref[at, :].astype(F32) + p1_ref[at, :].astype(F32))
        valid = (seg_ref[at, :] != 0).astype(F32)
        n2, r2 = norm_stats(n1_ref[at, :] * g1_ref[...] + s1_ref[...] + ffn)
        final = valid * (n2 * g2_ref[...] + s2_ref[...])
        out_ref[at, :] = final.astype(BF16)
        gf = valid * cot_ref[at, :].astype(F32)
        gr2 = norm_back(gf * g2_ref[...], n2, r2)
        gr2_ref[at, :] = gr2
        ffn_grad = gr2.astype(BF16)
        fg[at, :] = ffn_grad
        sums_ref[...] += jnp.concatenate(
            [row_sum(valid * ffn * ffn), row_sum(final * final), row_sum(gf * n2), row_sum(gf), row_sum(ffn_grad.astype(F32))], axis=0)
        return carry

    lax.fori_loop(0, rows // step, norm_body, 0)
    store(ddl_ref, dg(fg[...], hid_ref[:, :ff], TN))
    store(ddr_ref, dg(fg[...], hid_ref[:, ff:], TN))
    down_done()

    def body(i, carry):
        at = pl.ds(pl.multiple_of(i * step, step), step)
        part = 0.0
        for k, (up, down) in enumerate(((ul_ref, dl_ref), (ur_ref, dr_ref))):
            cols = slice(k * ff, (k + 1) * ff)
            hidden_grad = (slope_ref[at, cols].astype(F32) * dg(fg[at, :], matrix(down), NN)).astype(BF16)
            hg[at, cols] = hidden_grad
            dub_ref[:, cols] += row_sum(hidden_grad.astype(F32))
            part = part + dg(hidden_grad, matrix(up), NT)
        part_ref[at, :] = part.astype(BF16)
        sent(i, at)
        return carry

    lax.fori_loop(0, rows // step, body, 0)
    store(dul_ref, dg(low_ref[...], hg[:, :ff], TN))
    store(dur_ref, dg(low_ref[...], hg[:, ff:], TN))


def ffn_kernel(*refs):
    mixed, part1, other1, small, vecs, cot_in, wul_in, wur_in, own_t = refs[:9]
    (n1_out, r1, stat, show_out, gr2_out, part3, ddl_out, ddr_out, dul, dur, sums, dub, other3, first_l, across_r) = refs[9:24]
    (low, hid, slope, part2, other2, fg, hg, seg, wdl, wdr, rows_ref, n1, out_ref, gr2, ddl, ddr, cot, wul, wur) = refs[24:43]
    sem_2, sem_3, sem_f, send_w, recv_w, flow_in, flow_out = refs[43:]
    p = Place()
    straight = p.core == p.y
    crooked = jnp.logical_not(straight)
    load = Flow(flow_in, (wul_in, wul), (wur_in, wur), (cot_in, cot))
    load.start()
    save = Flow(flow_out, (n1, n1_out), (out_ref, show_out), (gr2, gr2_out), (ddl, ddl_out), (ddr, ddr_out))
    meet(partners(p))
    lines = [LineGather(p, own_t.at[2 + k], w, send_w, recv_w, k, "y", k == 0) for k, w in enumerate((wdl, wdr))]
    for k, g in enumerate(lines):
        g.round(0)
        g.buf[p.z, p.x, p.y] = own_t[2 + k]
    seg[...] = columns(small)[:, 0:1].astype(jnp.int32)
    ob, g1, s1, db, g2, s2, ub = lay_out(rows_ref, vecs, "out_bias", "gain1", "shift1", "down_bias", "gain2", "shift2", "up_bias")
    give2, give3 = Give(p, part2, other2, sem_2), Give(p, part3, other3, sem_3)
    over_y = push(ddl, first_l, sem_f, (0,), p.at(y=p.core))
    over_x = push(ddr.at[:, 1 - p.x], across_r, sem_f, (1,), p.at(x=1 - p.x))
    load.wait(0, 1)

    def beside(i):
        for n in range(4):
            @pl.when(i == n)
            def _(n=n):
                for g in lines:
                    g.round(n + 1)

    def before_down():
        save.start(0)
        load.wait(2)
        for g in lines:
            g.drain()

    def down_done():
        pl.when(crooked)(over_y.start)
        over_x.start()
        save.start(1, 2, 3, 4)

    ffn_fwd_kernel(mixed, part1, other1, seg, ob, g1, s1, wul, wur, ub, wdl, wdr,
                   n1, r1, low, hid, slope, part2, stat, beside, before_down, give2)
    ffn_bwd_kernel(n1, g1, s1, part2, other2, seg, db, g2, s2, cot, low, hid, slope, wul, wur, wdl, wdr,
                   out_ref, gr2, part3, ddl, ddr, dul, dur, sums, dub, fg, hg, give2.arrived, down_done, give3)
    give3.wait(4, 256)
    over_x.wait()
    pl.when(straight)(over_y.wait_recv)
    pl.when(crooked)(over_y.wait_send)
    save.wait()


def attn_bwd_kernel(gr2_ref, p0_ref, p1_ref, n1_ref, r1_ref, g1_ref, segc_ref, segr_ref, ctx_ref, qkv_ref, lse_ref,
                    mlow_ref, wqk_ref, wvo_ref,
                    dqk_ref, dvo_ref, sums_ref, dqkvb_ref, gr1, cg, qt, kt, ct, dqt, dk, dv, gqkv, finish, beside=nothing, normed=nothing):
    rows, width = gr2_ref.shape
    half = ctx_ref.shape[1]
    heads = half // HD
    step = 256
    core = lax.rem(lax.axis_index("dp"), 2)
    sums_ref[...] = jnp.zeros_like(sums_ref)
    row_sum = lambda v: jnp.sum(v, axis=0, keepdims=True)

    def norm_body(i, carry):
        at = pl.ds(pl.multiple_of(i * step, step), step)
        gn1 = gr2_ref[at, :] + (p0_ref[at, :].astype(F32) + p1_ref[at, :].astype(F32))
        n1 = n1_ref[at, :]
        g = norm_back(gn1 * g1_ref[...], n1, r1_ref[at, :])
        gr1[at, :] = g
        attn_grad = g.astype(BF16)
        sums_ref[...] += jnp.concatenate([row_sum(gn1 * n1), row_sum(gn1), row_sum(attn_grad.astype(F32))], axis=0)
        back = dg(attn_grad, wvo_ref[:, half:], NN)
        cg[at, :] = jnp.where(segc_ref[at, :] != 0, back, 0.0).astype(BF16)
        return carry

    lax.fori_loop(0, rows // step, norm_body, 0)
    normed()
    store = lambda ref, cols, v: ref.__setitem__((Ellipsis, cols), v.astype(BF16).reshape(ref.shape[:-1] + (v.shape[-1],)))
    store(dvo_ref, slice(half, 2 * half), dg(gr1[...].astype(BF16), ctx_ref[...], TN))
    scale = jnp.asarray(HD ** -0.5, BF16)
    qt[...] = (qkv_ref[:, 0:half] * scale).T
    kt[...] = qkv_ref[:, half:2 * half].T
    ct[...] = cg[...].T
    lane = lax.broadcasted_iota(jnp.int32, (1, 128), 1)

    def pair_body(p, carry):
        base = pl.multiple_of(p * 128, 128)
        k_at = pl.ds(pl.multiple_of(half + base, 128), 128)
        v_at = pl.ds(pl.multiple_of(2 * half + base, 128), 128)
        q_pair = qkv_ref[:, pl.ds(base, 128)] * scale
        o_pair = cg[:, pl.ds(base, 128)]
        dk[...] = jnp.zeros_like(dk)
        dv[...] = jnp.zeros_like(dv)
        for j in range(2):
            head_at = pl.ds(pl.multiple_of(base + j * HD, HD), HD)
            zero = jnp.zeros((HD, rows), BF16)
            put = lambda a: jnp.concatenate([a, zero] if j == 0 else [zero, a], axis=0)
            qz, cz, kh = put(qt[head_at, :]), put(ct[head_at, :]), kt[head_at, :]
            keep = (lane < HD) if j == 0 else (lane >= HD)
            for i in range(rows // step):
                at = slice(i * step, (i + 1) * step)
                s = dg(qkv_ref[:, k_at], qz[:, at], NN)
                pr = jnp.exp(s - lse_ref[pl.ds(2 * p + j, 1), at])
                pr = jnp.where(segc_ref[...] == segr_ref[:, at], pr, 0.0)
                gp = dg(qkv_ref[:, v_at], cz[:, at], NN)
                delta = jnp.sum(pr * gp, axis=0, keepdims=True)
                ds = (pr * (gp - delta)).astype(BF16)
                dv[...] += dg(pr.astype(BF16), jnp.where(keep, o_pair[at, :], jnp.zeros_like(o_pair[at, :])), NN)
                dk[...] += dg(ds, jnp.where(keep, q_pair[at, :], jnp.zeros_like(q_pair[at, :])), NN)
                dqt[head_at, at] = (dg(kh, ds, NN) * (HD ** -0.5)).astype(BF16)
                beside(p, j * (rows // step) + i)
        gqkv[:, k_at] = dk[...].astype(BF16)
        gqkv[:, v_at] = dv[...].astype(BF16)
        return carry

    lax.fori_loop(0, heads // 2, pair_body, 0)
    gqkv[:, 0:half] = dqt[...].T
    mine = pl.ds(pl.multiple_of(core * half, 128), half)
    other = pl.ds(pl.multiple_of((1 - core) * half, 128), half)
    to_mixed = lambda at: (dg(gqkv[:, :2 * half], wqk_ref[at, :], NT) + dg(gqkv[:, 2 * half:], wvo_ref[at, 0:half], NT))
    finish(lambda: to_mixed(other).astype(BF16), lambda: gr1[:, mine] + to_mixed(mine))
    dqkvb_ref[...] = row_sum(gqkv[...].astype(F32))
    dqk_ref[...] = dg(mlow_ref[...], gqkv[:, :2 * half], TN).astype(BF16).reshape(dqk_ref.shape)
    store(dvo_ref, slice(0, half), dg(mlow_ref[...], gqkv[:, 2 * half:], TN))


def attn_bwd_plain_kernel(*refs):
    ins, outs, scratch = refs[:14], refs[14:20], refs[20:]
    own_ref, send_ref = outs[:2]

    def finish(send, own):
        send_ref[...] = send()
        own_ref[...] = own()

    attn_bwd_kernel(*ins, *outs[2:], *scratch, finish)


def attn_bwd_fold_kernel(*refs):
    gr2, part3, other3, n1, r1, vecs, small, ctx_in, qkv_in, lse, mlow_in, wqk_in, wvo, ddl, ddr, dul_in, dur_in, first_l, across_r = refs[:19]
    outs, (gm_out, out_up, out_dn) = refs[19:23], refs[23:26]
    scratch, (segc, send, got, gm, out_dl, out_dr, rows_ref, ctx, qkv, mlow, wqk, dul, dur) = refs[26:35], refs[35:48]
    bufs, (sem_f, sem_g, flow) = refs[48:70], refs[70:]
    n = out_dl.shape[1]
    out_ul, out_ur = out_up.at[:, :n], out_up.at[:, n:]
    p = Place()
    load = Flow(flow, (dur_in, dur), (dul_in, dul), (ctx_in, ctx), (qkv_in, qkv), (mlow_in, mlow), (wqk_in, wqk))
    load.start()
    (g1,) = lay_out(rows_ref, vecs, "gain1")
    straight = p.core == p.y
    meet_all(p)
    segc[...] = columns(small)[:, 0:1].astype(jnp.int32)
    early = [Fold(0, p, ddl, sem_f, 0, first_l, *bufs[0:5], out_dl), Fold(1, p, ddr, sem_f, 1, bufs[5], across_r, *bufs[6:10], out_dr)]
    late = [Fold(0, p, dul, sem_f, 2, *bufs[10:16], out_ul), Fold(1, p, dur, sem_f, 3, *bufs[16:22], out_ur)]

    def step(folds, n, wait=True):
        for f in folds:
            if wait:
                f.wait(n - 1)
            f.start(n)

    step(early, 1, False)
    load.wait(0)
    late[1].start(0)

    def normed():
        load.wait(1, 2, 3, 4, 5)
        step(early, 2)
        late[0].start(0)

    def beside(pair, at):
        if at == 2:
            pl.when(pair == 1)(lambda: step(early, 3))
        if at == 6:
            pl.when(pair == 1)(lambda: step(late, 1))
        if at == 4:
            pl.when(pair == 2)(lambda: step(late, 2))
        if at == 7:
            @pl.when(pair == 2)
            def _():
                step(early, 4)
                out_dn[:, :n] = out_dl[...]
                out_dn[:, n:] = out_dr[...]

    to_sibling = push(send, got, sem_g, (0,), p.at(core=1 - p.core))
    turn = push(gm, gm_out, sem_g, (1,), p.at(core=p.y, y=p.core))

    def finish(give, own):
        send[...] = give()
        to_sibling.start()
        step(late, 3)
        mine = own()
        to_sibling.wait()
        value = (mine + got[...].astype(F32)).astype(BF16)

        @pl.when(straight)
        def _():
            gm_out[...] = value

        @pl.when(jnp.logical_not(straight))
        def _():
            gm[...] = value
            turn.start()

    attn_bwd_kernel(gr2, part3, other3, n1, r1, g1, segc, small.at[0:1], ctx, qkv, lse, mlow, wqk, wvo, *outs, *scratch, finish, beside, normed)
    step(late, 4)
    pl.when(jnp.logical_not(straight))(turn.wait)


class Total:
    def __init__(self, vec, got, sems, hops, p):
        self.vec, self.got, self.n = vec, got, len(hops)
        self.pair = [push(vec.at[n], got.at[n], sems, (n,), device) for n, device in enumerate(hops)]
        self.along = [push(vec.at[self.n], got.at[self.n + o - 1], sems, (self.n + o - 1,), p.at(z=lax.rem(p.z + o, 4))) for o in (1, 2, 3)]

    def step(self, n):
        if n > 0:
            self.pair[n - 1].wait()
            self.vec[n] = self.vec[n - 1] + self.got[n - 1]
        for c in self.along if n == self.n else [self.pair[n]]:
            c.start()

    def result(self):
        for c in self.along:
            c.wait()
        n = self.n
        return self.vec[n] + self.got[n] + self.got[n + 1] + self.got[n + 2]


def conv_fold_kernel(*refs):
    (seg_row, mask_row, xq, w_in, slope_ref, gm_ref, dqk, dvo, sums2, sums1, dqkvb, dub, stat_conv, stat_attn, shown,
     in_ref, dconv_ref, out_qk, out_vo, sums_out, me_out, layer_got, spread, dq, d_ref, gq) = refs[:26]
    seg_ref, mask_ref, small_ref, db_ref, dm_ref, d_all, got_c, sum_c, got_x, sum_x, got_z, vec, got_v, me, got_me, w_ref = refs[26:42]
    folds_bufs, (sem_c, sem_x, sem_z, sem_fold, sem_vec, sem_me, sem_out, flow) = refs[42:54], refs[54:]
    p = Place()
    straight = p.core == p.y
    crooked = jnp.logical_not(straight)
    load = Flow(flow, (w_in, w_ref))
    load.start()
    meet(partners(p))
    groups = 8
    wide = lambda v: v.astype(F32)
    folds = [Fold(FOLD_KINDS[0], p, dqk, sem_fold, 0, *folds_bufs[:6], out_qk), Fold(FOLD_KINDS[1], p, dvo, sem_fold, 1, *folds_bufs[6:], out_vo)]
    for f in folds:
        f.start(0)
    show = push(shown, layer_got, sem_out, (0,), p.at(y=1 - p.y))
    small_ref[...] = jnp.zeros_like(small_ref)
    small_ref[0:1, :] = seg_row[...]
    small_ref[1:2, :] = mask_row[...]
    cols = columns(small_ref)
    seg_ref[...] = cols[:, 0:1].astype(jnp.int32)
    mask_ref[...] = cols[:, 1:2].astype(jnp.int32)
    hops = [p.at(core=1 - p.core), p.at(x=1 - p.x)]
    total = Total(vec, got_v, sem_vec, hops + [p.at(y=1 - p.y)], p)
    me_total = Total(me, got_me, sem_me, hops, p)
    width = vec.shape[2]
    half = width // 2
    of_half = lambda which: (lax.broadcasted_iota(jnp.int32, (1, width), 1) // half == which).astype(F32)
    twice = lambda v: jnp.concatenate([v, v], axis=1)

    def ready():
        by_core, by_y = of_half(p.core), of_half(p.y)
        is_core = lambda c: (p.core == c).astype(F32)
        frames = jnp.sum(wide(seg_ref[...] != 0), axis=0, keepdims=True)
        rows = [sums1[2:3] * by_core, sums1[0:1] * by_core, sums1[1:2] * by_core, sums2[4:5] * by_core, sums2[2:3] * by_core, sums2[3:4] * by_core,
                twice(db_ref[...]) * by_y, twice(dqkvb[:, :half]) * by_core, twice(dqkvb[:, 2 * half:]) * by_core,
                dub[:, :width] * is_core(0), dub[:, width:] * is_core(0), dub[:, :width] * is_core(1), dub[:, width:] * is_core(1),
                twice(stat_conv[...]) * by_core * 0.5, stat_attn[...] * by_core, sums2[0:1] * by_core, sums2[1:2] * by_core,
                jnp.broadcast_to(frames * 0.5, (1, width))]
        rows.append(jnp.zeros((24 - len(rows), width), F32))
        vec[0] = jnp.concatenate(rows, axis=0)
        total.step(0)

    def store(g, dw):
        d_all[g] = dw.reshape(d_all.shape[1:])

    to_c = lambda g: push(d_all.at[g, :, :, 1 - p.core], got_c.at[g], sem_c, (g,), p.at(core=1 - p.core))
    to_x = lambda g: push(sum_c.at[g, :, 1 - p.x], got_x.at[g], sem_x, (g,), p.at(x=1 - p.x))
    to_z = lambda g: [push(sum_x.at[g, lax.rem(p.z + o, 4)], got_z.at[g, o - 1], sem_z, (g, o - 1), p.at(z=lax.rem(p.z + o, 4)))
                      for o in (1, 2, 3)]

    def fold_step(n):
        for f in folds:
            f.wait(n - 1)
        for f in folds:
            f.start(n)

    def crossed(k):
        to_x(k).wait()
        for z in range(4):
            sum_x[k, z] = (wide(sum_c[k, z, p.x]) + wide(got_x[k, z])).astype(BF16)
        for c in to_z(k):
            c.start()

    def beside(t):
        @pl.when(t < groups)
        def _():
            to_c(t).start()

        @pl.when(jnp.logical_and(t >= 1, t <= groups))
        def _():
            k = t - 1
            to_c(k).wait()
            for z in range(4):
                for x in range(2):
                    sum_c[k, z, x] = (wide(d_all[k, z, x, p.core]) + wide(got_c[k, z, x])).astype(BF16)
            to_x(k).start()

        for k, at in enumerate(CROSS_AT):
            pl.when(t == at)(functools.partial(crossed, k))
        for n, at in zip((1, 2, 3), FOLD_AT):
            pl.when(t == at)(functools.partial(fold_step, n))
        for n, at in zip((1, 2, 3), TOTAL_AT):
            pl.when(t == at)(functools.partial(total.step, n))
        pl.when(jnp.logical_and(t == SHOW_AT, straight))(show.start)
        pl.when(t == groups - 1)(load.wait)

    def summed():
        me[0] = jnp.broadcast_to(dm_ref[...], me.shape[1:])
        me_total.step(0)

    conv_bwd_kernel(seg_ref, xq, w_ref, slope_ref, gm_ref, mask_ref, None, in_ref, db_ref, dm_ref,
                    spread, dq, d_ref, gq, ready, beside, store, summed)
    me_total.step(1)
    sums_out[...] = total.result()
    me_total.step(2)
    for f in folds:
        f.wait(3)
        f.start(4)
    for k in range(groups):
        for c in to_z(k):
            c.wait()
        gq[k * CG:(k + 1) * CG, 0:TAPS * CG] = wide(sum_x[k, p.z]) + wide(got_z[k, 0]) + wide(got_z[k, 1]) + wide(got_z[k, 2])
    dconv_ref[...] = gq[:, 0:TAPS * CG].T
    me_out[...] = me_total.result()
    pl.when(straight)(show.wait_send)
    pl.when(crooked)(show.wait_recv)


def result_kernel(*refs):
    (shown, layer_got, grad, dconv, oqk, ovo, dup, ddn, sums, me,
     layer_out, input_grad, mask_out, conv_out, convb_out, q_out, k_out, v_out, qb_out, vb_out, o_out, ob_out, g1_out, s1_out,
     up_out, ub_out, dn_out, db_out, g2_out, s2_out, rms_out, flow) = refs
    y = lax.axis_index("mp")
    straight = lax.rem(lax.axis_index("dp"), 2) == y
    move = Flow(flow, (grad, input_grad), (dconv, conv_out), (dup, up_out), (ddn, dn_out), (shown, layer_out))
    got = pltpu.make_async_copy(layer_got, layer_out, flow.at[5])
    move.start(0, 1, 2, 3)
    pl.when(straight)(lambda: move.start(4))
    pl.when(jnp.logical_not(straight))(got.start)
    half = q_out.shape[1]
    width = sums.shape[1]
    q_out[...] = oqk[:, :half]
    k_out[...] = oqk[:, half:]
    v_out[...] = ovo[:, :half]
    o_out[...] = ovo[:, half:]
    line = lambda ref, v: ref.__setitem__(Ellipsis, v.reshape(ref.shape))
    part = lambda k: jnp.where(y == 0, sums[k:k + 1, :half], sums[k:k + 1, half:])
    for k, ref in enumerate((ob_out, g1_out, s1_out, db_out, g2_out, s2_out)):
        line(ref, sums[k:k + 1, :])
    line(mask_out, me[0:1, :])
    for k, ref in ((6, convb_out), (7, qb_out), (8, vb_out)):
        line(ref, part(k))
    pair = lambda k: jnp.concatenate([sums[k:k + 1, :], sums[k + 1:k + 2, :]], axis=1)
    line(ub_out, jnp.where(y == 0, pair(9), pair(11)))
    power = lambda k: jnp.sum(sums[k:k + 1, :], axis=1, keepdims=True)
    rms = jnp.sqrt(jnp.concatenate([power(k) for k in (13, 14, 15, 16)], axis=1) / (sums[17:18, 0:1] * width))
    line(rms_out, rms)
    move.wait(0, 1, 2, 3)
    pl.when(straight)(lambda: move.wait(4))
    pl.when(jnp.logical_not(straight))(got.wait)


def one_row(v):
    return v.astype(F32)[None]


def flat_turn(n_all):
    return [(f, f // 4 * 4 + (f % 2) * 2 + (f // 2) % 2) for f in range(n_all)]


def shapes(rows, width, ff):
    half = width // 2
    heads = half // HD
    spread_width = -(-(rows + 7 * 64 + 64) // 128) * 128
    blocks = KW // TAPS
    low, wide = lambda *s: (s, BF16), lambda *s: (s, F32)
    return dict(
        half=half, spread_width=spread_width, blocks=blocks,
        attn_out=[wide(rows, width), low(rows, width), low(rows, 3 * half), low(rows, half), wide(heads, rows), low(rows, width)],
        attn_scratch=[low(half, rows)] * 3,
        ffn_out=[wide(rows, width), wide(rows, 1), low(rows, width), low(rows, ff), low(rows, ff), low(rows, width), wide(1, width)],
        back_scratch=[wide(rows, width), low(rows, half), low(half, rows), low(half, rows), low(half, rows), low(half, rows),
                      wide(rows, 128), wide(rows, 128), low(rows, 3 * half)],
    )


def local_close(hidden_in, segment_ids, time_mask, mask_embed, conv_weight, conv_bias, query_weight, key_weight,
                value_weight, query_bias, value_bias, out_weight, out_bias, first_gain, first_shift, up_weight, up_bias,
                down_weight, down_bias, second_gain, second_shift, cotangent):
    _, rows, width = hidden_in.shape
    ff = up_weight.shape[1]
    n = ff // 2
    sh = shapes(rows, width, ff)
    half, sw, blocks = sh["half"], sh["spread_width"], sh["blocks"]
    low, wide = lambda *s: (s, BF16), lambda *s: (s, F32)
    block = wide(64, 128)
    column = ((rows, 1), jnp.int32)
    eight = ((8, rows), jnp.int32)
    seats = (4, 2, 2)
    wall = [low(*seats, 48, n)]
    line_sems = ((4, 2) + seats, (2,) + seats)

    xq, slope, conv_t, hid_s, cot_s, small_s, vecs_t, own_late, conv_full, w_qk, w_vo = call(
        conv_gather_kernel,
        [low(half, sw), wide(rows, half), low(rows, half), low(rows, width), low(rows, width), eight, block, low(4, 48, n),
         low(*seats, half, TAPS * CG)] + wall * 2,
        [low(rows, sw), low(half // CG, TAPS * CG, sw), wide(half, sw), low(rows, half), low(*seats, half, TAPS * CG), low(half, TAPS * CG),
         low(6, 48, n), low(2, 48, n), column, low(rows, half), eight, wide(8, width), block],
        mask_embed, out_bias, first_gain, first_shift, down_bias, second_gain, second_shift, query_bias, value_bias, up_bias, conv_bias,
        segment_ids, time_mask, hidden_in[0], cotangent[0], conv_weight, query_weight, key_weight, value_weight, out_weight.T, up_weight,
        down_weight.T, hbm_out=(3, 4, 5, 8, 9, 10), sems=((6,), (2, 9), (4, 1) + seats, (1,) + seats) + line_sems, meeting=1)
    flat = lambda w: w.reshape(width, n)
    w_qk, w_vo = flat(w_qk), flat(w_vo)
    held = [wide(rows, width), low(rows, width), low(rows, 3 * half)]
    mixed, mlow, qkv, ctx, lse, part1, stat_conv, other1, w_ul, w_ur = call(
        attn_gather_kernel, sh["attn_out"] + [wide(1, half), low(rows, width)] + wall * 2,
        sh["attn_scratch"] + [low(2, rows, half), column, column, wide(8, width)] + held,
        hid_s, conv_t, small_s, vecs_t, w_qk, w_vo, own_late,
        hbm_out=(0, 1, 2, 8, 9), sems=((2,), (3,), (2, 1)) + line_sems + ((4,), (4,)), meeting=2)
    w_ul, w_ur = flat(w_ul), flat(w_ur)
    grad = low(*seats, 48, n)
    weight = low(width, n)
    n1, r1, stat_attn, out_s, gr2, part3, ddl, ddr, dul, dur, sums2, d_ub, other3, first_l, across_r = call(
        ffn_kernel,
        [wide(rows, width), wide(rows, 1), wide(1, width), low(rows, width), wide(rows, width), low(rows, width)] + [grad] * 4
        + [wide(5, width), wide(1, ff), low(rows, width), grad, low(4, 2, 48, n)],
        [low(rows, width), low(rows, ff), low(rows, ff), low(rows, width), low(rows, width), low(rows, width), low(rows, ff), column, grad, grad,
         wide(8, ff), wide(rows, width), low(rows, width), wide(rows, width), grad, grad, low(rows, width), weight, weight],
        mixed, part1, other1, small_s, vecs_t, cot_s, w_ul, w_ur, own_late,
        hbm_in=(5, 6, 7), hbm_out=(0, 3, 4, 6, 7), sems=((2, 4), (2, 4), (2, 2)) + line_sems + ((3,), (5,)), meeting=3)
    kinds = [fold_scratch(0, n)[1:], fold_scratch(1, n)[:1] + fold_scratch(1, n)[2:], fold_scratch(0, n), fold_scratch(1, n)]
    own = [wide(48, n)] * 2
    dqk, dvo, sums1, d_qkvb, gm, d_up, d_down = call(
        attn_bwd_fold_kernel,
        [grad, grad, wide(3, width), wide(1, 3 * half), low(rows, half), wide(48, ff), wide(48, ff)],
        sh["back_scratch"] + [column, low(rows, half), low(rows, half), low(rows, half)] + own
        + [wide(8, width), low(rows, half), low(rows, 3 * half), low(rows, width), weight, grad, grad] + sum(kinds, []),
        gr2, part3, other3, n1, r1, vecs_t, small_s, ctx, qkv, lse, mlow, w_qk, w_vo, ddl, ddr, dul, dur, first_l, across_r,
        hbm_in=(7, 8, 10, 11, 15, 16), sems=((2, 4, 6), (2, 2), (6,)), meeting=5)
    in_grad, d_conv, d_qk, d_vo, sums, d_me, got_out = call(
        conv_fold_kernel,
        [wide(rows, half), wide(TAPS * CG, half), wide(48, n), wide(48, n), wide(24, width), wide(8, half), low(rows, width)],
        [low(rows, sw), low(half, sw), low(blocks * CG, sw), wide(half, sw), column, column, eight, wide(1, half), wide(1, half),
         low(8, *seats, CG, TAPS * CG), low(8, 4, 2, CG, TAPS * CG), low(8, 4, 2, CG, TAPS * CG), low(8, 4, CG, TAPS * CG),
         low(8, 4, CG, TAPS * CG), low(8, 3, CG, TAPS * CG), wide(4, 24, width), wide(6, 24, width), wide(3, 8, half), wide(5, 8, half),
         low(*seats, half, TAPS * CG)] + fold_scratch(FOLD_KINDS[0], n) + fold_scratch(FOLD_KINDS[1], n),
        segment_ids, time_mask, xq, conv_full, slope, gm, dqk, dvo, sums2, sums1, d_qkvb, d_ub, stat_conv, stat_attn, out_s,
        hbm_in=(3, 14), hbm_out=(6,), sems=((2, 8), (2, 8), (2, 8, 3), (2, 2, 6), (2, 6), (2, 5), (2, 1), (1,)), meeting=6)
    line, shard = lambda size: ((size,), F32), wide(48, half)
    results = list(call(
        result_kernel,
        [low(rows, width), wide(rows, half), line(half), wide(TAPS * CG, half), line(half), shard, shard, shard, line(half), line(half), shard,
         line(width), line(width), line(width), wide(48, ff), line(ff), wide(48, ff), line(width), line(width), line(width), line(4)],
        [], out_s, got_out, in_grad, d_conv, d_qk, d_vo, d_up, d_down, sums, d_me, hbm_in=(0, 1, 2, 3, 6, 7), sems=((6,),)))
    results[0], results[1], results[10], results[16] = results[0][None], results[1][None], results[10].T, results[16].T
    return tuple(results)


def local_any(n_dp, hidden_in, segment_ids, time_mask, mask_embed, conv_weight, conv_bias, query_weight, key_weight,
          value_weight, query_bias, value_bias, out_weight, out_bias, first_gain, first_shift, up_weight, up_bias,
          down_weight, down_bias, second_gain, second_shift, cotangent):
    _, rows, width = hidden_in.shape
    ff = up_weight.shape[1]
    n = ff // 2
    sh = shapes(rows, width, ff)
    half, spread_width, blocks = sh["half"], sh["spread_width"], sh["blocks"]
    part = lax.axis_index("mp")
    core = lax.rem(lax.axis_index("dp"), 2)
    n_all = 2 * n_dp
    turn = flat_turn(n_all)
    sibling = [(f, f ^ 2) for f in range(n_all)]
    core_groups = [[f for f in range(n_all) if (f // 2) % 2 == c] for c in range(2)]
    swap = lambda v: lax.ppermute(v, BOTH, sibling)
    turned = lambda v: lax.ppermute(v, BOTH, turn)
    mine = part == core

    down_t = down_weight.T
    w_shards = [jnp.concatenate([query_weight, key_weight], axis=1), jnp.concatenate([value_weight, out_weight.T], axis=1),
                up_weight[:, :n], up_weight[:, n:], down_t[:, :n], down_t[:, n:]]
    conv_full = lax.all_gather(conv_weight, "dp", axis=0, tiled=True)
    conv_full = conv_full.reshape(blocks, TAPS * CG, half).swapaxes(1, 2)
    w_qk, w_vo, w_ul, w_ur, w_dl, w_dr = (
        lax.all_gather(turned(w), BOTH, axis=0, tiled=True, axis_index_groups=core_groups) for w in w_shards)
    bias = turned(jnp.concatenate([query_bias, value_bias, up_bias])[None])
    qb, vb, ub = (b.astype(F32) for b in (bias[:, :half], bias[:, half:2 * half], bias[:, 2 * half:]))
    row = one_row

    hid, cot = hidden_in[0], cotangent[0]
    small = jnp.concatenate([segment_ids, time_mask], axis=0)
    hid_s = jnp.where(mine, hid, swap(hid))
    cot_s = jnp.where(mine, cot, swap(cot))
    small_s = jnp.where(mine, small, swap(small))
    seg_c, mask_c = segment_ids.reshape(rows, 1), time_mask.reshape(rows, 1)
    seg_sr, seg_sc, mask_sc = small_s[0:1], small_s[0].reshape(rows, 1), small_s[1].reshape(rows, 1)

    masked = mask_c.astype(F32)
    hid_half = lax.dynamic_slice_in_dim(hid, part * half, half, 1).astype(F32)
    emb_half = lax.dynamic_slice_in_dim(mask_embed, part * half, half, 0).astype(F32)
    start_half = (hid_half + masked * (emb_half - hid_half)).astype(BF16)
    low, wide = lambda *s: (s, BF16), lambda *s: (s, F32)
    conv_low, conv_slope, xq = call(
        conv_fwd_kernel, [low(rows, half), wide(rows, half), low(half, spread_width)],
        [low(rows, spread_width), low(half // CG, TAPS * CG, spread_width), wide(half, spread_width)],
        seg_c, start_half, conv_full.reshape(4, 2, blocks // 8, half, TAPS * CG), row(conv_bias))
    conv_s = turned(conv_low)
    conv_o = swap(conv_s)
    c0, c1 = jnp.where(core == 0, conv_s, conv_o), jnp.where(core == 0, conv_o, conv_s)

    def attn_kernel(*refs):
        attn_fwd_kernel(*refs[:7], refs[7:9], *refs[9:])

    mixed, mlow, qkv, ctx, lse, part1, stat_conv = call(
        attn_kernel, sh["attn_out"] + [wide(1, half)], sh["attn_scratch"],
        hid_s, c0, c1, mask_sc, seg_sc, seg_sr, row(mask_embed), w_qk, w_vo, qb, vb)
    n1, r1, nlow, hidden, slope, part2, stat_attn = call(
        ffn_fwd_kernel, sh["ffn_out"], [],
        mixed, part1, swap(part1), seg_sc, row(out_bias), row(first_gain), row(first_shift), w_ul, w_ur, ub, w_dl, w_dr)
    out_s, gr2, part3, ddl, ddr, dul, dur, sums2, d_ub = call(
        ffn_bwd_kernel,
        [low(rows, width), wide(rows, width), low(rows, width)] + [low(width, n)] * 4 + [wide(5, width), wide(1, ff)],
        [low(rows, width), low(rows, ff)],
        n1, row(first_gain), row(first_shift), part2, swap(part2), seg_sc, row(down_bias), row(second_gain), row(second_shift), cot_s, nlow,
        hidden, slope, w_ul, w_ur, w_dl, w_dr)
    other_out = lax.ppermute(out_s, "mp", [(0, 1), (1, 0)])
    layer_out = jnp.where(mine, out_s, other_out)[None]
    own, send, dqk, dvo, sums1, d_qkvb = call(
        attn_bwd_plain_kernel,
        [wide(rows, half), low(rows, half), low(width, 2 * half), low(width, 2 * half), wide(3, width), wide(1, 3 * half)], sh["back_scratch"],
        gr2, part3, swap(part3), n1, r1, row(first_gain), seg_sc, seg_sr, ctx, qkv, lse, mlow, w_qk, w_vo)
    gm_half = turned((own + swap(send).astype(F32)).astype(BF16))
    d_conv, input_grad, d_cb, d_me = call(
        conv_bwd_kernel,
        [low(blocks, half, TAPS * CG), wide(rows, half), wide(1, half), wide(1, half)],
        [low(rows, spread_width), low(half, spread_width), low(blocks * CG, spread_width), wide(half, spread_width)],
        seg_c, xq, conv_full, conv_slope, gm_half, mask_c)

    d_wall = jnp.concatenate([dqk, dvo, dul, dur, ddl, ddr], axis=1)
    d_wall = turned(lax.psum_scatter(d_wall, BOTH, scatter_dimension=0, tiled=True, axis_index_groups=core_groups)).astype(F32)
    d_conv = lax.psum_scatter(d_conv.swapaxes(1, 2).reshape(blocks * TAPS * CG, half), "dp", scatter_dimension=0, tiled=True).astype(F32)
    once = (jnp.arange(width) // half == core).astype(F32)[None]
    put = lambda v, which: lax.dynamic_update_slice(jnp.zeros((1, 2 * v.shape[1]), F32), v, (0, which * v.shape[1]))
    full = jnp.concatenate([sums2, sums1, stat_attn], axis=0) * once
    pieces = [put(d_me, part), put(d_cb, part), put(d_qkvb[:, :half], core), put(d_qkvb[:, 2 * half:], core), put(d_ub, core)]
    stats = jnp.stack([jnp.sum(stat_conv) * 0.5, jnp.sum(full[8]), jnp.sum(full[0]), jnp.sum(full[1]), jnp.sum((seg_c != 0).astype(F32)) * 0.5])
    flat = jnp.concatenate([jnp.concatenate(pieces, axis=1)[0], full[2:8].reshape(-1), stats])
    flat = lax.psum(flat, BOTH)
    at = 0
    sections = []
    for size in (width, width, width, width, 2 * ff) + (width,) * 6 + (5,):
        sections.append(flat[at:at + size])
        at += size
    me, cb, dqb, dvb, dub, g2, s2, db, g1, s1, ob, st = sections
    half_of = lambda v: lax.dynamic_slice_in_dim(v, part * (v.shape[0] // 2), v.shape[0] // 2, 0)
    stream_rms = jnp.sqrt(st[:4] / (st[4] * width))
    q_, k_, v_, o_, u_, d_ = jnp.split(d_wall, [half, 2 * half, 3 * half, 4 * half, 4 * half + ff], axis=1)
    return (layer_out, input_grad[None], half_of(me), d_conv, half_of(cb), q_, k_, v_, half_of(dqb), half_of(dvb), o_.T, ob, g1, s1,
            u_, half_of(dub), d_.T, db, g2, s2, stream_rms)


def solution(mesh):
    split, half, turn = P("dp", "mp"), P("mp"), P("mp", "dp")
    whole = P()
    rows = P("dp", None, None)
    return jax.shard_map(
        local_close if mesh.shape["dp"] == 16 else functools.partial(local_any, mesh.shape["dp"]),
        mesh=mesh,
        in_specs=(rows, P("dp", None), P("dp", None), whole, split, half, split, split, split, half, half, turn, whole, whole, whole,
                  split, half, turn, whole, whole, whole, rows),
        out_specs=(rows, P("dp", None, "mp"), half, split, half, split, split, split, half, half, turn, whole, whole, whole,
                   split, half, turn, whole, whole, whole, whole),
        check_vma=False,
    )
```

```python
import functools

import jax
import jax.numpy as jnp
from jax import lax
from jax.experimental import pallas as pl
from jax.experimental.pallas import tpu as pltpu
from jax.sharding import PartitionSpec as P

HD = 64
KW = 128
CG = 48
TAPS = 8
EPS = 1e-05
F32 = jnp.float32
BF16 = jnp.bfloat16
NN = (((1,), (0,)), ((), ()))
NT = (((1,), (1,)), ((), ()))
TN = (((0,), (0,)), ((), ()))
BOTH = ("dp", "mp")
CROSS_AT = (3, 5, 6, 8, 9, 11, 13, 15)
FOLD_AT = ((0, 1, 6), (1, 0, 6), (0, 2, 8), (0, 3, 12), (1, 1, 14), (1, 2, 15))
TOTAL_AT = (2, 4, 6)
SHOW_AT = 13
FOLD_KINDS = (0, 0)


def dg(a, b, dims):
    return lax.dot_general(a, b, dims, preferred_element_type=F32)


def gelu_parts(v):
    t = 1.0 / (1.0 + (0.3275911 * 0.7071067811865476) * jnp.abs(v))
    e = jnp.exp(-0.5 * v * v)
    poly = t * (0.254829592 + t * (-0.284496736 + t * (1.421413741 + t * (-1.453152027 + t * 1.061405429))))
    tail = 0.5 * poly * e
    return jnp.where(v >= 0, 1.0 - tail, tail), e


def gelu_and_slope(v):
    phi, e = gelu_parts(v)
    return v * phi, phi + v * e * 0.3989422804014327


def call(kernel, outs, scratch, *args, hbm_in=(), hbm_out=(), sems=(), meeting=None):
    space = lambda here: pl.BlockSpec(memory_space=pl.ANY if here else pltpu.VMEM)
    return pl.pallas_call(
        kernel,
        out_shape=[jax.ShapeDtypeStruct(s, d) for s, d in outs],
        in_specs=[space(i in hbm_in) for i in range(len(args))],
        out_specs=[space(i in hbm_out) for i in range(len(outs))],
        scratch_shapes=[pltpu.VMEM(s, d) for s, d in scratch] + [pltpu.SemaphoreType.DMA(s) for s in sems],
        compiler_params=pltpu.CompilerParams(vmem_limit_bytes=60 * 2**20, has_side_effects=bool(sems), collective_id=meeting),
    )(*args)


def split_low(v):
    hi = v.astype(BF16)
    return hi, (v - hi.astype(F32)).astype(BF16)


def spread_matrix(seg, length, width):
    rank = jnp.where(seg == 0, 7, seg - 1)
    pos = lax.broadcasted_iota(jnp.int32, (length, 1), 0) + 64 * rank + 8
    hit = pos == lax.broadcasted_iota(jnp.int32, (length, width), 1)
    return hit.astype(F32).astype(BF16)


def rolled(x, left):
    width = x.shape[1]
    left = left % width
    return x if left == 0 else pltpu.roll(x, width - left, 1)


def tap_patches(xg):
    return jnp.concatenate([rolled(xg, r) for r in range(TAPS)], axis=0)


def nothing(*_):
    pass


def block_rows(w_ref, at):
    w = w_ref[(slice(None),) * (len(w_ref.shape) - 2) + (at, slice(None))]
    return w.reshape(-1, w.shape[-1])


def conv_plane(w_ref, patches, ot, plane, first):
    rows = w_ref.shape[0] * w_ref.shape[1]
    per = rows * TAPS

    def body(g, carry):
        at = pl.ds(pl.multiple_of(g * CG, 16), CG)
        y = dg(block_rows(w_ref, at), patches[g], NN)
        acc = y[0:CG, :]
        for j in range(1, rows):
            acc = acc + rolled(y[j * CG:(j + 1) * CG, :], TAPS * j)
        width = acc.shape[1]
        acc = pltpu.roll(acc, lax.rem(width + 64 - per * plane, width), 1)
        if first:
            ot[at, :] = acc
        else:
            ot[at, :] += acc
        return carry

    lax.fori_loop(0, ot.shape[0] // CG, body, 0)


def conv_prepare(seg_ref, x_ref, spread, xq, patches):
    length, width = spread.shape
    spread[...] = spread_matrix(seg_ref[...], length, width)
    xq[...] = dg(x_ref[...], spread[...], TN).astype(BF16)

    def body(g, carry):
        patches[g] = tap_patches(xq[pl.ds(pl.multiple_of(g * CG, 16), CG), :])
        return carry

    lax.fori_loop(0, xq.shape[0] // CG, body, 0)


def conv_finish(seg_ref, b_ref, spread, ot, low_ref, slope_ref, cols):
    hi, lo = split_low(ot[cols, :])
    pre = dg(spread[...], hi, NT) + dg(spread[...], lo, NT) + b_ref[:, cols]
    valid = (seg_ref[...] != 0).astype(F32)
    value, slope = gelu_and_slope(pre)
    low_ref[:, cols] = (valid * value).astype(BF16)
    slope_ref[:, cols] = valid * slope


def conv_fwd_kernel(seg_ref, x_ref, w_ref, b_ref, low_ref, slope_ref, xq, spread, patches, ot):
    conv_prepare(seg_ref, x_ref, spread, xq, patches)
    for plane in range(w_ref.shape[0]):
        conv_plane(w_ref.at[plane], patches, ot, plane, plane == 0)
    conv_finish(seg_ref, b_ref, spread, ot, low_ref, slope_ref, slice(0, x_ref.shape[1]))


def conv_bwd_kernel(seg_ref, xq, w_ref, slope_ref, gm_ref, mask_ref, dw_ref, in_ref, db_ref, dm_ref,
                    spread, dq, d_ref, gq, ready=nothing, beside=nothing, store=None, summed=nothing, between=nothing):
    length, width = spread.shape
    blocks = KW // TAPS
    groups = xq.shape[0] // CG
    spread[...] = spread_matrix(seg_ref[...], length, width)
    dpre = (slope_ref[...] * gm_ref[...].astype(F32)).astype(BF16)
    db_ref[...] = jnp.sum(dpre.astype(F32), axis=0, keepdims=True)
    masked = mask_ref[...].astype(F32)
    ready()
    mask_cols = dg(jnp.broadcast_to(masked, (length, 128)).astype(BF16), spread[...], TN)[0:1, :]
    dq[...] = dg(dpre, spread[...], TN).astype(BF16)
    place = lambda g: pl.ds(pl.multiple_of(g * CG, 16), CG)

    def shifts(g):
        dqg = dq[place(g), :]
        for b in range(blocks):
            d_ref[b * CG:(b + 1) * CG, :] = rolled(dqg, 64 - TAPS * b)
        return d_ref[...]

    def weight_body(g, carry):
        dw = dg(shifts(g), tap_patches(xq[place(g), :]), NT).astype(BF16).reshape(blocks, CG, TAPS * CG)
        if store is None:
            dw_ref[:, place(g), :] = dw
        else:
            store(g, dw)
        beside(g)
        return carry

    def input_body(g, carry):
        v = dg(block_rows(w_ref, place(g)), shifts(g), TN)
        acc = v[0:CG, :]
        for r in range(1, TAPS):
            acc = acc + rolled(v[r * CG:(r + 1) * CG, :], -r)
        gq[place(g), :] = acc
        beside(groups + g)
        return carry

    lax.fori_loop(0, groups, weight_body, 0)
    lax.fori_loop(0, groups, input_body, 0)
    of_taps = jnp.sum(gq[...] * mask_cols, axis=1, keepdims=True)
    dm_ref[...] = jnp.broadcast_to(of_taps, (of_taps.shape[0], 128)).T[0:1, :] + jnp.sum(masked * gm_ref[...].astype(F32), axis=0, keepdims=True)
    summed()
    hi, lo = split_low(gq[...])
    grad = dg(spread[...], hi, NT) + gm_ref[...].astype(F32)
    between()
    in_ref[...] = (1.0 - masked) * (grad + dg(spread[...], lo, NT))


class Place:
    def __init__(self):
        self.dp, self.y = lax.axis_index("dp"), lax.axis_index("mp")
        self.z, self.x, self.core = self.dp // 4, lax.rem(self.dp // 2, 2), lax.rem(self.dp, 2)

    def at(self, z=None, x=None, core=None, y=None):
        pick = lambda new, old: old if new is None else new
        dp = pick(z, self.z) * 4 + pick(x, self.x) * 2 + pick(core, self.core)
        return {"dp": dp, "mp": pick(y, self.y)}


def push(src, dst, sems, index, device):
    send, recv = sems if isinstance(sems, tuple) else (sems.at[0], sems.at[1])
    return pltpu.make_async_remote_copy(
        src_ref=src, dst_ref=dst, send_sem=send.at[index], recv_sem=recv.at[index],
        device_id=device, device_id_type=pl.DeviceIdType.MESH)


def meet(devices):
    here = pltpu.get_barrier_semaphore()
    for device in devices:
        pl.semaphore_signal(here, inc=1, device_id=device, device_id_type=pl.DeviceIdType.MESH)
    pl.semaphore_wait(here, len(devices))


def partners(p):
    return [p.at(z=lax.rem(p.z + o, 4)) for o in (1, 2, 3)] + [p.at(x=1 - p.x), p.at(core=1 - p.core), p.at(y=1 - p.y)]


def meet_all(p):
    crooked = p.core != p.y
    pl.when(crooked)(lambda: meet(partners(p) + [p.at(core=p.y, y=p.core)]))
    pl.when(jnp.logical_not(crooked))(lambda: meet(partners(p)))


class LineGather:
    UP, DOWN, ACROSS, LAST = range(4)

    def __init__(self, place, own, buf, send, recv, k, third, x_first=True):
        p = self.p = place
        self.own, self.buf, self.send, self.recv, self.k, self.x_first = own, buf, send, recv, k, x_first
        self.t = p.core if third == "core" else p.y
        over_x, over_t = p.at(x=1 - p.x), p.at(**{third: 1 - self.t})
        self.to = [p.at(z=jnp.minimum(p.z + 1, 3)), p.at(z=jnp.maximum(p.z - 1, 0))] + ([over_x, over_t] if x_first else [over_t, over_x])

    def slot(self, z, across=False, last=False):
        flip = lambda v, yes: 1 - v if yes else v
        x, t = (across, last) if self.x_first else (last, across)
        return (z, flip(self.p.x, x), flip(self.t, t))

    def copy(self, way, slot, src=None):
        at = (self.k,) + slot
        return pltpu.make_async_remote_copy(
            src_ref=self.buf.at[slot] if src is None else src, dst_ref=self.buf.at[slot], send_sem=self.send.at[(way,) + at],
            recv_sem=self.recv.at[at], device_id=self.to[way], device_id_type=pl.DeviceIdType.MESH)

    def walk(self, d, start, finish):
        p = self.p
        if d == 0:
            mine = self.slot(p.z)
            pl.when(p.z < 3)(lambda: start(self.UP, mine, True))
            pl.when(p.z > 0)(lambda: start(self.DOWN, mine, True))
            start(self.ACROSS, mine, True)
            start(self.LAST, mine, True)
            return

        def passing(z, way, further):
            slot = self.slot(z)
            finish(slot)
            pl.when(further)(lambda: start(way, slot, False))
            start(self.ACROSS, slot, False)
            start(self.LAST, slot, False)

        def crossed(z):
            slot = self.slot(z, across=True)
            finish(slot)
            start(self.LAST, slot, False)

        if d < 4:
            pl.when(p.z >= d)(lambda: passing(p.z - d, self.UP, p.z < 3))
            pl.when(p.z + d <= 3)(lambda: passing(p.z + d, self.DOWN, p.z > 0))
        if d == 1:
            crossed(p.z)
        else:
            pl.when(p.z >= d - 1)(lambda: crossed(p.z - d + 1))
            pl.when(p.z + d - 1 <= 3)(lambda: crossed(p.z + d - 1))

    def begin(self, way, slot, own):
        self.copy(way, slot, self.own if own else None).start()

    def round(self, d):
        self.walk(d, self.begin, lambda slot: self.copy(0, slot).wait_recv())

    def drain(self):
        for z in range(4):
            for across in (False, True):
                self.copy(0, self.slot(z, across, True)).wait_recv()
        self.sent()

    def sent(self):
        for d in range(5):
            self.walk(d, lambda way, slot, own: self.copy(way, slot, self.own if own else None).wait_send(), nothing)


class Fold:
    def __init__(self, kind, place, grad, sems, k, first, across, out1, cur, mid, last, out):
        self.kind, self.p, self.d, self.first, self.across, self.out1 = kind, place, grad, first, across, out1
        self.cur, self.mid, self.last, self.out = cur, mid, last, out
        p = place
        self.straight = p.core == p.y
        copy = lambda src, dst, n, dev: push(src, dst, sems, (k, n), dev)
        home, partner, sibling = p.at(y=p.core), p.at(x=1 - p.x), p.at(core=1 - p.core)
        away = grad.at[:, 1 - p.x]
        if kind == 0:
            self.over_y = copy(grad, first, 0, home)
            self.to_sibling = copy(out1, cur, 1, sibling)
            self.over_x = copy(cur.at[:, 1 - p.x], across, 2, partner)
        else:
            self.over_x = copy(away, across, 2, partner)
            self.over_y = copy(mid, first, 0, home)
            self.to_sibling = copy(out1, cur, 1, sibling)
        held = mid if kind == 0 else cur
        self.along = [copy(held.at[lax.rem(p.z + o, 4)], last.at[o - 1], 2 + o, p.at(z=lax.rem(p.z + o, 4))) for o in (1, 2, 3)]
        self.held = held

    def one_way(self, copy, sends, wait):
        pl.when(sends)(copy.wait_send if wait else copy.start)
        if wait:
            pl.when(jnp.logical_not(sends))(copy.wait_recv)

    def start(self, n):
        p, wide = self.p, lambda ref: ref.astype(F32)
        crooked = jnp.logical_not(self.straight)
        if n == 0:
            if self.kind == 0:
                self.one_way(self.over_y, crooked, False)
            else:
                self.over_x.start()
        elif n == 1:
            if self.kind == 0:
                @pl.when(self.straight)
                def _():
                    for z in range(4):
                        for x in range(2):
                            self.cur[z, x] = (wide(self.d[z, x, p.core]) + wide(self.first[z, x, p.core])).astype(BF16)
                            self.out1[z, x] = (wide(self.d[z, x, 1 - p.core]) + wide(self.first[z, x, 1 - p.core])).astype(BF16)
                    self.to_sibling.start()
            else:
                for z in range(4):
                    for c in range(2):
                        self.mid[z, c] = (wide(self.d[z, p.x, c]) + wide(self.across[z, c])).astype(BF16)
                self.one_way(self.over_y, crooked, False)
        elif n == 2:
            if self.kind == 0:
                self.over_x.start()
            else:
                @pl.when(self.straight)
                def _():
                    for z in range(4):
                        self.cur[z] = (wide(self.mid[z, p.core]) + wide(self.first[z, p.core])).astype(BF16)
                        self.out1[z] = (wide(self.mid[z, 1 - p.core]) + wide(self.first[z, 1 - p.core])).astype(BF16)
                    self.to_sibling.start()
        elif n == 3:
            if self.kind == 0:
                for z in range(4):
                    self.mid[z] = (wide(self.cur[z, p.x]) + wide(self.across[z])).astype(BF16)
            for c in self.along:
                c.start()
        else:
            self.out[...] = wide(self.held[p.z]) + wide(self.last[0]) + wide(self.last[1]) + wide(self.last[2])

    def wait(self, n):
        crooked = jnp.logical_not(self.straight)
        if n == 3:
            for c in self.along:
                c.wait()
        elif (self.kind, n) in ((0, 0), (1, 1)):
            self.one_way(self.over_y, crooked, True)
        elif (self.kind, n) in ((0, 1), (1, 2)):
            self.one_way(self.to_sibling, self.straight, True)
        else:
            self.over_x.wait()


def fold_scratch(kind, n):
    wide = (4, 2, 48, n)
    if kind == 0:
        shapes = ((4, 2, 2, 48, n), (4, 48, n), wide, wide, (4, 48, n), (3, 48, n))
    else:
        shapes = (wide, wide, (4, 48, n), (4, 48, n), wide, (3, 48, n))
    return [(s, BF16) for s in shapes]


def columns(rows_ref):
    return rows_ref[...].astype(F32).T


VECS = dict(embed=(0, 6), out_bias=(6, 6), gain1=(12, 6), shift1=(18, 6), down_bias=(24, 6), gain2=(30, 6), shift2=(36, 6),
            query_bias=(42, 3), value_bias=(45, 3), up_bias=(48, 12), conv_bias=(60, 3))


def lay_out(rows_ref, block_ref, *names):
    for k, name in enumerate(names):
        start, count = VECS[name]
        for j in range(count):
            rows_ref[k:k + 1, j * 128:(j + 1) * 128] = block_ref[start + j:start + j + 1, :]
    return [rows_ref.at[k:k + 1, 0:VECS[name][1] * 128] for k, name in enumerate(names)]


class Flow:
    def __init__(self, sems, *pairs):
        self.copies = [pltpu.make_async_copy(a, b, sems.at[k]) for k, (a, b) in enumerate(pairs)]

    def start(self, *which):
        for k in which or range(len(self.copies)):
            self.copies[k].start()

    def wait(self, *which):
        for k in which or range(len(self.copies)):
            self.copies[k].wait()


def transposed(x):
    a = x.shape[0]
    x = x.astype(F32)
    pad = -a % 128
    if pad:
        x = jnp.concatenate([x, jnp.zeros((pad, x.shape[1]), F32)], axis=0)
    return x.T[:, :a]


def conv_gather_kernel(*refs):
    vectors, refs = refs[:len(VECS)], refs[len(VECS):]
    (seg_row, mask_row, hid_ref, cot_ref, conv_ref, q_ref, k_ref, v_ref, o_ref, up_ref, dn_ref,
     xq, slope_ref, conv_t, hid_s, cot_s, small_s, vecs_t, own_late, w_out, wqk, wvo,
     spread, patches, ot, low, w_ref, shard, staged, own_t, seg, x_ref, small_ref, rows_ref, vecs_ref,
     local, turn, send_c, recv_c, send_w, recv_w) = refs
    p = Place()
    straight = p.core == p.y
    crooked = jnp.logical_not(straight)
    half, n = x_ref.shape[1], staged.shape[2]
    shard[...] = conv_ref[...].T
    meet_all(p)
    conv = LineGather(p, shard, w_ref, send_c, recv_c, 0, "core")
    conv.round(0)
    vecs_ref[...] = jnp.zeros_like(vecs_ref)
    for ref, (start, count) in zip(vectors, VECS.values()):
        line = ref[...].astype(F32).reshape(1, count * 128)
        for j in range(count):
            vecs_ref[start + j:start + j + 1, :] = line[:, j * 128:(j + 1) * 128]
    small_ref[...] = jnp.zeros_like(small_ref)
    small_ref[0:1, :] = seg_row[...]
    small_ref[1:2, :] = mask_row[...]
    w_ref[p.z, p.x, p.core] = shard[...]
    save_w = pltpu.make_async_copy(w_ref, w_out, local.at[0])
    walls = (wqk, wvo)
    lines = [LineGather(p, own_t.at[k], walls[k], send_w, recv_w, k, "y", k == 0) for k in range(2)]
    keep = [pltpu.make_async_copy(own_t.at[k], walls[k].at[p.z, p.x, p.y], local.at[1 + k]) for k in range(2)]
    twin = p.at(core=p.y, y=p.core)
    turned = [push(staged.at[0:2], own_t, turn, (0,), twin), push(staged.at[2:6], own_late, turn, (1,), twin), push(vecs_ref, vecs_t, turn, (2,), twin)]
    pairs = ((hid_ref, hid_s), (cot_ref, cot_s), (small_ref, small_s))
    keep_rows = [pltpu.make_async_copy(a, b, local.at[3 + k]) for k, (a, b) in enumerate(pairs)]
    push_rows = [push(a, b, turn, (3 + k,), p.at(core=1 - p.core)) for k, (a, b) in enumerate(pairs)]

    staged[0, :, :half] = q_ref[...]
    staged[0, :, half:] = k_ref[...]
    staged[1, :, :half] = v_ref[...]
    staged[1, :, half:] = o_ref[...]
    staged[2] = up_ref[:, :n]
    staged[3] = up_ref[:, n:]
    staged[4] = dn_ref[:, :n]
    staged[5] = dn_ref[:, n:]

    @pl.when(straight)
    def _():
        own_t[...] = staged[0:2]
        own_late[...] = staged[2:6]
        vecs_t[...] = vecs_ref[...]
        for c in keep_rows + push_rows:
            c.start()

    @pl.when(crooked)
    def _():
        for c in turned:
            c.start()

    cols = columns(small_ref)
    seg[...] = cols[:, 0:1].astype(jnp.int32)
    mine = pl.ds(pl.multiple_of(p.y * half, 128), half)
    hid = hid_ref[:, mine].astype(F32)
    embed, conv_bias = lay_out(rows_ref, vecs_ref, "embed", "conv_bias")
    x_ref[...] = (hid + cols[:, 1:2] * (rows_ref[0:1, mine] - hid)).astype(BF16)
    conv_prepare(seg, x_ref, spread, xq, patches)

    @pl.when(crooked)
    def _():
        for c in turned:
            c.wait()

    for c in keep:
        c.start()

    def nearest(n):
        pick = lambda *v: jnp.where(p.z == 0, v[0], jnp.where(p.z == 1, v[1], jnp.where(p.z == 2, v[2], v[3])))
        return (p.z, pick(1, 0, 1, 2), pick(2, 2, 3, 1), pick(3, 3, 0, 0))[n]

    def compute(n):
        z = nearest(n)
        for across in (False, True):
            conv.copy(0, conv.slot(z, across, True)).wait_recv()
        conv_plane(w_ref.at[z], patches, ot, z, n == 0)

    conv.round(1)
    compute(0)
    conv.round(2)
    compute(1)
    conv.round(3)
    for g in lines:
        g.round(0)
    compute(2)
    conv.round(4)
    for g in lines:
        g.round(1)
    compute(3)
    conv.sent()
    save_w.start()
    for g in lines:
        g.round(2)
    tile = 128
    turn_conv = [push(low.at[:, j * tile:(j + 1) * tile], conv_t.at[:, j * tile:(j + 1) * tile], turn, (6 + j,), twin) for j in range(half // tile)]
    for j in range(half // tile):
        conv_finish(seg, conv_bias, spread, ot, low, slope_ref, slice(j * tile, (j + 1) * tile))
        pl.when(crooked)(turn_conv[j].start)
        if j == 0:
            for g in lines:
                g.round(3)

    for g in lines:
        g.round(4)

    @pl.when(straight)
    def _():
        conv_t[...] = low[...]
        for c in keep_rows:
            c.wait()
        for c in push_rows:
            c.wait_send()

    @pl.when(crooked)
    def _():
        for c in push_rows:
            c.wait_recv()

    for g in lines:
        g.drain()
    for c in keep:
        c.wait()
    save_w.wait()

    @pl.when(crooked)
    def _():
        for c in turn_conv:
            c.wait()


def attn_gather_kernel(*refs):
    (hid_ref, conv_t, small_ref, vecs_ref, wqk_ref, wvo_ref, own_t,
     mixed_out, mlow_out, qkv_out, ctx_ref, lse_ref, part_ref, stat_ref, other_ref, wul, wur,
     qt, vt, ot, both, segc, mask, rows_ref, mixed_ref, mlow_ref, qkv_ref, local, flow, turn, send_w, recv_w, send_p, recv_p) = refs
    p = Place()
    half = conv_t.shape[1]
    sibling = p.at(core=1 - p.core)
    meet(partners(p))
    walls = (wul, wur)
    lines = [LineGather(p, own_t.at[k], walls[k], send_w, recv_w, k, "y", k == 0) for k in range(2)]
    keep = [pltpu.make_async_copy(own_t.at[k], walls[k].at[p.z, p.x, p.y], local.at[k]) for k in range(2)]
    give = push(conv_t, both.at[p.core], turn, (0,), sibling)
    give.start()
    for c in keep:
        c.start()
    for g in lines:
        g.round(0)
    embed, query_bias, value_bias = lay_out(rows_ref, vecs_ref, "embed", "query_bias", "value_bias")
    save = Flow(flow, (mixed_ref, mixed_out), (mlow_ref, mlow_out), (qkv_ref, qkv_out))
    both[p.core] = conv_t[...]
    cols = columns(small_ref)
    segc[...] = cols[:, 0:1].astype(jnp.int32)
    mask[...] = cols[:, 1:2].astype(jnp.int32)
    give.wait()

    def rounds(d):
        for g in lines:
            g.round(d)

    def beside(n):
        if isinstance(n, int):
            if n in (-3, -1):
                rounds((n + 5) // 2)
            if n == -1:
                save.start()
        else:
            for at in (0, 1):
                pl.when(n == at)(functools.partial(rounds, 3 + at))

    def sent(i, at):
        c = push(part_ref.at[at], other_ref.at[at], (send_p, recv_p), (i,), sibling)
        c.start()
        return c

    copies = attn_fwd_kernel(hid_ref, both.at[0], both.at[1], mask, segc, small_ref.at[0:1], embed, (wqk_ref, wvo_ref), query_bias, value_bias,
                             mixed_ref, mlow_ref, qkv_ref, ctx_ref, lse_ref, part_ref, stat_ref, qt, vt, ot, beside, sent)
    for g in lines:
        g.drain()
    for c in keep + copies:
        c.wait()
    save.wait()


def attn_fwd_kernel(hid_ref, c0_ref, c1_ref, mask_ref, segc_ref, segr_ref, emb_ref, w_refs, qb_ref, vb_ref,
                    mixed_ref, mlow_ref, qkv_ref, ctx_ref, lse_ref, part_ref, stat_ref, qt, vt, ot, beside=nothing, sent=nothing):
    wqk_ref, wvo_ref = w_refs
    rows, width = hid_ref.shape
    half = c0_ref.shape[1]
    heads = half // HD
    step = 256
    stat = jnp.zeros((1, half), F32)
    for i in range(rows // step):
        at = pl.ds(i * step, step)
        conv = jnp.concatenate([c0_ref[at, :].astype(F32), c1_ref[at, :].astype(F32)], axis=1)
        hid = hid_ref[at, :].astype(F32)
        masked = mask_ref[at, :].astype(F32)
        mixed = hid + masked * (emb_ref[...] - hid) + conv
        low = mixed.astype(BF16)
        mixed_ref[at, :] = mixed
        mlow_ref[at, :] = low
        stat = stat + jnp.sum(conv[:, :half] * conv[:, :half] + conv[:, half:] * conv[:, half:], axis=0, keepdims=True)
        qk = dg(low, wqk_ref[...], NN)
        qkv_ref[at, 0:half] = (qk[:, :half] + qb_ref[...]).astype(BF16)
        qkv_ref[at, half:2 * half] = qk[:, half:].astype(BF16)
        qkv_ref[at, 2 * half:] = (dg(low, wvo_ref[:, :half], NN) + vb_ref[...]).astype(BF16)
        beside(i - 4)
    stat_ref[...] = stat
    qt[...] = (qkv_ref[:, 0:half] * jnp.asarray(HD ** -0.5, BF16)).T
    vt[...] = qkv_ref[:, 2 * half:].T

    def pair_body(p, carry):
        beside(p)
        lanes = pl.ds(pl.multiple_of(half + p * 128, 128), 128)
        k_pair = qkv_ref[:, lanes]
        for j in range(2):
            head_at = pl.ds(pl.multiple_of(p * 128 + j * HD, HD), HD)
            qh = qt[head_at, :]
            vh = vt[head_at, :]
            zero = jnp.zeros_like(qh)
            qz = jnp.concatenate([qh, zero] if j == 0 else [zero, qh], axis=0)
            for i in range(rows // step):
                at = slice(i * step, (i + 1) * step)
                s = dg(k_pair, qz[:, at], NN)
                s = jnp.where(segc_ref[...] == segr_ref[:, at], s, -1000000000.0)
                top = jnp.max(s, axis=0, keepdims=True)
                e = jnp.exp(s - top)
                den = jnp.sum(e, axis=0, keepdims=True)
                o = dg(vh, e.astype(BF16), NN) / den
                ot[head_at, at] = jnp.where(segr_ref[:, at] != 0, o, 0.0).astype(BF16)
                lse_ref[pl.ds(2 * p + j, 1), at] = top + jnp.log(den)
        return carry

    lax.fori_loop(0, heads // 2, pair_body, 0)
    ctx_ref[...] = ot[...].T
    copies = []
    for i in range(rows // step):
        at = pl.ds(i * step, step)
        part_ref[at, :] = dg(ctx_ref[at, :], wvo_ref[:, half:], NT).astype(BF16)
        copies.append(sent(i, at))
    return copies


def norm_stats(x):
    centre = x - jnp.mean(x, axis=-1, keepdims=True)
    r = lax.rsqrt(jnp.mean(centre * centre, axis=-1, keepdims=True) + EPS)
    return centre * r, r


def matrix(ref):
    w = ref[...]
    return w if len(w.shape) == 2 else w.reshape(-1, w.shape[-1])


def ffn_fwd_kernel(mixed_ref, p0_ref, p1_ref, seg_ref, ob_ref, g1_ref, s1_ref, ul_ref, ur_ref, ub_ref, dl_ref, dr_ref,
                   n1_ref, r1_ref, low_ref, hid_ref, slope_ref, part_ref, stat_ref, beside=nothing, before_down=nothing, sent=nothing):
    rows, width = mixed_ref.shape
    ff = ul_ref.shape[-1]
    step = 256
    stat_ref[...] = jnp.zeros_like(stat_ref)

    def up_body(i, carry):
        at = pl.ds(pl.multiple_of(i * step, step), step)
        attn = ob_ref[...] + (p0_ref[at, :].astype(F32) + p1_ref[at, :].astype(F32))
        valid = (seg_ref[at, :] != 0).astype(F32)
        stat_ref[...] += jnp.sum(valid * attn * attn, axis=0, keepdims=True)
        n1, r1 = norm_stats(mixed_ref[at, :] + attn)
        n1_ref[at, :] = n1
        r1_ref[at, :] = r1
        low = (n1 * g1_ref[...] + s1_ref[...]).astype(BF16)
        low_ref[at, :] = low
        for k, up in enumerate((ul_ref, ur_ref)):
            cols = slice(k * ff, (k + 1) * ff)
            value, slope = gelu_and_slope(dg(low, matrix(up), NN) + ub_ref[:, cols])
            hid_ref[at, cols] = value.astype(BF16)
            slope_ref[at, cols] = slope.astype(BF16)
        beside(i)
        return carry

    def down_body(i, carry):
        at = pl.ds(pl.multiple_of(i * step, step), step)
        part_ref[at, :] = (dg(hid_ref[at, :ff], matrix(dl_ref), NT) + dg(hid_ref[at, ff:], matrix(dr_ref), NT)).astype(BF16)
        sent(i, at)
        return carry

    lax.fori_loop(0, rows // step, up_body, 0)
    before_down()
    lax.fori_loop(0, rows // step, down_body, 0)


class Give:
    def __init__(self, place, part, other, sems):
        self.make = lambda i, at: push(part.at[at], other.at[at], sems, (i,), place.at(core=1 - place.core))

    def __call__(self, i, at):
        self.make(i, at).start()

    def arrived(self, i, at):
        self.make(i, at).wait()

    def wait(self, parts, step):
        for i in range(parts):
            self.make(i, pl.ds(i * step, step)).wait()


def norm_back(gn, n, r):
    return r * (gn - jnp.mean(gn, axis=-1, keepdims=True) - n * jnp.mean(gn * n, axis=-1, keepdims=True))


def ffn_bwd_kernel(n1_ref, g1_ref, s1_ref, p0_ref, p1_ref, seg_ref, db_ref, g2_ref, s2_ref, cot_ref, low_ref,
                   hid_ref, slope_ref, ul_ref, ur_ref, dl_ref, dr_ref,
                   out_ref, gr2_ref, part_ref, ddl_ref, ddr_ref, dul_ref, dur_ref, sums_ref, dub_ref, fg, hg,
                   here=nothing, down_done=nothing, sent=nothing):
    rows, width = n1_ref.shape
    ff = ul_ref.shape[-1]
    step = 256
    sums_ref[...] = jnp.zeros_like(sums_ref)
    dub_ref[...] = jnp.zeros_like(dub_ref)
    row_sum = lambda v: jnp.sum(v, axis=0, keepdims=True)
    store = lambda ref, v: ref.__setitem__(Ellipsis, v.astype(ref.dtype).reshape(ref.shape))

    def norm_body(i, carry):
        at = pl.ds(pl.multiple_of(i * step, step), step)
        here(i, at)
        ffn = db_ref[...] + (p0_ref[at, :].astype(F32) + p1_ref[at, :].astype(F32))
        valid = (seg_ref[at, :] != 0).astype(F32)
        n2, r2 = norm_stats(n1_ref[at, :] * g1_ref[...] + s1_ref[...] + ffn)
        final = valid * (n2 * g2_ref[...] + s2_ref[...])
        out_ref[at, :] = final.astype(BF16)
        gf = valid * cot_ref[at, :].astype(F32)
        gr2 = norm_back(gf * g2_ref[...], n2, r2)
        gr2_ref[at, :] = gr2
        ffn_grad = gr2.astype(BF16)
        fg[at, :] = ffn_grad
        sums_ref[...] += jnp.concatenate(
            [row_sum(valid * ffn * ffn), row_sum(final * final), row_sum(gf * n2), row_sum(gf), row_sum(ffn_grad.astype(F32))], axis=0)
        return carry

    lax.fori_loop(0, rows // step, norm_body, 0)
    store(ddl_ref, dg(fg[...], hid_ref[:, :ff], TN))
    store(ddr_ref, dg(fg[...], hid_ref[:, ff:], TN))
    down_done()

    def body(i, carry):
        at = pl.ds(pl.multiple_of(i * step, step), step)
        part = 0.0
        for k, (up, down) in enumerate(((ul_ref, dl_ref), (ur_ref, dr_ref))):
            cols = slice(k * ff, (k + 1) * ff)
            hidden_grad = (slope_ref[at, cols].astype(F32) * dg(fg[at, :], matrix(down), NN)).astype(BF16)
            hg[at, cols] = hidden_grad
            dub_ref[:, cols] += row_sum(hidden_grad.astype(F32))
            part = part + dg(hidden_grad, matrix(up), NT)
        part_ref[at, :] = part.astype(BF16)
        sent(i, at)
        return carry

    lax.fori_loop(0, rows // step, body, 0)
    store(dul_ref, dg(low_ref[...], hg[:, :ff], TN))
    store(dur_ref, dg(low_ref[...], hg[:, ff:], TN))


def ffn_kernel(*refs):
    mixed, part1, other1, small, vecs, cot_in, wul_in, wur_in, own_t = refs[:9]
    (n1_out, r1, stat, show_out, gr2_out, part3, ddl_out, ddr_out, dul, dur, sums, dub, other3, first_l, across_r) = refs[9:24]
    (low, hid, slope, part2, other2, fg, hg, seg, wdl, wdr, rows_ref, n1, out_ref, gr2, ddl, ddr, cot, wul, wur) = refs[24:43]
    sem_2, sem_3, sem_f, send_w, recv_w, flow_in, flow_out = refs[43:]
    p = Place()
    straight = p.core == p.y
    crooked = jnp.logical_not(straight)
    load = Flow(flow_in, (wul_in, wul), (wur_in, wur), (cot_in, cot))
    load.start()
    save = Flow(flow_out, (n1, n1_out), (out_ref, show_out), (gr2, gr2_out), (ddl, ddl_out), (ddr, ddr_out))
    meet(partners(p))
    lines = [LineGather(p, own_t.at[2 + k], w, send_w, recv_w, k, "y", k == 0) for k, w in enumerate((wdl, wdr))]
    for k, g in enumerate(lines):
        g.round(0)
        g.buf[p.z, p.x, p.y] = own_t[2 + k]
    seg[...] = columns(small)[:, 0:1].astype(jnp.int32)
    ob, g1, s1, db, g2, s2, ub = lay_out(rows_ref, vecs, "out_bias", "gain1", "shift1", "down_bias", "gain2", "shift2", "up_bias")
    give2, give3 = Give(p, part2, other2, sem_2), Give(p, part3, other3, sem_3)
    over_y = push(ddl, first_l, sem_f, (0,), p.at(y=p.core))
    over_x = push(ddr.at[:, 1 - p.x], across_r, sem_f, (1,), p.at(x=1 - p.x))
    load.wait(0, 1)

    def beside(i):
        for n in range(4):
            @pl.when(i == n)
            def _(n=n):
                for g in lines:
                    g.round(n + 1)

    def before_down():
        save.start(0)
        load.wait(2)
        for g in lines:
            g.drain()

    def down_done():
        pl.when(crooked)(over_y.start)
        over_x.start()
        save.start(1, 2, 3, 4)

    ffn_fwd_kernel(mixed, part1, other1, seg, ob, g1, s1, wul, wur, ub, wdl, wdr,
                   n1, r1, low, hid, slope, part2, stat, beside, before_down, give2)
    ffn_bwd_kernel(n1, g1, s1, part2, other2, seg, db, g2, s2, cot, low, hid, slope, wul, wur, wdl, wdr,
                   out_ref, gr2, part3, ddl, ddr, dul, dur, sums, dub, fg, hg, give2.arrived, down_done, give3)
    give3.wait(4, 256)
    over_x.wait()
    pl.when(straight)(over_y.wait_recv)
    pl.when(crooked)(over_y.wait_send)
    save.wait()


def attn_bwd_kernel(gr2_ref, p0_ref, p1_ref, n1_ref, r1_ref, g1_ref, segc_ref, segr_ref, ctx_ref, qkv_ref, lse_ref,
                    mlow_ref, wqk_ref, wvo_ref,
                    dqk_ref, dvo_ref, sums_ref, dqkvb_ref, gr1, cg, qt, kt, ct, dqt, dk, dv, gqkv, finish, beside=nothing, normed=nothing):
    rows, width = gr2_ref.shape
    half = ctx_ref.shape[1]
    heads = half // HD
    step = 256
    core = lax.rem(lax.axis_index("dp"), 2)
    sums_ref[...] = jnp.zeros_like(sums_ref)
    row_sum = lambda v: jnp.sum(v, axis=0, keepdims=True)

    def norm_body(i, carry):
        at = pl.ds(pl.multiple_of(i * step, step), step)
        gn1 = gr2_ref[at, :] + (p0_ref[at, :].astype(F32) + p1_ref[at, :].astype(F32))
        n1 = n1_ref[at, :]
        g = norm_back(gn1 * g1_ref[...], n1, r1_ref[at, :])
        gr1[at, :] = g
        attn_grad = g.astype(BF16)
        sums_ref[...] += jnp.concatenate([row_sum(gn1 * n1), row_sum(gn1), row_sum(attn_grad.astype(F32))], axis=0)
        back = dg(attn_grad, wvo_ref[:, half:], NN)
        cg[at, :] = jnp.where(segc_ref[at, :] != 0, back, 0.0).astype(BF16)
        return carry

    lax.fori_loop(0, rows // step, norm_body, 0)
    normed()
    store = lambda ref, cols, v: ref.__setitem__((Ellipsis, cols), v.astype(BF16).reshape(ref.shape[:-1] + (v.shape[-1],)))
    store(dvo_ref, slice(half, 2 * half), dg(gr1[...].astype(BF16), ctx_ref[...], TN))
    scale = jnp.asarray(HD ** -0.5, BF16)
    qt[...] = (qkv_ref[:, 0:half] * scale).T
    kt[...] = qkv_ref[:, half:2 * half].T
    ct[...] = cg[...].T
    lane = lax.broadcasted_iota(jnp.int32, (1, 128), 1)

    def pair_body(p, carry):
        base = pl.multiple_of(p * 128, 128)
        k_at = pl.ds(pl.multiple_of(half + base, 128), 128)
        v_at = pl.ds(pl.multiple_of(2 * half + base, 128), 128)
        q_pair = qkv_ref[:, pl.ds(base, 128)] * scale
        o_pair = cg[:, pl.ds(base, 128)]
        dk[...] = jnp.zeros_like(dk)
        dv[...] = jnp.zeros_like(dv)
        for j in range(2):
            head_at = pl.ds(pl.multiple_of(base + j * HD, HD), HD)
            zero = jnp.zeros((HD, rows), BF16)
            put = lambda a: jnp.concatenate([a, zero] if j == 0 else [zero, a], axis=0)
            qz, cz, kh = put(qt[head_at, :]), put(ct[head_at, :]), kt[head_at, :]
            keep = (lane < HD) if j == 0 else (lane >= HD)
            for i in range(rows // step):
                at = slice(i * step, (i + 1) * step)
                s = dg(qkv_ref[:, k_at], qz[:, at], NN)
                pr = jnp.exp(s - lse_ref[pl.ds(2 * p + j, 1), at])
                pr = jnp.where(segc_ref[...] == segr_ref[:, at], pr, 0.0)
                gp = dg(qkv_ref[:, v_at], cz[:, at], NN)
                delta = jnp.sum(pr * gp, axis=0, keepdims=True)
                ds = (pr * (gp - delta)).astype(BF16)
                dv[...] += dg(pr.astype(BF16), jnp.where(keep, o_pair[at, :], jnp.zeros_like(o_pair[at, :])), NN)
                dk[...] += dg(ds, jnp.where(keep, q_pair[at, :], jnp.zeros_like(q_pair[at, :])), NN)
                dqt[head_at, at] = (dg(kh, ds, NN) * (HD ** -0.5)).astype(BF16)
                beside(p, j * (rows // step) + i)
        gqkv[:, k_at] = dk[...].astype(BF16)
        gqkv[:, v_at] = dv[...].astype(BF16)
        return carry

    lax.fori_loop(0, heads // 2, pair_body, 0)
    gqkv[:, 0:half] = dqt[...].T
    mine = pl.ds(pl.multiple_of(core * half, 128), half)
    other = pl.ds(pl.multiple_of((1 - core) * half, 128), half)
    to_mixed = lambda at: (dg(gqkv[:, :2 * half], wqk_ref[at, :], NT) + dg(gqkv[:, 2 * half:], wvo_ref[at, 0:half], NT))
    finish(lambda: to_mixed(other).astype(BF16), lambda: gr1[:, mine] + to_mixed(mine))
    dqkvb_ref[...] = row_sum(gqkv[...].astype(F32))
    dqk_ref[...] = dg(mlow_ref[...], gqkv[:, :2 * half], TN).astype(BF16).reshape(dqk_ref.shape)
    store(dvo_ref, slice(0, half), dg(mlow_ref[...], gqkv[:, 2 * half:], TN))


def attn_bwd_plain_kernel(*refs):
    ins, outs, scratch = refs[:14], refs[14:20], refs[20:]
    own_ref, send_ref = outs[:2]

    def finish(send, own):
        send_ref[...] = send()
        own_ref[...] = own()

    attn_bwd_kernel(*ins, *outs[2:], *scratch, finish)


def attn_bwd_fold_kernel(*refs):
    gr2, part3, other3, n1, r1, vecs, small, ctx_in, qkv_in, lse, mlow_in, wqk_in, wvo, ddl, ddr, dul_in, dur_in, first_l, across_r = refs[:19]
    outs, (gm_out, out_up, out_dn) = refs[19:23], refs[23:26]
    scratch, (segc, send, got, gm, out_dl, out_dr, rows_ref, ctx, qkv, mlow, wqk, dul, dur) = refs[26:35], refs[35:48]
    bufs, (sem_f, sem_g, flow) = refs[48:70], refs[70:]
    n = out_dl.shape[1]
    out_ul, out_ur = out_up.at[:, :n], out_up.at[:, n:]
    p = Place()
    load = Flow(flow, (dur_in, dur), (dul_in, dul), (ctx_in, ctx), (qkv_in, qkv), (mlow_in, mlow), (wqk_in, wqk))
    load.start()
    (g1,) = lay_out(rows_ref, vecs, "gain1")
    straight = p.core == p.y
    meet_all(p)
    segc[...] = columns(small)[:, 0:1].astype(jnp.int32)
    early = [Fold(0, p, ddl, sem_f, 0, first_l, *bufs[0:5], out_dl), Fold(1, p, ddr, sem_f, 1, bufs[5], across_r, *bufs[6:10], out_dr)]
    late = [Fold(0, p, dul, sem_f, 2, *bufs[10:16], out_ul), Fold(1, p, dur, sem_f, 3, *bufs[16:22], out_ur)]

    def step(folds, n, wait=True):
        for f in folds:
            if wait:
                f.wait(n - 1)
            f.start(n)

    step(early, 1, False)
    load.wait(0)
    late[1].start(0)

    def normed():
        load.wait(1, 2, 3, 4, 5)
        step(early, 2)
        late[0].start(0)

    def beside(pair, at):
        if at == 2:
            pl.when(pair == 1)(lambda: step(early, 3))
        if at == 6:
            pl.when(pair == 1)(lambda: step(late, 1))
        if at == 4:
            pl.when(pair == 2)(lambda: step(late, 2))
        if at == 7:
            @pl.when(pair == 2)
            def _():
                step(early, 4)
                out_dn[:, :n] = out_dl[...]
                out_dn[:, n:] = out_dr[...]

    to_sibling = push(send, got, sem_g, (0,), p.at(core=1 - p.core))
    turn = push(gm, gm_out, sem_g, (1,), p.at(core=p.y, y=p.core))

    def finish(give, own):
        send[...] = give()
        to_sibling.start()
        step(late, 3)
        mine = own()
        to_sibling.wait()
        value = (mine + got[...].astype(F32)).astype(BF16)

        @pl.when(straight)
        def _():
            gm_out[...] = value

        @pl.when(jnp.logical_not(straight))
        def _():
            gm[...] = value
            turn.start()

    attn_bwd_kernel(gr2, part3, other3, n1, r1, g1, segc, small.at[0:1], ctx, qkv, lse, mlow, wqk, wvo, *outs, *scratch, finish, beside, normed)
    step(late, 4)
    pl.when(jnp.logical_not(straight))(turn.wait)


class Total:
    def __init__(self, vec, got, sems, hops, p):
        self.vec, self.got, self.n = vec, got, len(hops)
        self.pair = [push(vec.at[n], got.at[n], sems, (n,), device) for n, device in enumerate(hops)]
        self.along = [push(vec.at[self.n], got.at[self.n + o - 1], sems, (self.n + o - 1,), p.at(z=lax.rem(p.z + o, 4))) for o in (1, 2, 3)]

    def step(self, n):
        if n > 0:
            self.pair[n - 1].wait()
            self.vec[n] = self.vec[n - 1] + self.got[n - 1]
        for c in self.along if n == self.n else [self.pair[n]]:
            c.start()

    def result(self):
        for c in self.along:
            c.wait()
        n = self.n
        return self.vec[n] + self.got[n] + self.got[n + 1] + self.got[n + 2]


def conv_fold_kernel(*refs):
    (seg_row, mask_row, xq, w_in, slope_ref, gm_ref, dqk, dvo, sums2, sums1, dqkvb, dub, stat_conv, stat_attn, shown,
     in_ref, dconv_ref, out_qk, out_vo, sums_out, me_out, layer_got, spread, dq, d_ref, gq) = refs[:26]
    seg_ref, mask_ref, small_ref, db_ref, dm_ref, d_all, got_c, sum_c, got_x, sum_x, got_z, vec, got_v, me, got_me, w_ref = refs[26:42]
    folds_bufs, (sem_c, sem_x, sem_z, sem_fold, sem_vec, sem_me, sem_out, flow) = refs[42:54], refs[54:]
    p = Place()
    straight = p.core == p.y
    crooked = jnp.logical_not(straight)
    load = Flow(flow, (w_in, w_ref))
    load.start()
    meet(partners(p))
    groups = 8
    wide = lambda v: v.astype(F32)
    folds = [Fold(FOLD_KINDS[0], p, dqk, sem_fold, 0, *folds_bufs[:6], out_qk), Fold(FOLD_KINDS[1], p, dvo, sem_fold, 1, *folds_bufs[6:], out_vo)]
    folds[0].start(0)
    show = push(shown, layer_got, sem_out, (0,), p.at(y=1 - p.y))
    small_ref[...] = jnp.zeros_like(small_ref)
    small_ref[0:1, :] = seg_row[...]
    small_ref[1:2, :] = mask_row[...]
    cols = columns(small_ref)
    seg_ref[...] = cols[:, 0:1].astype(jnp.int32)
    mask_ref[...] = cols[:, 1:2].astype(jnp.int32)
    hops = [p.at(core=1 - p.core), p.at(x=1 - p.x)]
    total = Total(vec, got_v, sem_vec, hops + [p.at(y=1 - p.y)], p)
    me_total = Total(me, got_me, sem_me, hops, p)
    width = vec.shape[2]
    half = width // 2
    of_half = lambda which: (lax.broadcasted_iota(jnp.int32, (1, width), 1) // half == which).astype(F32)
    twice = lambda v: jnp.concatenate([v, v], axis=1)

    def ready():
        by_core, by_y = of_half(p.core), of_half(p.y)
        is_core = lambda c: (p.core == c).astype(F32)
        frames = jnp.sum(wide(seg_ref[...] != 0), axis=0, keepdims=True)
        rows = [sums1[2:3] * by_core, sums1[0:1] * by_core, sums1[1:2] * by_core, sums2[4:5] * by_core, sums2[2:3] * by_core, sums2[3:4] * by_core,
                twice(db_ref[...]) * by_y, twice(dqkvb[:, :half]) * by_core, twice(dqkvb[:, 2 * half:]) * by_core,
                dub[:, :width] * is_core(0), dub[:, width:] * is_core(0), dub[:, :width] * is_core(1), dub[:, width:] * is_core(1),
                twice(stat_conv[...]) * by_core * 0.5, stat_attn[...] * by_core, sums2[0:1] * by_core, sums2[1:2] * by_core,
                jnp.broadcast_to(frames * 0.5, (1, width))]
        rows.append(jnp.zeros((24 - len(rows), width), F32))
        vec[0] = jnp.concatenate(rows, axis=0)
        total.step(0)

    def store(g, dw):
        d_all[g] = dw.reshape(d_all.shape[1:])

    to_c = lambda g: push(d_all.at[g, :, :, 1 - p.core], got_c.at[g], sem_c, (g,), p.at(core=1 - p.core))
    to_x = lambda g: push(sum_c.at[g, :, 1 - p.x], got_x.at[g], sem_x, (g,), p.at(x=1 - p.x))
    to_z = lambda g: [push(sum_x.at[g, lax.rem(p.z + o, 4)], got_z.at[g, o - 1], sem_z, (g, o - 1), p.at(z=lax.rem(p.z + o, 4)))
                      for o in (1, 2, 3)]

    def fold_step(k, n):
        if n > 0:
            folds[k].wait(n - 1)
        folds[k].start(n)

    def crossed(k):
        to_x(k).wait()
        for z in range(4):
            sum_x[k, z] = (wide(sum_c[k, z, p.x]) + wide(got_x[k, z])).astype(BF16)
        for c in to_z(k):
            c.start()

    def beside(t):
        @pl.when(t < groups)
        def _():
            to_c(t).start()

        @pl.when(jnp.logical_and(t >= 1, t <= groups))
        def _():
            k = t - 1
            to_c(k).wait()
            for z in range(4):
                for x in range(2):
                    sum_c[k, z, x] = (wide(d_all[k, z, x, p.core]) + wide(got_c[k, z, x])).astype(BF16)
            to_x(k).start()

        for k, at in enumerate(CROSS_AT):
            pl.when(t == at)(functools.partial(crossed, k))
        for k, n, at in FOLD_AT:
            pl.when(t == at)(functools.partial(fold_step, k, n))
        for n, at in zip((1, 2, 3), TOTAL_AT):
            pl.when(t == at)(functools.partial(total.step, n))
        pl.when(jnp.logical_and(t == SHOW_AT, straight))(show.start)
        pl.when(t == groups - 1)(load.wait)

    def summed():
        me[0] = jnp.broadcast_to(dm_ref[...], me.shape[1:])
        me_total.step(0)

    conv_bwd_kernel(seg_ref, xq, w_ref, slope_ref, gm_ref, mask_ref, None, in_ref, db_ref, dm_ref,
                    spread, dq, d_ref, gq, ready, beside, store, summed, lambda: me_total.step(1))
    me_total.step(2)
    if (1, 3) not in [at[:2] for at in FOLD_AT]:
        fold_step(1, 3)
    for k in range(len(CROSS_AT), groups):
        crossed(k)
    sums_out[...] = total.result()
    me_out[...] = me_total.result()
    for k in range(2):
        fold_step(k, 4)
    for k in range(groups):
        for c in to_z(k):
            c.wait()
        gq[k * CG:(k + 1) * CG, 0:TAPS * CG] = wide(sum_x[k, p.z]) + wide(got_z[k, 0]) + wide(got_z[k, 1]) + wide(got_z[k, 2])
    dconv_ref[...] = gq[:, 0:TAPS * CG].T
    pl.when(straight)(show.wait_send)
    pl.when(crooked)(show.wait_recv)


def result_kernel(*refs):
    (shown, layer_got, grad, dconv, oqk, ovo, dup, ddn, sums, me,
     layer_out, input_grad, mask_out, conv_out, convb_out, q_out, k_out, v_out, qb_out, vb_out, o_out, ob_out, g1_out, s1_out,
     up_out, ub_out, dn_out, db_out, g2_out, s2_out, rms_out, flow) = refs
    y = lax.axis_index("mp")
    straight = lax.rem(lax.axis_index("dp"), 2) == y
    move = Flow(flow, (grad, input_grad), (dconv, conv_out), (dup, up_out), (ddn, dn_out), (shown, layer_out))
    got = pltpu.make_async_copy(layer_got, layer_out, flow.at[5])
    move.start(0, 1, 2, 3)
    pl.when(straight)(lambda: move.start(4))
    pl.when(jnp.logical_not(straight))(got.start)
    half = q_out.shape[1]
    width = sums.shape[1]
    q_out[...] = oqk[:, :half]
    k_out[...] = oqk[:, half:]
    v_out[...] = ovo[:, :half]
    o_out[...] = ovo[:, half:]
    line = lambda ref, v: ref.__setitem__(Ellipsis, v.reshape(ref.shape))
    part = lambda k: jnp.where(y == 0, sums[k:k + 1, :half], sums[k:k + 1, half:])
    for k, ref in enumerate((ob_out, g1_out, s1_out, db_out, g2_out, s2_out)):
        line(ref, sums[k:k + 1, :])
    line(mask_out, me[0:1, :])
    for k, ref in ((6, convb_out), (7, qb_out), (8, vb_out)):
        line(ref, part(k))
    pair = lambda k: jnp.concatenate([sums[k:k + 1, :], sums[k + 1:k + 2, :]], axis=1)
    line(ub_out, jnp.where(y == 0, pair(9), pair(11)))
    power = lambda k: jnp.sum(sums[k:k + 1, :], axis=1, keepdims=True)
    rms = jnp.sqrt(jnp.concatenate([power(k) for k in (13, 14, 15, 16)], axis=1) / (sums[17:18, 0:1] * width))
    line(rms_out, rms)
    move.wait(0, 1, 2, 3)
    pl.when(straight)(lambda: move.wait(4))
    pl.when(jnp.logical_not(straight))(got.wait)


def one_row(v):
    return v.astype(F32)[None]


def flat_turn(n_all):
    return [(f, f // 4 * 4 + (f % 2) * 2 + (f // 2) % 2) for f in range(n_all)]


def shapes(rows, width, ff):
    half = width // 2
    heads = half // HD
    spread_width = -(-(rows + 7 * 64 + 64) // 128) * 128
    blocks = KW // TAPS
    low, wide = lambda *s: (s, BF16), lambda *s: (s, F32)
    return dict(
        half=half, spread_width=spread_width, blocks=blocks,
        attn_out=[wide(rows, width), low(rows, width), low(rows, 3 * half), low(rows, half), wide(heads, rows), low(rows, width)],
        attn_scratch=[low(half, rows)] * 3,
        ffn_out=[wide(rows, width), wide(rows, 1), low(rows, width), low(rows, ff), low(rows, ff), low(rows, width), wide(1, width)],
        back_scratch=[wide(rows, width), low(rows, half), low(half, rows), low(half, rows), low(half, rows), low(half, rows),
                      wide(rows, 128), wide(rows, 128), low(rows, 3 * half)],
    )


def local_close(hidden_in, segment_ids, time_mask, mask_embed, conv_weight, conv_bias, query_weight, key_weight,
                value_weight, query_bias, value_bias, out_weight, out_bias, first_gain, first_shift, up_weight, up_bias,
                down_weight, down_bias, second_gain, second_shift, cotangent):
    _, rows, width = hidden_in.shape
    ff = up_weight.shape[1]
    n = ff // 2
    sh = shapes(rows, width, ff)
    half, sw, blocks = sh["half"], sh["spread_width"], sh["blocks"]
    low, wide = lambda *s: (s, BF16), lambda *s: (s, F32)
    block = wide(64, 128)
    column = ((rows, 1), jnp.int32)
    eight = ((8, rows), jnp.int32)
    seats = (4, 2, 2)
    wall = [low(*seats, 48, n)]
    line_sems = ((4, 2) + seats, (2,) + seats)

    xq, slope, conv_t, hid_s, cot_s, small_s, vecs_t, own_late, conv_full, w_qk, w_vo = call(
        conv_gather_kernel,
        [low(half, sw), wide(rows, half), low(rows, half), low(rows, width), low(rows, width), eight, block, low(4, 48, n),
         low(*seats, half, TAPS * CG)] + wall * 2,
        [low(rows, sw), low(half // CG, TAPS * CG, sw), wide(half, sw), low(rows, half), low(*seats, half, TAPS * CG), low(half, TAPS * CG),
         low(6, 48, n), low(2, 48, n), column, low(rows, half), eight, wide(8, width), block],
        mask_embed, out_bias, first_gain, first_shift, down_bias, second_gain, second_shift, query_bias, value_bias, up_bias, conv_bias,
        segment_ids, time_mask, hidden_in[0], cotangent[0], conv_weight, query_weight, key_weight, value_weight, out_weight.T, up_weight,
        down_weight.T, hbm_out=(3, 4, 5, 8, 9, 10), sems=((6,), (2, 9), (4, 1) + seats, (1,) + seats) + line_sems, meeting=1)
    flat = lambda w: w.reshape(width, n)
    w_qk, w_vo = flat(w_qk), flat(w_vo)
    held = [wide(rows, width), low(rows, width), low(rows, 3 * half)]
    mixed, mlow, qkv, ctx, lse, part1, stat_conv, other1, w_ul, w_ur = call(
        attn_gather_kernel, sh["attn_out"] + [wide(1, half), low(rows, width)] + wall * 2,
        sh["attn_scratch"] + [low(2, rows, half), column, column, wide(8, width)] + held,
        hid_s, conv_t, small_s, vecs_t, w_qk, w_vo, own_late,
        hbm_out=(0, 1, 2, 8, 9), sems=((2,), (3,), (2, 1)) + line_sems + ((4,), (4,)), meeting=2)
    w_ul, w_ur = flat(w_ul), flat(w_ur)
    grad = low(*seats, 48, n)
    weight = low(width, n)
    n1, r1, stat_attn, out_s, gr2, part3, ddl, ddr, dul, dur, sums2, d_ub, other3, first_l, across_r = call(
        ffn_kernel,
        [wide(rows, width), wide(rows, 1), wide(1, width), low(rows, width), wide(rows, width), low(rows, width)] + [grad] * 4
        + [wide(5, width), wide(1, ff), low(rows, width), grad, low(4, 2, 48, n)],
        [low(rows, width), low(rows, ff), low(rows, ff), low(rows, width), low(rows, width), low(rows, width), low(rows, ff), column, grad, grad,
         wide(8, ff), wide(rows, width), low(rows, width), wide(rows, width), grad, grad, low(rows, width), weight, weight],
        mixed, part1, other1, small_s, vecs_t, cot_s, w_ul, w_ur, own_late,
        hbm_in=(5, 6, 7), hbm_out=(0, 3, 4, 6, 7), sems=((2, 4), (2, 4), (2, 2)) + line_sems + ((3,), (5,)), meeting=3)
    kinds = [fold_scratch(0, n)[1:], fold_scratch(1, n)[:1] + fold_scratch(1, n)[2:], fold_scratch(0, n), fold_scratch(1, n)]
    own = [wide(48, n)] * 2
    dqk, dvo, sums1, d_qkvb, gm, d_up, d_down = call(
        attn_bwd_fold_kernel,
        [grad, grad, wide(3, width), wide(1, 3 * half), low(rows, half), wide(48, ff), wide(48, ff)],
        sh["back_scratch"] + [column, low(rows, half), low(rows, half), low(rows, half)] + own
        + [wide(8, width), low(rows, half), low(rows, 3 * half), low(rows, width), weight, grad, grad] + sum(kinds, []),
        gr2, part3, other3, n1, r1, vecs_t, small_s, ctx, qkv, lse, mlow, w_qk, w_vo, ddl, ddr, dul, dur, first_l, across_r,
        hbm_in=(7, 8, 10, 11, 15, 16), sems=((2, 4, 6), (2, 2), (6,)), meeting=5)
    in_grad, d_conv, d_qk, d_vo, sums, d_me, got_out = call(
        conv_fold_kernel,
        [wide(rows, half), wide(TAPS * CG, half), wide(48, n), wide(48, n), wide(24, width), wide(8, half), low(rows, width)],
        [low(rows, sw), low(half, sw), low(blocks * CG, sw), wide(half, sw), column, column, eight, wide(1, half), wide(1, half),
         low(8, *seats, CG, TAPS * CG), low(8, 4, 2, CG, TAPS * CG), low(8, 4, 2, CG, TAPS * CG), low(8, 4, CG, TAPS * CG),
         low(8, 4, CG, TAPS * CG), low(8, 3, CG, TAPS * CG), wide(4, 24, width), wide(6, 24, width), wide(3, 8, half), wide(5, 8, half),
         low(*seats, half, TAPS * CG)] + fold_scratch(FOLD_KINDS[0], n) + fold_scratch(FOLD_KINDS[1], n),
        segment_ids, time_mask, xq, conv_full, slope, gm, dqk, dvo, sums2, sums1, d_qkvb, d_ub, stat_conv, stat_attn, out_s,
        hbm_in=(3, 14), hbm_out=(6,), sems=((2, 8), (2, 8), (2, 8, 3), (2, 2, 6), (2, 6), (2, 5), (2, 1), (1,)), meeting=6)
    line, shard = lambda size: ((size,), F32), wide(48, half)
    results = list(call(
        result_kernel,
        [low(rows, width), wide(rows, half), line(half), wide(TAPS * CG, half), line(half), shard, shard, shard, line(half), line(half), shard,
         line(width), line(width), line(width), wide(48, ff), line(ff), wide(48, ff), line(width), line(width), line(width), line(4)],
        [], out_s, got_out, in_grad, d_conv, d_qk, d_vo, d_up, d_down, sums, d_me, hbm_in=(0, 1, 2, 3, 6, 7), sems=((6,),)))
    results[0], results[1], results[10], results[16] = results[0][None], results[1][None], results[10].T, results[16].T
    return tuple(results)


def local_any(n_dp, hidden_in, segment_ids, time_mask, mask_embed, conv_weight, conv_bias, query_weight, key_weight,
          value_weight, query_bias, value_bias, out_weight, out_bias, first_gain, first_shift, up_weight, up_bias,
          down_weight, down_bias, second_gain, second_shift, cotangent):
    _, rows, width = hidden_in.shape
    ff = up_weight.shape[1]
    n = ff // 2
    sh = shapes(rows, width, ff)
    half, spread_width, blocks = sh["half"], sh["spread_width"], sh["blocks"]
    part = lax.axis_index("mp")
    core = lax.rem(lax.axis_index("dp"), 2)
    n_all = 2 * n_dp
    turn = flat_turn(n_all)
    sibling = [(f, f ^ 2) for f in range(n_all)]
    core_groups = [[f for f in range(n_all) if (f // 2) % 2 == c] for c in range(2)]
    swap = lambda v: lax.ppermute(v, BOTH, sibling)
    turned = lambda v: lax.ppermute(v, BOTH, turn)
    mine = part == core

    down_t = down_weight.T
    w_shards = [jnp.concatenate([query_weight, key_weight], axis=1), jnp.concatenate([value_weight, out_weight.T], axis=1),
                up_weight[:, :n], up_weight[:, n:], down_t[:, :n], down_t[:, n:]]
    conv_full = lax.all_gather(conv_weight, "dp", axis=0, tiled=True)
    conv_full = conv_full.reshape(blocks, TAPS * CG, half).swapaxes(1, 2)
    w_qk, w_vo, w_ul, w_ur, w_dl, w_dr = (
        lax.all_gather(turned(w), BOTH, axis=0, tiled=True, axis_index_groups=core_groups) for w in w_shards)
    bias = turned(jnp.concatenate([query_bias, value_bias, up_bias])[None])
    qb, vb, ub = (b.astype(F32) for b in (bias[:, :half], bias[:, half:2 * half], bias[:, 2 * half:]))
    row = one_row

    hid, cot = hidden_in[0], cotangent[0]
    small = jnp.concatenate([segment_ids, time_mask], axis=0)
    hid_s = jnp.where(mine, hid, swap(hid))
    cot_s = jnp.where(mine, cot, swap(cot))
    small_s = jnp.where(mine, small, swap(small))
    seg_c, mask_c = segment_ids.reshape(rows, 1), time_mask.reshape(rows, 1)
    seg_sr, seg_sc, mask_sc = small_s[0:1], small_s[0].reshape(rows, 1), small_s[1].reshape(rows, 1)

    masked = mask_c.astype(F32)
    hid_half = lax.dynamic_slice_in_dim(hid, part * half, half, 1).astype(F32)
    emb_half = lax.dynamic_slice_in_dim(mask_embed, part * half, half, 0).astype(F32)
    start_half = (hid_half + masked * (emb_half - hid_half)).astype(BF16)
    low, wide = lambda *s: (s, BF16), lambda *s: (s, F32)
    conv_low, conv_slope, xq = call(
        conv_fwd_kernel, [low(rows, half), wide(rows, half), low(half, spread_width)],
        [low(rows, spread_width), low(half // CG, TAPS * CG, spread_width), wide(half, spread_width)],
        seg_c, start_half, conv_full.reshape(4, 2, blocks // 8, half, TAPS * CG), row(conv_bias))
    conv_s = turned(conv_low)
    conv_o = swap(conv_s)
    c0, c1 = jnp.where(core == 0, conv_s, conv_o), jnp.where(core == 0, conv_o, conv_s)

    def attn_kernel(*refs):
        attn_fwd_kernel(*refs[:7], refs[7:9], *refs[9:])

    mixed, mlow, qkv, ctx, lse, part1, stat_conv = call(
        attn_kernel, sh["attn_out"] + [wide(1, half)], sh["attn_scratch"],
        hid_s, c0, c1, mask_sc, seg_sc, seg_sr, row(mask_embed), w_qk, w_vo, qb, vb)
    n1, r1, nlow, hidden, slope, part2, stat_attn = call(
        ffn_fwd_kernel, sh["ffn_out"], [],
        mixed, part1, swap(part1), seg_sc, row(out_bias), row(first_gain), row(first_shift), w_ul, w_ur, ub, w_dl, w_dr)
    out_s, gr2, part3, ddl, ddr, dul, dur, sums2, d_ub = call(
        ffn_bwd_kernel,
        [low(rows, width), wide(rows, width), low(rows, width)] + [low(width, n)] * 4 + [wide(5, width), wide(1, ff)],
        [low(rows, width), low(rows, ff)],
        n1, row(first_gain), row(first_shift), part2, swap(part2), seg_sc, row(down_bias), row(second_gain), row(second_shift), cot_s, nlow,
        hidden, slope, w_ul, w_ur, w_dl, w_dr)
    other_out = lax.ppermute(out_s, "mp", [(0, 1), (1, 0)])
    layer_out = jnp.where(mine, out_s, other_out)[None]
    own, send, dqk, dvo, sums1, d_qkvb = call(
        attn_bwd_plain_kernel,
        [wide(rows, half), low(rows, half), low(width, 2 * half), low(width, 2 * half), wide(3, width), wide(1, 3 * half)], sh["back_scratch"],
        gr2, part3, swap(part3), n1, r1, row(first_gain), seg_sc, seg_sr, ctx, qkv, lse, mlow, w_qk, w_vo)
    gm_half = turned((own + swap(send).astype(F32)).astype(BF16))
    d_conv, input_grad, d_cb, d_me = call(
        conv_bwd_kernel,
        [low(blocks, half, TAPS * CG), wide(rows, half), wide(1, half), wide(1, half)],
        [low(rows, spread_width), low(half, spread_width), low(blocks * CG, spread_width), wide(half, spread_width)],
        seg_c, xq, conv_full, conv_slope, gm_half, mask_c)

    d_wall = jnp.concatenate([dqk, dvo, dul, dur, ddl, ddr], axis=1)
    d_wall = turned(lax.psum_scatter(d_wall, BOTH, scatter_dimension=0, tiled=True, axis_index_groups=core_groups)).astype(F32)
    d_conv = lax.psum_scatter(d_conv.swapaxes(1, 2).reshape(blocks * TAPS * CG, half), "dp", scatter_dimension=0, tiled=True).astype(F32)
    once = (jnp.arange(width) // half == core).astype(F32)[None]
    put = lambda v, which: lax.dynamic_update_slice(jnp.zeros((1, 2 * v.shape[1]), F32), v, (0, which * v.shape[1]))
    full = jnp.concatenate([sums2, sums1, stat_attn], axis=0) * once
    pieces = [put(d_me, part), put(d_cb, part), put(d_qkvb[:, :half], core), put(d_qkvb[:, 2 * half:], core), put(d_ub, core)]
    stats = jnp.stack([jnp.sum(stat_conv) * 0.5, jnp.sum(full[8]), jnp.sum(full[0]), jnp.sum(full[1]), jnp.sum((seg_c != 0).astype(F32)) * 0.5])
    flat = jnp.concatenate([jnp.concatenate(pieces, axis=1)[0], full[2:8].reshape(-1), stats])
    flat = lax.psum(flat, BOTH)
    at = 0
    sections = []
    for size in (width, width, width, width, 2 * ff) + (width,) * 6 + (5,):
        sections.append(flat[at:at + size])
        at += size
    me, cb, dqb, dvb, dub, g2, s2, db, g1, s1, ob, st = sections
    half_of = lambda v: lax.dynamic_slice_in_dim(v, part * (v.shape[0] // 2), v.shape[0] // 2, 0)
    stream_rms = jnp.sqrt(st[:4] / (st[4] * width))
    q_, k_, v_, o_, u_, d_ = jnp.split(d_wall, [half, 2 * half, 3 * half, 4 * half, 4 * half + ff], axis=1)
    return (layer_out, input_grad[None], half_of(me), d_conv, half_of(cb), q_, k_, v_, half_of(dqb), half_of(dvb), o_.T, ob, g1, s1,
            u_, half_of(dub), d_.T, db, g2, s2, stream_rms)


def solution(mesh):
    split, half, turn = P("dp", "mp"), P("mp"), P("mp", "dp")
    whole = P()
    rows = P("dp", None, None)
    return jax.shard_map(
        local_close if mesh.shape["dp"] == 16 else functools.partial(local_any, mesh.shape["dp"]),
        mesh=mesh,
        in_specs=(rows, P("dp", None), P("dp", None), whole, split, half, split, split, split, half, half, turn, whole, whole, whole,
                  split, half, turn, whole, whole, whole, rows),
        out_specs=(rows, P("dp", None, "mp"), half, split, half, split, split, split, half, half, turn, whole, whole, whole,
                   split, half, turn, whole, whole, whole, whole),
        check_vma=False,
    )
```

```python
import functools

import jax
import jax.numpy as jnp
from jax import lax
from jax.experimental import pallas as pl
from jax.experimental.pallas import tpu as pltpu
from jax.sharding import PartitionSpec as P

HD = 64
KW = 128
CG = 48
TAPS = 8
EPS = 1e-05
F32 = jnp.float32
BF16 = jnp.bfloat16
NN = (((1,), (0,)), ((), ()))
NT = (((1,), (1,)), ((), ()))
TN = (((0,), (0,)), ((), ()))
BOTH = ("dp", "mp")
CROSS_AT = (3, 5, 6, 8, 9, 11, 13, 15)
FOLD_AT = ((0, 1, 6), (1, 0, 6), (0, 2, 8), (0, 3, 12), (1, 1, 14), (1, 2, 15))
TOTAL_AT = (2, 4, 6)
SHOW_AT = 13
FOLD_KINDS = (0, 0)


def dg(a, b, dims):
    return lax.dot_general(a, b, dims, preferred_element_type=F32)


def gelu_parts(v):
    t = 1.0 / (1.0 + (0.3275911 * 0.7071067811865476) * jnp.abs(v))
    e = jnp.exp(-0.5 * v * v)
    poly = t * (0.254829592 + t * (-0.284496736 + t * (1.421413741 + t * (-1.453152027 + t * 1.061405429))))
    tail = 0.5 * poly * e
    return jnp.where(v >= 0, 1.0 - tail, tail), e


def gelu_and_slope(v):
    phi, e = gelu_parts(v)
    return v * phi, phi + v * e * 0.3989422804014327


def call(kernel, outs, scratch, *args, hbm_in=(), hbm_out=(), sems=(), meeting=None):
    space = lambda here: pl.BlockSpec(memory_space=pl.ANY if here else pltpu.VMEM)
    return pl.pallas_call(
        kernel,
        out_shape=[jax.ShapeDtypeStruct(s, d) for s, d in outs],
        in_specs=[space(i in hbm_in) for i in range(len(args))],
        out_specs=[space(i in hbm_out) for i in range(len(outs))],
        scratch_shapes=[pltpu.VMEM(s, d) for s, d in scratch] + [pltpu.SemaphoreType.DMA(s) for s in sems],
        compiler_params=pltpu.CompilerParams(vmem_limit_bytes=60 * 2**20, has_side_effects=bool(sems), collective_id=meeting),
    )(*args)


def split_low(v):
    hi = v.astype(BF16)
    return hi, (v - hi.astype(F32)).astype(BF16)


def spread_matrix(seg, length, width):
    rank = jnp.where(seg == 0, 7, seg - 1)
    pos = lax.broadcasted_iota(jnp.int32, (length, 1), 0) + 64 * rank + 8
    hit = pos == lax.broadcasted_iota(jnp.int32, (length, width), 1)
    return hit.astype(F32).astype(BF16)


def rolled(x, left):
    width = x.shape[1]
    left = left % width
    return x if left == 0 else pltpu.roll(x, width - left, 1)


def tap_patches(xg):
    return jnp.concatenate([rolled(xg, r) for r in range(TAPS)], axis=0)


def nothing(*_):
    pass


def block_rows(w_ref, at):
    w = w_ref[(slice(None),) * (len(w_ref.shape) - 2) + (at, slice(None))]
    return w.reshape(-1, w.shape[-1])


def conv_plane(w_ref, patches, ot, plane, first):
    rows = w_ref.shape[0] * w_ref.shape[1]
    per = rows * TAPS

    def body(g, carry):
        at = pl.ds(pl.multiple_of(g * CG, 16), CG)
        y = dg(block_rows(w_ref, at), patches[g], NN)
        acc = y[0:CG, :]
        for j in range(1, rows):
            acc = acc + rolled(y[j * CG:(j + 1) * CG, :], TAPS * j)
        width = acc.shape[1]
        acc = pltpu.roll(acc, lax.rem(width + 64 - per * plane, width), 1)
        if first:
            ot[at, :] = acc
        else:
            ot[at, :] += acc
        return carry

    lax.fori_loop(0, ot.shape[0] // CG, body, 0)


def conv_prepare(seg_ref, x_ref, spread, xq, patches):
    length, width = spread.shape
    spread[...] = spread_matrix(seg_ref[...], length, width)
    xq[...] = dg(x_ref[...], spread[...], TN).astype(BF16)

    def body(g, carry):
        patches[g] = tap_patches(xq[pl.ds(pl.multiple_of(g * CG, 16), CG), :])
        return carry

    lax.fori_loop(0, xq.shape[0] // CG, body, 0)


def conv_finish(seg_ref, b_ref, spread, ot, low_ref, slope_ref, cols):
    hi, lo = split_low(ot[cols, :])
    pre = dg(spread[...], hi, NT) + dg(spread[...], lo, NT) + b_ref[:, cols]
    valid = (seg_ref[...] != 0).astype(F32)
    value, slope = gelu_and_slope(pre)
    low_ref[:, cols] = (valid * value).astype(BF16)
    slope_ref[:, cols] = valid * slope


def conv_fwd_kernel(seg_ref, x_ref, w_ref, b_ref, low_ref, slope_ref, xq, spread, patches, ot):
    conv_prepare(seg_ref, x_ref, spread, xq, patches)
    for plane in range(w_ref.shape[0]):
        conv_plane(w_ref.at[plane], patches, ot, plane, plane == 0)
    conv_finish(seg_ref, b_ref, spread, ot, low_ref, slope_ref, slice(0, x_ref.shape[1]))


def conv_bwd_kernel(seg_ref, xq, w_ref, slope_ref, gm_ref, mask_ref, dw_ref, in_ref, db_ref, dm_ref,
                    spread, dq, d_ref, gq, ready=nothing, beside=nothing, store=None, summed=nothing, between=nothing):
    length, width = spread.shape
    blocks = KW // TAPS
    groups = xq.shape[0] // CG
    spread[...] = spread_matrix(seg_ref[...], length, width)
    dpre = (slope_ref[...] * gm_ref[...].astype(F32)).astype(BF16)
    db_ref[...] = jnp.sum(dpre.astype(F32), axis=0, keepdims=True)
    masked = mask_ref[...].astype(F32)
    ready()
    mask_cols = dg(jnp.broadcast_to(masked, (length, 128)).astype(BF16), spread[...], TN)[0:1, :]
    dq[...] = dg(dpre, spread[...], TN).astype(BF16)
    place = lambda g: pl.ds(pl.multiple_of(g * CG, 16), CG)

    def shifts(g):
        dqg = dq[place(g), :]
        for b in range(blocks):
            d_ref[b * CG:(b + 1) * CG, :] = rolled(dqg, 64 - TAPS * b)
        return d_ref[...]

    def weight_body(g, carry):
        dw = dg(shifts(g), tap_patches(xq[place(g), :]), NT).astype(BF16).reshape(blocks, CG, TAPS * CG)
        if store is None:
            dw_ref[:, place(g), :] = dw
        else:
            store(g, dw)
        beside(g)
        return carry

    def input_body(g, carry):
        v = dg(block_rows(w_ref, place(g)), shifts(g), TN)
        acc = v[0:CG, :]
        for r in range(1, TAPS):
            acc = acc + rolled(v[r * CG:(r + 1) * CG, :], -r)
        gq[place(g), :] = acc
        beside(groups + g)
        return carry

    lax.fori_loop(0, groups, weight_body, 0)
    lax.fori_loop(0, groups, input_body, 0)
    of_taps = jnp.sum(gq[...] * mask_cols, axis=1, keepdims=True)
    dm_ref[...] = jnp.broadcast_to(of_taps, (of_taps.shape[0], 128)).T[0:1, :] + jnp.sum(masked * gm_ref[...].astype(F32), axis=0, keepdims=True)
    summed()
    hi, lo = split_low(gq[...])
    grad = dg(spread[...], hi, NT) + gm_ref[...].astype(F32)
    between()
    in_ref[...] = (1.0 - masked) * (grad + dg(spread[...], lo, NT))


class Place:
    def __init__(self):
        self.dp, self.y = lax.axis_index("dp"), lax.axis_index("mp")
        self.z, self.x, self.core = self.dp // 4, lax.rem(self.dp // 2, 2), lax.rem(self.dp, 2)

    def at(self, z=None, x=None, core=None, y=None):
        pick = lambda new, old: old if new is None else new
        dp = pick(z, self.z) * 4 + pick(x, self.x) * 2 + pick(core, self.core)
        return {"dp": dp, "mp": pick(y, self.y)}


def push(src, dst, sems, index, device):
    send, recv = sems if isinstance(sems, tuple) else (sems.at[0], sems.at[1])
    return pltpu.make_async_remote_copy(
        src_ref=src, dst_ref=dst, send_sem=send.at[index], recv_sem=recv.at[index],
        device_id=device, device_id_type=pl.DeviceIdType.MESH)


def meet(devices):
    here = pltpu.get_barrier_semaphore()
    for device in devices:
        pl.semaphore_signal(here, inc=1, device_id=device, device_id_type=pl.DeviceIdType.MESH)
    pl.semaphore_wait(here, len(devices))


def partners(p):
    return [p.at(z=lax.rem(p.z + o, 4)) for o in (1, 2, 3)] + [p.at(x=1 - p.x), p.at(core=1 - p.core), p.at(y=1 - p.y)]


def meet_all(p):
    crooked = p.core != p.y
    pl.when(crooked)(lambda: meet(partners(p) + [p.at(core=p.y, y=p.core)]))
    pl.when(jnp.logical_not(crooked))(lambda: meet(partners(p)))


class LineGather:
    UP, DOWN, ACROSS, LAST = range(4)

    def __init__(self, place, own, buf, send, recv, k, third, x_first=True):
        p = self.p = place
        self.own, self.buf, self.send, self.recv, self.k, self.x_first = own, buf, send, recv, k, x_first
        self.t = p.core if third == "core" else p.y
        over_x, over_t = p.at(x=1 - p.x), p.at(**{third: 1 - self.t})
        self.to = [p.at(z=jnp.minimum(p.z + 1, 3)), p.at(z=jnp.maximum(p.z - 1, 0))] + ([over_x, over_t] if x_first else [over_t, over_x])

    def slot(self, z, across=False, last=False):
        flip = lambda v, yes: 1 - v if yes else v
        x, t = (across, last) if self.x_first else (last, across)
        return (z, flip(self.p.x, x), flip(self.t, t))

    def copy(self, way, slot, src=None):
        at = (self.k,) + slot
        return pltpu.make_async_remote_copy(
            src_ref=self.buf.at[slot] if src is None else src, dst_ref=self.buf.at[slot], send_sem=self.send.at[(way,) + at],
            recv_sem=self.recv.at[at], device_id=self.to[way], device_id_type=pl.DeviceIdType.MESH)

    def walk(self, d, start, finish):
        p = self.p
        if d == 0:
            mine = self.slot(p.z)
            pl.when(p.z < 3)(lambda: start(self.UP, mine, True))
            pl.when(p.z > 0)(lambda: start(self.DOWN, mine, True))
            start(self.ACROSS, mine, True)
            start(self.LAST, mine, True)
            return

        def passing(z, way, further):
            slot = self.slot(z)
            finish(slot)
            pl.when(further)(lambda: start(way, slot, False))
            start(self.ACROSS, slot, False)
            start(self.LAST, slot, False)

        def crossed(z):
            slot = self.slot(z, across=True)
            finish(slot)
            start(self.LAST, slot, False)

        if d < 4:
            pl.when(p.z >= d)(lambda: passing(p.z - d, self.UP, p.z < 3))
            pl.when(p.z + d <= 3)(lambda: passing(p.z + d, self.DOWN, p.z > 0))
        if d == 1:
            crossed(p.z)
        else:
            pl.when(p.z >= d - 1)(lambda: crossed(p.z - d + 1))
            pl.when(p.z + d - 1 <= 3)(lambda: crossed(p.z + d - 1))

    def begin(self, way, slot, own):
        self.copy(way, slot, self.own if own else None).start()

    def round(self, d):
        self.walk(d, self.begin, lambda slot: self.copy(0, slot).wait_recv())

    def drain(self):
        for z in range(4):
            for across in (False, True):
                self.copy(0, self.slot(z, across, True)).wait_recv()
        self.sent()

    def sent(self):
        for d in range(5):
            self.walk(d, lambda way, slot, own: self.copy(way, slot, self.own if own else None).wait_send(), nothing)


class Fold:
    def __init__(self, kind, place, grad, sems, k, first, across, out1, cur, mid, last, out):
        self.kind, self.p, self.d, self.first, self.across, self.out1 = kind, place, grad, first, across, out1
        self.cur, self.mid, self.last, self.out = cur, mid, last, out
        p = place
        self.straight = p.core == p.y
        copy = lambda src, dst, n, dev: push(src, dst, sems, (k, n), dev)
        home, partner, sibling = p.at(y=p.core), p.at(x=1 - p.x), p.at(core=1 - p.core)
        away = grad.at[:, 1 - p.x]
        if kind == 0:
            self.over_y = copy(grad, first, 0, home)
            self.to_sibling = copy(out1, cur, 1, sibling)
            self.over_x = copy(cur.at[:, 1 - p.x], across, 2, partner)
        else:
            self.over_x = copy(away, across, 2, partner)
            self.over_y = copy(mid, first, 0, home)
            self.to_sibling = copy(out1, cur, 1, sibling)
        held = mid if kind == 0 else cur
        self.along = [copy(held.at[lax.rem(p.z + o, 4)], last.at[o - 1], 2 + o, p.at(z=lax.rem(p.z + o, 4))) for o in (1, 2, 3)]
        self.held = held

    def one_way(self, copy, sends, wait):
        pl.when(sends)(copy.wait_send if wait else copy.start)
        if wait:
            pl.when(jnp.logical_not(sends))(copy.wait_recv)

    def start(self, n):
        p, wide = self.p, lambda ref: ref.astype(F32)
        crooked = jnp.logical_not(self.straight)
        if n == 0:
            if self.kind == 0:
                self.one_way(self.over_y, crooked, False)
            else:
                self.over_x.start()
        elif n == 1:
            if self.kind == 0:
                @pl.when(self.straight)
                def _():
                    for z in range(4):
                        for x in range(2):
                            self.cur[z, x] = (wide(self.d[z, x, p.core]) + wide(self.first[z, x, p.core])).astype(BF16)
                            self.out1[z, x] = (wide(self.d[z, x, 1 - p.core]) + wide(self.first[z, x, 1 - p.core])).astype(BF16)
                    self.to_sibling.start()
            else:
                for z in range(4):
                    for c in range(2):
                        self.mid[z, c] = (wide(self.d[z, p.x, c]) + wide(self.across[z, c])).astype(BF16)
                self.one_way(self.over_y, crooked, False)
        elif n == 2:
            if self.kind == 0:
                self.over_x.start()
            else:
                @pl.when(self.straight)
                def _():
                    for z in range(4):
                        self.cur[z] = (wide(self.mid[z, p.core]) + wide(self.first[z, p.core])).astype(BF16)
                        self.out1[z] = (wide(self.mid[z, 1 - p.core]) + wide(self.first[z, 1 - p.core])).astype(BF16)
                    self.to_sibling.start()
        elif n == 3:
            if self.kind == 0:
                for z in range(4):
                    self.mid[z] = (wide(self.cur[z, p.x]) + wide(self.across[z])).astype(BF16)
            for c in self.along:
                c.start()
        else:
            self.out[...] = wide(self.held[p.z]) + wide(self.last[0]) + wide(self.last[1]) + wide(self.last[2])

    def wait(self, n):
        crooked = jnp.logical_not(self.straight)
        if n == 3:
            for c in self.along:
                c.wait()
        elif (self.kind, n) in ((0, 0), (1, 1)):
            self.one_way(self.over_y, crooked, True)
        elif (self.kind, n) in ((0, 1), (1, 2)):
            self.one_way(self.to_sibling, self.straight, True)
        else:
            self.over_x.wait()


def fold_scratch(kind, n):
    wide = (4, 2, 48, n)
    if kind == 0:
        shapes = ((4, 2, 2, 48, n), (4, 48, n), wide, wide, (4, 48, n), (3, 48, n))
    else:
        shapes = (wide, wide, (4, 48, n), (4, 48, n), wide, (3, 48, n))
    return [(s, BF16) for s in shapes]


def columns(rows_ref):
    return rows_ref[...].astype(F32).T


VECS = dict(embed=(0, 6), out_bias=(6, 6), gain1=(12, 6), shift1=(18, 6), down_bias=(24, 6), gain2=(30, 6), shift2=(36, 6),
            query_bias=(42, 3), value_bias=(45, 3), up_bias=(48, 12), conv_bias=(60, 3))


def lay_out(rows_ref, block_ref, *names):
    for k, name in enumerate(names):
        start, count = VECS[name]
        for j in range(count):
            rows_ref[k:k + 1, j * 128:(j + 1) * 128] = block_ref[start + j:start + j + 1, :]
    return [rows_ref.at[k:k + 1, 0:VECS[name][1] * 128] for k, name in enumerate(names)]


class Flow:
    def __init__(self, sems, *pairs):
        self.copies = [pltpu.make_async_copy(a, b, sems.at[k]) for k, (a, b) in enumerate(pairs)]

    def start(self, *which):
        for k in which or range(len(self.copies)):
            self.copies[k].start()

    def wait(self, *which):
        for k in which or range(len(self.copies)):
            self.copies[k].wait()


def transposed(x):
    a = x.shape[0]
    x = x.astype(F32)
    pad = -a % 128
    if pad:
        x = jnp.concatenate([x, jnp.zeros((pad, x.shape[1]), F32)], axis=0)
    return x.T[:, :a]


def conv_gather_kernel(*refs):
    vectors, refs = refs[:len(VECS)], refs[len(VECS):]
    (seg_row, mask_row, hid_ref, cot_ref, conv_ref, q_ref, k_ref, v_ref, o_ref, up_ref, dn_ref,
     xq, slope_ref, conv_t, hid_s, cot_s, small_s, vecs_t, own_late, w_out, wqk, wvo,
     spread, patches, ot, low, w_ref, shard, staged, own_t, seg, x_ref, small_ref, rows_ref, vecs_ref,
     local, turn, send_c, recv_c, send_w, recv_w) = refs
    p = Place()
    straight = p.core == p.y
    crooked = jnp.logical_not(straight)
    half, n = x_ref.shape[1], staged.shape[2]
    shard[...] = conv_ref[...].T
    meet_all(p)
    conv = LineGather(p, shard, w_ref, send_c, recv_c, 0, "core")
    conv.round(0)
    vecs_ref[...] = jnp.zeros_like(vecs_ref)
    for ref, (start, count) in zip(vectors, VECS.values()):
        line = ref[...].astype(F32).reshape(1, count * 128)
        for j in range(count):
            vecs_ref[start + j:start + j + 1, :] = line[:, j * 128:(j + 1) * 128]
    small_ref[...] = jnp.zeros_like(small_ref)
    small_ref[0:1, :] = seg_row[...]
    small_ref[1:2, :] = mask_row[...]
    w_ref[p.z, p.x, p.core] = shard[...]
    save_w = pltpu.make_async_copy(w_ref, w_out, local.at[0])
    walls = (wqk, wvo)
    lines = [LineGather(p, own_t.at[k], walls[k], send_w, recv_w, k, "y", k == 0) for k in range(2)]
    keep = [pltpu.make_async_copy(own_t.at[k], walls[k].at[p.z, p.x, p.y], local.at[1 + k]) for k in range(2)]
    twin = p.at(core=p.y, y=p.core)
    turned = [push(staged.at[0:2], own_t, turn, (0,), twin), push(staged.at[2:6], own_late, turn, (1,), twin), push(vecs_ref, vecs_t, turn, (2,), twin)]
    pairs = ((hid_ref, hid_s), (cot_ref, cot_s), (small_ref, small_s))
    keep_rows = [pltpu.make_async_copy(a, b, local.at[3 + k]) for k, (a, b) in enumerate(pairs)]
    push_rows = [push(a, b, turn, (3 + k,), p.at(core=1 - p.core)) for k, (a, b) in enumerate(pairs)]

    staged[0, :, :half] = q_ref[...]
    staged[0, :, half:] = k_ref[...]
    staged[1, :, :half] = v_ref[...]
    staged[1, :, half:] = o_ref[...]
    staged[2] = up_ref[:, :n]
    staged[3] = up_ref[:, n:]
    staged[4] = dn_ref[:, :n]
    staged[5] = dn_ref[:, n:]

    @pl.when(straight)
    def _():
        own_t[...] = staged[0:2]
        own_late[...] = staged[2:6]
        vecs_t[...] = vecs_ref[...]
        for c in keep_rows + push_rows:
            c.start()

    @pl.when(crooked)
    def _():
        for c in turned:
            c.start()

    cols = columns(small_ref)
    seg[...] = cols[:, 0:1].astype(jnp.int32)
    mine = pl.ds(pl.multiple_of(p.y * half, 128), half)
    hid = hid_ref[:, mine].astype(F32)
    embed, conv_bias = lay_out(rows_ref, vecs_ref, "embed", "conv_bias")
    x_ref[...] = (hid + cols[:, 1:2] * (rows_ref[0:1, mine] - hid)).astype(BF16)
    conv_prepare(seg, x_ref, spread, xq, patches)

    @pl.when(crooked)
    def _():
        for c in turned:
            c.wait()

    for c in keep:
        c.start()

    def nearest(n):
        pick = lambda *v: jnp.where(p.z == 0, v[0], jnp.where(p.z == 1, v[1], jnp.where(p.z == 2, v[2], v[3])))
        return (p.z, pick(1, 0, 1, 2), pick(2, 2, 3, 1), pick(3, 3, 0, 0))[n]

    def compute(n):
        z = nearest(n)
        for across in (False, True):
            conv.copy(0, conv.slot(z, across, True)).wait_recv()
        conv_plane(w_ref.at[z], patches, ot, z, n == 0)

    conv.round(1)
    compute(0)
    conv.round(2)
    for g in lines:
        g.round(0)
    compute(1)
    conv.round(3)
    for g in lines:
        g.round(1)
    compute(2)
    conv.round(4)
    for g in lines:
        g.round(2)
    compute(3)
    conv.sent()
    save_w.start()
    for g in lines:
        g.round(3)
    tile = 128
    turn_conv = [push(low.at[:, j * tile:(j + 1) * tile], conv_t.at[:, j * tile:(j + 1) * tile], turn, (6 + j,), twin) for j in range(half // tile)]
    for j in range(half // tile):
        conv_finish(seg, conv_bias, spread, ot, low, slope_ref, slice(j * tile, (j + 1) * tile))
        pl.when(crooked)(turn_conv[j].start)
        if j == 0:
            for g in lines:
                g.round(4)

    @pl.when(straight)
    def _():
        conv_t[...] = low[...]
        for c in keep_rows:
            c.wait()
        for c in push_rows:
            c.wait_send()

    @pl.when(crooked)
    def _():
        for c in push_rows:
            c.wait_recv()

    for g in lines:
        g.drain()
    for c in keep:
        c.wait()
    save_w.wait()

    @pl.when(crooked)
    def _():
        for c in turn_conv:
            c.wait()


def attn_gather_kernel(*refs):
    (hid_ref, conv_t, small_ref, vecs_ref, wqk_ref, wvo_ref, own_t,
     mixed_out, mlow_out, qkv_out, ctx_ref, lse_ref, part_ref, stat_ref, other_ref, wul, wur,
     qt, vt, ot, both, segc, mask, rows_ref, mixed_ref, mlow_ref, qkv_ref, local, flow, turn, send_w, recv_w, send_p, recv_p) = refs
    p = Place()
    half = conv_t.shape[1]
    sibling = p.at(core=1 - p.core)
    meet(partners(p))
    walls = (wul, wur)
    lines = [LineGather(p, own_t.at[k], walls[k], send_w, recv_w, k, "y", k == 0) for k in range(2)]
    keep = [pltpu.make_async_copy(own_t.at[k], walls[k].at[p.z, p.x, p.y], local.at[k]) for k in range(2)]
    give = push(conv_t, both.at[p.core], turn, (0,), sibling)
    give.start()
    for c in keep:
        c.start()
    for g in lines:
        g.round(0)
    embed, query_bias, value_bias = lay_out(rows_ref, vecs_ref, "embed", "query_bias", "value_bias")
    save = Flow(flow, (mixed_ref, mixed_out), (mlow_ref, mlow_out), (qkv_ref, qkv_out))
    both[p.core] = conv_t[...]
    cols = columns(small_ref)
    segc[...] = cols[:, 0:1].astype(jnp.int32)
    mask[...] = cols[:, 1:2].astype(jnp.int32)
    give.wait()

    def rounds(d):
        for g in lines:
            g.round(d)

    def beside(n):
        if isinstance(n, int):
            if n in (-3, -1):
                rounds((n + 5) // 2)
            if n == -1:
                save.start()
        else:
            for at in (0, 1):
                pl.when(n == at)(functools.partial(rounds, 3 + at))

    def sent(i, at):
        c = push(part_ref.at[at], other_ref.at[at], (send_p, recv_p), (i,), sibling)
        c.start()
        return c

    copies = attn_fwd_kernel(hid_ref, both.at[0], both.at[1], mask, segc, small_ref.at[0:1], embed, (wqk_ref, wvo_ref), query_bias, value_bias,
                             mixed_ref, mlow_ref, qkv_ref, ctx_ref, lse_ref, part_ref, stat_ref, qt, vt, ot, beside, sent)
    for g in lines:
        g.drain()
    for c in keep + copies:
        c.wait()
    save.wait()


def attn_fwd_kernel(hid_ref, c0_ref, c1_ref, mask_ref, segc_ref, segr_ref, emb_ref, w_refs, qb_ref, vb_ref,
                    mixed_ref, mlow_ref, qkv_ref, ctx_ref, lse_ref, part_ref, stat_ref, qt, vt, ot, beside=nothing, sent=nothing):
    wqk_ref, wvo_ref = w_refs
    rows, width = hid_ref.shape
    half = c0_ref.shape[1]
    heads = half // HD
    step = 256
    stat = jnp.zeros((1, half), F32)
    for i in range(rows // step):
        at = pl.ds(i * step, step)
        conv = jnp.concatenate([c0_ref[at, :].astype(F32), c1_ref[at, :].astype(F32)], axis=1)
        hid = hid_ref[at, :].astype(F32)
        masked = mask_ref[at, :].astype(F32)
        mixed = hid + masked * (emb_ref[...] - hid) + conv
        low = mixed.astype(BF16)
        mixed_ref[at, :] = mixed
        mlow_ref[at, :] = low
        stat = stat + jnp.sum(conv[:, :half] * conv[:, :half] + conv[:, half:] * conv[:, half:], axis=0, keepdims=True)
        qk = dg(low, wqk_ref[...], NN)
        qkv_ref[at, 0:half] = (qk[:, :half] + qb_ref[...]).astype(BF16)
        qkv_ref[at, half:2 * half] = qk[:, half:].astype(BF16)
        qkv_ref[at, 2 * half:] = (dg(low, wvo_ref[:, :half], NN) + vb_ref[...]).astype(BF16)
        beside(i - 4)
    stat_ref[...] = stat
    qt[...] = (qkv_ref[:, 0:half] * jnp.asarray(HD ** -0.5, BF16)).T
    vt[...] = qkv_ref[:, 2 * half:].T

    def pair_body(p, carry):
        beside(p)
        lanes = pl.ds(pl.multiple_of(half + p * 128, 128), 128)
        k_pair = qkv_ref[:, lanes]
        for j in range(2):
            head_at = pl.ds(pl.multiple_of(p * 128 + j * HD, HD), HD)
            qh = qt[head_at, :]
            vh = vt[head_at, :]
            zero = jnp.zeros_like(qh)
            qz = jnp.concatenate([qh, zero] if j == 0 else [zero, qh], axis=0)
            for i in range(rows // step):
                at = slice(i * step, (i + 1) * step)
                s = dg(k_pair, qz[:, at], NN)
                s = jnp.where(segc_ref[...] == segr_ref[:, at], s, -1000000000.0)
                top = jnp.max(s, axis=0, keepdims=True)
                e = jnp.exp(s - top)
                den = jnp.sum(e, axis=0, keepdims=True)
                o = dg(vh, e.astype(BF16), NN) / den
                ot[head_at, at] = jnp.where(segr_ref[:, at] != 0, o, 0.0).astype(BF16)
                lse_ref[pl.ds(2 * p + j, 1), at] = top + jnp.log(den)
        return carry

    lax.fori_loop(0, heads // 2, pair_body, 0)
    ctx_ref[...] = ot[...].T
    copies = []
    for i in range(rows // step):
        at = pl.ds(i * step, step)
        part_ref[at, :] = dg(ctx_ref[at, :], wvo_ref[:, half:], NT).astype(BF16)
        copies.append(sent(i, at))
    return copies


def norm_stats(x):
    centre = x - jnp.mean(x, axis=-1, keepdims=True)
    r = lax.rsqrt(jnp.mean(centre * centre, axis=-1, keepdims=True) + EPS)
    return centre * r, r


def matrix(ref):
    w = ref[...]
    return w if len(w.shape) == 2 else w.reshape(-1, w.shape[-1])


def ffn_fwd_kernel(mixed_ref, p0_ref, p1_ref, seg_ref, ob_ref, g1_ref, s1_ref, ul_ref, ur_ref, ub_ref, dl_ref, dr_ref,
                   n1_ref, r1_ref, low_ref, hid_ref, slope_ref, part_ref, stat_ref, beside=nothing, before_down=nothing, sent=nothing):
    rows, width = mixed_ref.shape
    ff = ul_ref.shape[-1]
    step = 256
    stat_ref[...] = jnp.zeros_like(stat_ref)

    def up_body(i, carry):
        at = pl.ds(pl.multiple_of(i * step, step), step)
        attn = ob_ref[...] + (p0_ref[at, :].astype(F32) + p1_ref[at, :].astype(F32))
        valid = (seg_ref[at, :] != 0).astype(F32)
        stat_ref[...] += jnp.sum(valid * attn * attn, axis=0, keepdims=True)
        n1, r1 = norm_stats(mixed_ref[at, :] + attn)
        n1_ref[at, :] = n1
        r1_ref[at, :] = r1
        low = (n1 * g1_ref[...] + s1_ref[...]).astype(BF16)
        low_ref[at, :] = low
        for k, up in enumerate((ul_ref, ur_ref)):
            cols = slice(k * ff, (k + 1) * ff)
            value, slope = gelu_and_slope(dg(low, matrix(up), NN) + ub_ref[:, cols])
            hid_ref[at, cols] = value.astype(BF16)
            slope_ref[at, cols] = slope.astype(BF16)
        beside(i)
        return carry

    def down_body(i, carry):
        at = pl.ds(pl.multiple_of(i * step, step), step)
        part_ref[at, :] = (dg(hid_ref[at, :ff], matrix(dl_ref), NT) + dg(hid_ref[at, ff:], matrix(dr_ref), NT)).astype(BF16)
        sent(i, at)
        return carry

    lax.fori_loop(0, rows // step, up_body, 0)
    before_down()
    lax.fori_loop(0, rows // step, down_body, 0)


class Give:
    def __init__(self, place, part, other, sems):
        self.make = lambda i, at: push(part.at[at], other.at[at], sems, (i,), place.at(core=1 - place.core))

    def __call__(self, i, at):
        self.make(i, at).start()

    def arrived(self, i, at):
        self.make(i, at).wait()

    def wait(self, parts, step):
        for i in range(parts):
            self.make(i, pl.ds(i * step, step)).wait()


def norm_back(gn, n, r):
    return r * (gn - jnp.mean(gn, axis=-1, keepdims=True) - n * jnp.mean(gn * n, axis=-1, keepdims=True))


def ffn_bwd_kernel(n1_ref, g1_ref, s1_ref, p0_ref, p1_ref, seg_ref, db_ref, g2_ref, s2_ref, cot_ref, low_ref,
                   hid_ref, slope_ref, ul_ref, ur_ref, dl_ref, dr_ref,
                   out_ref, gr2_ref, part_ref, ddl_ref, ddr_ref, dul_ref, dur_ref, sums_ref, dub_ref, fg, hg,
                   here=nothing, down_done=nothing, sent=nothing):
    rows, width = n1_ref.shape
    ff = ul_ref.shape[-1]
    step = 256
    sums_ref[...] = jnp.zeros_like(sums_ref)
    dub_ref[...] = jnp.zeros_like(dub_ref)
    row_sum = lambda v: jnp.sum(v, axis=0, keepdims=True)
    store = lambda ref, v: ref.__setitem__(Ellipsis, v.astype(ref.dtype).reshape(ref.shape))

    def norm_body(i, carry):
        at = pl.ds(pl.multiple_of(i * step, step), step)
        here(i, at)
        ffn = db_ref[...] + (p0_ref[at, :].astype(F32) + p1_ref[at, :].astype(F32))
        valid = (seg_ref[at, :] != 0).astype(F32)
        n2, r2 = norm_stats(n1_ref[at, :] * g1_ref[...] + s1_ref[...] + ffn)
        final = valid * (n2 * g2_ref[...] + s2_ref[...])
        out_ref[at, :] = final.astype(BF16)
        gf = valid * cot_ref[at, :].astype(F32)
        gr2 = norm_back(gf * g2_ref[...], n2, r2)
        gr2_ref[at, :] = gr2
        ffn_grad = gr2.astype(BF16)
        fg[at, :] = ffn_grad
        sums_ref[...] += jnp.concatenate(
            [row_sum(valid * ffn * ffn), row_sum(final * final), row_sum(gf * n2), row_sum(gf), row_sum(ffn_grad.astype(F32))], axis=0)
        return carry

    lax.fori_loop(0, rows // step, norm_body, 0)
    store(ddl_ref, dg(fg[...], hid_ref[:, :ff], TN))
    store(ddr_ref, dg(fg[...], hid_ref[:, ff:], TN))
    down_done()

    def body(i, carry):
        at = pl.ds(pl.multiple_of(i * step, step), step)
        part = 0.0
        for k, (up, down) in enumerate(((ul_ref, dl_ref), (ur_ref, dr_ref))):
            cols = slice(k * ff, (k + 1) * ff)
            hidden_grad = (slope_ref[at, cols].astype(F32) * dg(fg[at, :], matrix(down), NN)).astype(BF16)
            hg[at, cols] = hidden_grad
            dub_ref[:, cols] += row_sum(hidden_grad.astype(F32))
            part = part + dg(hidden_grad, matrix(up), NT)
        part_ref[at, :] = part.astype(BF16)
        sent(i, at)
        return carry

    lax.fori_loop(0, rows // step, body, 0)
    store(dul_ref, dg(low_ref[...], hg[:, :ff], TN))
    store(dur_ref, dg(low_ref[...], hg[:, ff:], TN))


def ffn_kernel(*refs):
    mixed, part1, other1, small, vecs, cot_in, wul_in, wur_in, own_t = refs[:9]
    (n1_out, r1, stat, show_out, gr2_out, part3, ddl_out, ddr_out, dul, dur, sums, dub, other3, first_l, across_r) = refs[9:24]
    (low, hid, slope, part2, other2, fg, hg, seg, wdl, wdr, rows_ref, n1, out_ref, gr2, ddl, ddr, cot, wul, wur) = refs[24:43]
    sem_2, sem_3, sem_f, send_w, recv_w, flow_in, flow_out = refs[43:]
    p = Place()
    straight = p.core == p.y
    crooked = jnp.logical_not(straight)
    load = Flow(flow_in, (wul_in, wul), (wur_in, wur), (cot_in, cot))
    load.start()
    save = Flow(flow_out, (n1, n1_out), (out_ref, show_out), (gr2, gr2_out), (ddl, ddl_out), (ddr, ddr_out))
    meet(partners(p))
    lines = [LineGather(p, own_t.at[2 + k], w, send_w, recv_w, k, "y", k == 0) for k, w in enumerate((wdl, wdr))]
    for k, g in enumerate(lines):
        g.round(0)
        g.buf[p.z, p.x, p.y] = own_t[2 + k]
    seg[...] = columns(small)[:, 0:1].astype(jnp.int32)
    ob, g1, s1, db, g2, s2, ub = lay_out(rows_ref, vecs, "out_bias", "gain1", "shift1", "down_bias", "gain2", "shift2", "up_bias")
    give2, give3 = Give(p, part2, other2, sem_2), Give(p, part3, other3, sem_3)
    over_y = push(ddl, first_l, sem_f, (0,), p.at(y=p.core))
    over_x = push(ddr.at[:, 1 - p.x], across_r, sem_f, (1,), p.at(x=1 - p.x))
    load.wait(0, 1)

    def beside(i):
        for n in range(4):
            @pl.when(i == n)
            def _(n=n):
                for g in lines:
                    g.round(n + 1)

    def before_down():
        save.start(0)
        load.wait(2)
        for g in lines:
            g.drain()

    def down_done():
        pl.when(crooked)(over_y.start)
        over_x.start()
        save.start(1, 2, 3, 4)

    ffn_fwd_kernel(mixed, part1, other1, seg, ob, g1, s1, wul, wur, ub, wdl, wdr,
                   n1, r1, low, hid, slope, part2, stat, beside, before_down, give2)
    ffn_bwd_kernel(n1, g1, s1, part2, other2, seg, db, g2, s2, cot, low, hid, slope, wul, wur, wdl, wdr,
                   out_ref, gr2, part3, ddl, ddr, dul, dur, sums, dub, fg, hg, give2.arrived, down_done, give3)
    give3.wait(4, 256)
    over_x.wait()
    pl.when(straight)(over_y.wait_recv)
    pl.when(crooked)(over_y.wait_send)
    save.wait()


def attn_bwd_kernel(gr2_ref, p0_ref, p1_ref, n1_ref, r1_ref, g1_ref, segc_ref, segr_ref, ctx_ref, qkv_ref, lse_ref,
                    mlow_ref, wqk_ref, wvo_ref,
                    dqk_ref, dvo_ref, sums_ref, dqkvb_ref, gr1, cg, qt, kt, ct, dqt, dk, dv, gqkv, finish, beside=nothing, normed=nothing):
    rows, width = gr2_ref.shape
    half = ctx_ref.shape[1]
    heads = half // HD
    step = 256
    core = lax.rem(lax.axis_index("dp"), 2)
    sums_ref[...] = jnp.zeros_like(sums_ref)
    row_sum = lambda v: jnp.sum(v, axis=0, keepdims=True)

    def norm_body(i, carry):
        at = pl.ds(pl.multiple_of(i * step, step), step)
        gn1 = gr2_ref[at, :] + (p0_ref[at, :].astype(F32) + p1_ref[at, :].astype(F32))
        n1 = n1_ref[at, :]
        g = norm_back(gn1 * g1_ref[...], n1, r1_ref[at, :])
        gr1[at, :] = g
        attn_grad = g.astype(BF16)
        sums_ref[...] += jnp.concatenate([row_sum(gn1 * n1), row_sum(gn1), row_sum(attn_grad.astype(F32))], axis=0)
        back = dg(attn_grad, wvo_ref[:, half:], NN)
        cg[at, :] = jnp.where(segc_ref[at, :] != 0, back, 0.0).astype(BF16)
        return carry

    lax.fori_loop(0, rows // step, norm_body, 0)
    normed()
    store = lambda ref, cols, v: ref.__setitem__((Ellipsis, cols), v.astype(BF16).reshape(ref.shape[:-1] + (v.shape[-1],)))
    store(dvo_ref, slice(half, 2 * half), dg(gr1[...].astype(BF16), ctx_ref[...], TN))
    scale = jnp.asarray(HD ** -0.5, BF16)
    qt[...] = (qkv_ref[:, 0:half] * scale).T
    kt[...] = qkv_ref[:, half:2 * half].T
    ct[...] = cg[...].T
    lane = lax.broadcasted_iota(jnp.int32, (1, 128), 1)

    def pair_body(p, carry):
        base = pl.multiple_of(p * 128, 128)
        k_at = pl.ds(pl.multiple_of(half + base, 128), 128)
        v_at = pl.ds(pl.multiple_of(2 * half + base, 128), 128)
        q_pair = qkv_ref[:, pl.ds(base, 128)] * scale
        o_pair = cg[:, pl.ds(base, 128)]
        dk[...] = jnp.zeros_like(dk)
        dv[...] = jnp.zeros_like(dv)
        for j in range(2):
            head_at = pl.ds(pl.multiple_of(base + j * HD, HD), HD)
            zero = jnp.zeros((HD, rows), BF16)
            put = lambda a: jnp.concatenate([a, zero] if j == 0 else [zero, a], axis=0)
            qz, cz, kh = put(qt[head_at, :]), put(ct[head_at, :]), kt[head_at, :]
            keep = (lane < HD) if j == 0 else (lane >= HD)
            for i in range(rows // step):
                at = slice(i * step, (i + 1) * step)
                s = dg(qkv_ref[:, k_at], qz[:, at], NN)
                pr = jnp.exp(s - lse_ref[pl.ds(2 * p + j, 1), at])
                pr = jnp.where(segc_ref[...] == segr_ref[:, at], pr, 0.0)
                gp = dg(qkv_ref[:, v_at], cz[:, at], NN)
                delta = jnp.sum(pr * gp, axis=0, keepdims=True)
                ds = (pr * (gp - delta)).astype(BF16)
                dv[...] += dg(pr.astype(BF16), jnp.where(keep, o_pair[at, :], jnp.zeros_like(o_pair[at, :])), NN)
                dk[...] += dg(ds, jnp.where(keep, q_pair[at, :], jnp.zeros_like(q_pair[at, :])), NN)
                dqt[head_at, at] = (dg(kh, ds, NN) * (HD ** -0.5)).astype(BF16)
                beside(p, j * (rows // step) + i)
        gqkv[:, k_at] = dk[...].astype(BF16)
        gqkv[:, v_at] = dv[...].astype(BF16)
        return carry

    lax.fori_loop(0, heads // 2, pair_body, 0)
    gqkv[:, 0:half] = dqt[...].T
    mine = pl.ds(pl.multiple_of(core * half, 128), half)
    other = pl.ds(pl.multiple_of((1 - core) * half, 128), half)
    to_mixed = lambda at: (dg(gqkv[:, :2 * half], wqk_ref[at, :], NT) + dg(gqkv[:, 2 * half:], wvo_ref[at, 0:half], NT))
    finish(lambda: to_mixed(other).astype(BF16), lambda: gr1[:, mine] + to_mixed(mine))
    dqkvb_ref[...] = row_sum(gqkv[...].astype(F32))
    dqk_ref[...] = dg(mlow_ref[...], gqkv[:, :2 * half], TN).astype(BF16).reshape(dqk_ref.shape)
    store(dvo_ref, slice(0, half), dg(mlow_ref[...], gqkv[:, 2 * half:], TN))


def attn_bwd_plain_kernel(*refs):
    ins, outs, scratch = refs[:14], refs[14:20], refs[20:]
    own_ref, send_ref = outs[:2]

    def finish(send, own):
        send_ref[...] = send()
        own_ref[...] = own()

    attn_bwd_kernel(*ins, *outs[2:], *scratch, finish)


def attn_bwd_fold_kernel(*refs):
    gr2, part3, other3, n1, r1, vecs, small, ctx_in, qkv_in, lse, mlow_in, wqk_in, wvo, ddl, ddr, dul_in, dur_in, first_l, across_r = refs[:19]
    outs, (gm_out, out_up, out_dn) = refs[19:23], refs[23:26]
    scratch, (segc, send, got, gm, out_dl, out_dr, rows_ref, ctx, qkv, mlow, wqk, dul, dur) = refs[26:35], refs[35:48]
    bufs, (sem_f, sem_g, flow) = refs[48:70], refs[70:]
    n = out_dl.shape[1]
    out_ul, out_ur = out_up.at[:, :n], out_up.at[:, n:]
    p = Place()
    load = Flow(flow, (dur_in, dur), (dul_in, dul), (ctx_in, ctx), (qkv_in, qkv), (mlow_in, mlow), (wqk_in, wqk))
    load.start()
    (g1,) = lay_out(rows_ref, vecs, "gain1")
    straight = p.core == p.y
    meet_all(p)
    segc[...] = columns(small)[:, 0:1].astype(jnp.int32)
    early = [Fold(0, p, ddl, sem_f, 0, first_l, *bufs[0:5], out_dl), Fold(1, p, ddr, sem_f, 1, bufs[5], across_r, *bufs[6:10], out_dr)]
    late = [Fold(0, p, dul, sem_f, 2, *bufs[10:16], out_ul), Fold(1, p, dur, sem_f, 3, *bufs[16:22], out_ur)]

    def step(folds, n, wait=True):
        for f in folds:
            if wait:
                f.wait(n - 1)
            f.start(n)

    step(early, 1, False)
    load.wait(0)
    late[1].start(0)

    def normed():
        load.wait(1, 2, 3, 4, 5)
        step(early, 2)
        late[0].start(0)

    def beside(pair, at):
        if at == 2:
            pl.when(pair == 1)(lambda: step(early, 3))
        if at == 6:
            pl.when(pair == 1)(lambda: step(late, 1))
        if at == 4:
            pl.when(pair == 2)(lambda: step(late, 2))
        if at == 7:
            @pl.when(pair == 2)
            def _():
                step(early, 4)
                out_dn[:, :n] = out_dl[...]
                out_dn[:, n:] = out_dr[...]

    to_sibling = push(send, got, sem_g, (0,), p.at(core=1 - p.core))
    turn = push(gm, gm_out, sem_g, (1,), p.at(core=p.y, y=p.core))

    def finish(give, own):
        send[...] = give()
        to_sibling.start()
        step(late, 3)
        mine = own()
        to_sibling.wait()
        value = (mine + got[...].astype(F32)).astype(BF16)

        @pl.when(straight)
        def _():
            gm_out[...] = value

        @pl.when(jnp.logical_not(straight))
        def _():
            gm[...] = value
            turn.start()

    attn_bwd_kernel(gr2, part3, other3, n1, r1, g1, segc, small.at[0:1], ctx, qkv, lse, mlow, wqk, wvo, *outs, *scratch, finish, beside, normed)
    step(late, 4)
    pl.when(jnp.logical_not(straight))(turn.wait)


class Total:
    def __init__(self, vec, got, sems, hops, p):
        self.vec, self.got, self.n = vec, got, len(hops)
        self.pair = [push(vec.at[n], got.at[n], sems, (n,), device) for n, device in enumerate(hops)]
        self.along = [push(vec.at[self.n], got.at[self.n + o - 1], sems, (self.n + o - 1,), p.at(z=lax.rem(p.z + o, 4))) for o in (1, 2, 3)]

    def step(self, n):
        if n > 0:
            self.pair[n - 1].wait()
            self.vec[n] = self.vec[n - 1] + self.got[n - 1]
        for c in self.along if n == self.n else [self.pair[n]]:
            c.start()

    def result(self):
        for c in self.along:
            c.wait()
        n = self.n
        return self.vec[n] + self.got[n] + self.got[n + 1] + self.got[n + 2]


def conv_fold_kernel(*refs):
    (seg_row, mask_row, xq, w_in, slope_ref, gm_ref, dqk, dvo, sums2, sums1, dqkvb, dub, stat_conv, stat_attn, shown,
     in_ref, dconv_ref, out_qk, out_vo, sums_out, me_out, layer_got, spread, dq, d_ref, gq) = refs[:26]
    seg_ref, mask_ref, small_ref, db_ref, dm_ref, d_all, got_c, sum_c, got_x, sum_x, got_z, vec, got_v, me, got_me, w_ref = refs[26:42]
    folds_bufs, (sem_c, sem_x, sem_z, sem_fold, sem_vec, sem_me, sem_out, flow) = refs[42:54], refs[54:]
    p = Place()
    straight = p.core == p.y
    crooked = jnp.logical_not(straight)
    load = Flow(flow, (w_in, w_ref))
    load.start()
    meet(partners(p))
    groups = 8
    wide = lambda v: v.astype(F32)
    folds = [Fold(FOLD_KINDS[0], p, dqk, sem_fold, 0, *folds_bufs[:6], out_qk), Fold(FOLD_KINDS[1], p, dvo, sem_fold, 1, *folds_bufs[6:], out_vo)]
    folds[0].start(0)
    show = push(shown, layer_got, sem_out, (0,), p.at(y=1 - p.y))
    small_ref[...] = jnp.zeros_like(small_ref)
    small_ref[0:1, :] = seg_row[...]
    small_ref[1:2, :] = mask_row[...]
    cols = columns(small_ref)
    seg_ref[...] = cols[:, 0:1].astype(jnp.int32)
    mask_ref[...] = cols[:, 1:2].astype(jnp.int32)
    hops = [p.at(core=1 - p.core), p.at(x=1 - p.x)]
    total = Total(vec, got_v, sem_vec, hops + [p.at(y=1 - p.y)], p)
    me_total = Total(me, got_me, sem_me, hops, p)
    width = vec.shape[2]
    half = width // 2
    of_half = lambda which: (lax.broadcasted_iota(jnp.int32, (1, width), 1) // half == which).astype(F32)
    twice = lambda v: jnp.concatenate([v, v], axis=1)

    def ready():
        by_core, by_y = of_half(p.core), of_half(p.y)
        is_core = lambda c: (p.core == c).astype(F32)
        frames = jnp.sum(wide(seg_ref[...] != 0), axis=0, keepdims=True)
        rows = [sums1[2:3] * by_core, sums1[0:1] * by_core, sums1[1:2] * by_core, sums2[4:5] * by_core, sums2[2:3] * by_core, sums2[3:4] * by_core,
                twice(db_ref[...]) * by_y, twice(dqkvb[:, :half]) * by_core, twice(dqkvb[:, 2 * half:]) * by_core,
                dub[:, :width] * is_core(0), dub[:, width:] * is_core(0), dub[:, :width] * is_core(1), dub[:, width:] * is_core(1),
                twice(stat_conv[...]) * by_core * 0.5, stat_attn[...] * by_core, sums2[0:1] * by_core, sums2[1:2] * by_core,
                jnp.broadcast_to(frames * 0.5, (1, width))]
        rows.append(jnp.zeros((24 - len(rows), width), F32))
        vec[0] = jnp.concatenate(rows, axis=0)
        total.step(0)

    def store(g, dw):
        d_all[g] = dw.reshape(d_all.shape[1:])

    to_c = lambda g: push(d_all.at[g, :, :, 1 - p.core], got_c.at[g], sem_c, (g,), p.at(core=1 - p.core))
    to_x = lambda g: push(sum_c.at[g, :, 1 - p.x], got_x.at[g], sem_x, (g,), p.at(x=1 - p.x))
    to_z = lambda g: [push(sum_x.at[g, lax.rem(p.z + o, 4)], got_z.at[g, o - 1], sem_z, (g, o - 1), p.at(z=lax.rem(p.z + o, 4)))
                      for o in (1, 2, 3)]

    def fold_step(k, n):
        if n > 0:
            folds[k].wait(n - 1)
        folds[k].start(n)

    def crossed(k):
        to_x(k).wait()
        for z in range(4):
            sum_x[k, z] = (wide(sum_c[k, z, p.x]) + wide(got_x[k, z])).astype(BF16)
        for c in to_z(k):
            c.start()

    def beside(t):
        @pl.when(t < groups)
        def _():
            to_c(t).start()

        @pl.when(jnp.logical_and(t >= 1, t <= groups))
        def _():
            k = t - 1
            to_c(k).wait()
            for z in range(4):
                for x in range(2):
                    sum_c[k, z, x] = (wide(d_all[k, z, x, p.core]) + wide(got_c[k, z, x])).astype(BF16)
            to_x(k).start()

        for k, at in enumerate(CROSS_AT):
            pl.when(t == at)(functools.partial(crossed, k))
        for k, n, at in FOLD_AT:
            pl.when(t == at)(functools.partial(fold_step, k, n))
        for n, at in zip((1, 2, 3), TOTAL_AT):
            pl.when(t == at)(functools.partial(total.step, n))
        pl.when(jnp.logical_and(t == SHOW_AT, straight))(show.start)
        pl.when(t == groups - 1)(load.wait)

    def summed():
        me[0] = jnp.broadcast_to(dm_ref[...], me.shape[1:])
        me_total.step(0)

    conv_bwd_kernel(seg_ref, xq, w_ref, slope_ref, gm_ref, mask_ref, None, in_ref, db_ref, dm_ref,
                    spread, dq, d_ref, gq, ready, beside, store, summed, lambda: me_total.step(1))
    me_total.step(2)
    if (1, 3) not in [at[:2] for at in FOLD_AT]:
        fold_step(1, 3)
    for k in range(len(CROSS_AT), groups):
        crossed(k)
    sums_out[...] = total.result()
    me_out[...] = me_total.result()
    for k in range(2):
        fold_step(k, 4)
    for k in range(groups):
        for c in to_z(k):
            c.wait()
        gq[k * CG:(k + 1) * CG, 0:TAPS * CG] = wide(sum_x[k, p.z]) + wide(got_z[k, 0]) + wide(got_z[k, 1]) + wide(got_z[k, 2])
    dconv_ref[...] = gq[:, 0:TAPS * CG].T
    pl.when(straight)(show.wait_send)
    pl.when(crooked)(show.wait_recv)


def result_kernel(*refs):
    (shown, layer_got, grad, dconv, oqk, ovo, dup, ddn, sums, me,
     layer_out, input_grad, mask_out, conv_out, convb_out, q_out, k_out, v_out, qb_out, vb_out, o_out, ob_out, g1_out, s1_out,
     up_out, ub_out, dn_out, db_out, g2_out, s2_out, rms_out, flow) = refs
    y = lax.axis_index("mp")
    straight = lax.rem(lax.axis_index("dp"), 2) == y
    move = Flow(flow, (grad, input_grad), (dconv, conv_out), (dup, up_out), (ddn, dn_out), (shown, layer_out))
    got = pltpu.make_async_copy(layer_got, layer_out, flow.at[5])
    move.start(0, 1, 2, 3)
    pl.when(straight)(lambda: move.start(4))
    pl.when(jnp.logical_not(straight))(got.start)
    half = q_out.shape[1]
    width = sums.shape[1]
    q_out[...] = oqk[:, :half]
    k_out[...] = oqk[:, half:]
    v_out[...] = ovo[:, :half]
    o_out[...] = ovo[:, half:]
    line = lambda ref, v: ref.__setitem__(Ellipsis, v.reshape(ref.shape))
    part = lambda k: jnp.where(y == 0, sums[k:k + 1, :half], sums[k:k + 1, half:])
    for k, ref in enumerate((ob_out, g1_out, s1_out, db_out, g2_out, s2_out)):
        line(ref, sums[k:k + 1, :])
    line(mask_out, me[0:1, :])
    for k, ref in ((6, convb_out), (7, qb_out), (8, vb_out)):
        line(ref, part(k))
    pair = lambda k: jnp.concatenate([sums[k:k + 1, :], sums[k + 1:k + 2, :]], axis=1)
    line(ub_out, jnp.where(y == 0, pair(9), pair(11)))
    power = lambda k: jnp.sum(sums[k:k + 1, :], axis=1, keepdims=True)
    rms = jnp.sqrt(jnp.concatenate([power(k) for k in (13, 14, 15, 16)], axis=1) / (sums[17:18, 0:1] * width))
    line(rms_out, rms)
    move.wait(0, 1, 2, 3)
    pl.when(straight)(lambda: move.wait(4))
    pl.when(jnp.logical_not(straight))(got.wait)


def one_row(v):
    return v.astype(F32)[None]


def flat_turn(n_all):
    return [(f, f // 4 * 4 + (f % 2) * 2 + (f // 2) % 2) for f in range(n_all)]


def shapes(rows, width, ff):
    half = width // 2
    heads = half // HD
    spread_width = -(-(rows + 7 * 64 + 64) // 128) * 128
    blocks = KW // TAPS
    low, wide = lambda *s: (s, BF16), lambda *s: (s, F32)
    return dict(
        half=half, spread_width=spread_width, blocks=blocks,
        attn_out=[wide(rows, width), low(rows, width), low(rows, 3 * half), low(rows, half), wide(heads, rows), low(rows, width)],
        attn_scratch=[low(half, rows)] * 3,
        ffn_out=[wide(rows, width), wide(rows, 1), low(rows, width), low(rows, ff), low(rows, ff), low(rows, width), wide(1, width)],
        back_scratch=[wide(rows, width), low(rows, half), low(half, rows), low(half, rows), low(half, rows), low(half, rows),
                      wide(rows, 128), wide(rows, 128), low(rows, 3 * half)],
    )


def local_close(hidden_in, segment_ids, time_mask, mask_embed, conv_weight, conv_bias, query_weight, key_weight,
                value_weight, query_bias, value_bias, out_weight, out_bias, first_gain, first_shift, up_weight, up_bias,
                down_weight, down_bias, second_gain, second_shift, cotangent):
    _, rows, width = hidden_in.shape
    ff = up_weight.shape[1]
    n = ff // 2
    sh = shapes(rows, width, ff)
    half, sw, blocks = sh["half"], sh["spread_width"], sh["blocks"]
    low, wide = lambda *s: (s, BF16), lambda *s: (s, F32)
    block = wide(64, 128)
    column = ((rows, 1), jnp.int32)
    eight = ((8, rows), jnp.int32)
    seats = (4, 2, 2)
    wall = [low(*seats, 48, n)]
    line_sems = ((4, 2) + seats, (2,) + seats)

    xq, slope, conv_t, hid_s, cot_s, small_s, vecs_t, own_late, conv_full, w_qk, w_vo = call(
        conv_gather_kernel,
        [low(half, sw), wide(rows, half), low(rows, half), low(rows, width), low(rows, width), eight, block, low(4, 48, n),
         low(*seats, half, TAPS * CG)] + wall * 2,
        [low(rows, sw), low(half // CG, TAPS * CG, sw), wide(half, sw), low(rows, half), low(*seats, half, TAPS * CG), low(half, TAPS * CG),
         low(6, 48, n), low(2, 48, n), column, low(rows, half), eight, wide(8, width), block],
        mask_embed, out_bias, first_gain, first_shift, down_bias, second_gain, second_shift, query_bias, value_bias, up_bias, conv_bias,
        segment_ids, time_mask, hidden_in[0], cotangent[0], conv_weight, query_weight, key_weight, value_weight, out_weight.T, up_weight,
        down_weight.T, hbm_out=(3, 4, 5, 8, 9, 10), sems=((6,), (2, 9), (4, 1) + seats, (1,) + seats) + line_sems, meeting=1)
    flat = lambda w: w.reshape(width, n)
    w_qk, w_vo = flat(w_qk), flat(w_vo)
    held = [wide(rows, width), low(rows, width), low(rows, 3 * half)]
    mixed, mlow, qkv, ctx, lse, part1, stat_conv, other1, w_ul, w_ur = call(
        attn_gather_kernel, sh["attn_out"] + [wide(1, half), low(rows, width)] + wall * 2,
        sh["attn_scratch"] + [low(2, rows, half), column, column, wide(8, width)] + held,
        hid_s, conv_t, small_s, vecs_t, w_qk, w_vo, own_late,
        hbm_out=(0, 1, 2, 8, 9), sems=((2,), (3,), (2, 1)) + line_sems + ((4,), (4,)), meeting=2)
    w_ul, w_ur = flat(w_ul), flat(w_ur)
    grad = low(*seats, 48, n)
    weight = low(width, n)
    n1, r1, stat_attn, out_s, gr2, part3, ddl, ddr, dul, dur, sums2, d_ub, other3, first_l, across_r = call(
        ffn_kernel,
        [wide(rows, width), wide(rows, 1), wide(1, width), low(rows, width), wide(rows, width), low(rows, width)] + [grad] * 4
        + [wide(5, width), wide(1, ff), low(rows, width), grad, low(4, 2, 48, n)],
        [low(rows, width), low(rows, ff), low(rows, ff), low(rows, width), low(rows, width), low(rows, width), low(rows, ff), column, grad, grad,
         wide(8, ff), wide(rows, width), low(rows, width), wide(rows, width), grad, grad, low(rows, width), weight, weight],
        mixed, part1, other1, small_s, vecs_t, cot_s, w_ul, w_ur, own_late,
        hbm_in=(5, 6, 7), hbm_out=(0, 3, 4, 6, 7), sems=((2, 4), (2, 4), (2, 2)) + line_sems + ((3,), (5,)), meeting=3)
    kinds = [fold_scratch(0, n)[1:], fold_scratch(1, n)[:1] + fold_scratch(1, n)[2:], fold_scratch(0, n), fold_scratch(1, n)]
    own = [wide(48, n)] * 2
    dqk, dvo, sums1, d_qkvb, gm, d_up, d_down = call(
        attn_bwd_fold_kernel,
        [grad, grad, wide(3, width), wide(1, 3 * half), low(rows, half), wide(48, ff), wide(48, ff)],
        sh["back_scratch"] + [column, low(rows, half), low(rows, half), low(rows, half)] + own
        + [wide(8, width), low(rows, half), low(rows, 3 * half), low(rows, width), weight, grad, grad] + sum(kinds, []),
        gr2, part3, other3, n1, r1, vecs_t, small_s, ctx, qkv, lse, mlow, w_qk, w_vo, ddl, ddr, dul, dur, first_l, across_r,
        hbm_in=(7, 8, 10, 11, 15, 16), sems=((2, 4, 6), (2, 2), (6,)), meeting=5)
    in_grad, d_conv, d_qk, d_vo, sums, d_me, got_out = call(
        conv_fold_kernel,
        [wide(rows, half), wide(TAPS * CG, half), wide(48, n), wide(48, n), wide(24, width), wide(8, half), low(rows, width)],
        [low(rows, sw), low(half, sw), low(blocks * CG, sw), wide(half, sw), column, column, eight, wide(1, half), wide(1, half),
         low(8, *seats, CG, TAPS * CG), low(8, 4, 2, CG, TAPS * CG), low(8, 4, 2, CG, TAPS * CG), low(8, 4, CG, TAPS * CG),
         low(8, 4, CG, TAPS * CG), low(8, 3, CG, TAPS * CG), wide(4, 24, width), wide(6, 24, width), wide(3, 8, half), wide(5, 8, half),
         low(*seats, half, TAPS * CG)] + fold_scratch(FOLD_KINDS[0], n) + fold_scratch(FOLD_KINDS[1], n),
        segment_ids, time_mask, xq, conv_full, slope, gm, dqk, dvo, sums2, sums1, d_qkvb, d_ub, stat_conv, stat_attn, out_s,
        hbm_in=(3, 14), hbm_out=(6,), sems=((2, 8), (2, 8), (2, 8, 3), (2, 2, 6), (2, 6), (2, 5), (2, 1), (1,)), meeting=6)
    line, shard = lambda size: ((size,), F32), wide(48, half)
    results = list(call(
        result_kernel,
        [low(rows, width), wide(rows, half), line(half), wide(TAPS * CG, half), line(half), shard, shard, shard, line(half), line(half), shard,
         line(width), line(width), line(width), wide(48, ff), line(ff), wide(48, ff), line(width), line(width), line(width), line(4)],
        [], out_s, got_out, in_grad, d_conv, d_qk, d_vo, d_up, d_down, sums, d_me, hbm_in=(0, 1, 2, 3, 6, 7), sems=((6,),)))
    results[0], results[1], results[10], results[16] = results[0][None], results[1][None], results[10].T, results[16].T
    return tuple(results)


def local_any(n_dp, hidden_in, segment_ids, time_mask, mask_embed, conv_weight, conv_bias, query_weight, key_weight,
          value_weight, query_bias, value_bias, out_weight, out_bias, first_gain, first_shift, up_weight, up_bias,
          down_weight, down_bias, second_gain, second_shift, cotangent):
    _, rows, width = hidden_in.shape
    ff = up_weight.shape[1]
    n = ff // 2
    sh = shapes(rows, width, ff)
    half, spread_width, blocks = sh["half"], sh["spread_width"], sh["blocks"]
    part = lax.axis_index("mp")
    core = lax.rem(lax.axis_index("dp"), 2)
    n_all = 2 * n_dp
    turn = flat_turn(n_all)
    sibling = [(f, f ^ 2) for f in range(n_all)]
    core_groups = [[f for f in range(n_all) if (f // 2) % 2 == c] for c in range(2)]
    swap = lambda v: lax.ppermute(v, BOTH, sibling)
    turned = lambda v: lax.ppermute(v, BOTH, turn)
    mine = part == core

    down_t = down_weight.T
    w_shards = [jnp.concatenate([query_weight, key_weight], axis=1), jnp.concatenate([value_weight, out_weight.T], axis=1),
                up_weight[:, :n], up_weight[:, n:], down_t[:, :n], down_t[:, n:]]
    conv_full = lax.all_gather(conv_weight, "dp", axis=0, tiled=True)
    conv_full = conv_full.reshape(blocks, TAPS * CG, half).swapaxes(1, 2)
    w_qk, w_vo, w_ul, w_ur, w_dl, w_dr = (
        lax.all_gather(turned(w), BOTH, axis=0, tiled=True, axis_index_groups=core_groups) for w in w_shards)
    bias = turned(jnp.concatenate([query_bias, value_bias, up_bias])[None])
    qb, vb, ub = (b.astype(F32) for b in (bias[:, :half], bias[:, half:2 * half], bias[:, 2 * half:]))
    row = one_row

    hid, cot = hidden_in[0], cotangent[0]
    small = jnp.concatenate([segment_ids, time_mask], axis=0)
    hid_s = jnp.where(mine, hid, swap(hid))
    cot_s = jnp.where(mine, cot, swap(cot))
    small_s = jnp.where(mine, small, swap(small))
    seg_c, mask_c = segment_ids.reshape(rows, 1), time_mask.reshape(rows, 1)
    seg_sr, seg_sc, mask_sc = small_s[0:1], small_s[0].reshape(rows, 1), small_s[1].reshape(rows, 1)

    masked = mask_c.astype(F32)
    hid_half = lax.dynamic_slice_in_dim(hid, part * half, half, 1).astype(F32)
    emb_half = lax.dynamic_slice_in_dim(mask_embed, part * half, half, 0).astype(F32)
    start_half = (hid_half + masked * (emb_half - hid_half)).astype(BF16)
    low, wide = lambda *s: (s, BF16), lambda *s: (s, F32)
    conv_low, conv_slope, xq = call(
        conv_fwd_kernel, [low(rows, half), wide(rows, half), low(half, spread_width)],
        [low(rows, spread_width), low(half // CG, TAPS * CG, spread_width), wide(half, spread_width)],
        seg_c, start_half, conv_full.reshape(4, 2, blocks // 8, half, TAPS * CG), row(conv_bias))
    conv_s = turned(conv_low)
    conv_o = swap(conv_s)
    c0, c1 = jnp.where(core == 0, conv_s, conv_o), jnp.where(core == 0, conv_o, conv_s)

    def attn_kernel(*refs):
        attn_fwd_kernel(*refs[:7], refs[7:9], *refs[9:])

    mixed, mlow, qkv, ctx, lse, part1, stat_conv = call(
        attn_kernel, sh["attn_out"] + [wide(1, half)], sh["attn_scratch"],
        hid_s, c0, c1, mask_sc, seg_sc, seg_sr, row(mask_embed), w_qk, w_vo, qb, vb)
    n1, r1, nlow, hidden, slope, part2, stat_attn = call(
        ffn_fwd_kernel, sh["ffn_out"], [],
        mixed, part1, swap(part1), seg_sc, row(out_bias), row(first_gain), row(first_shift), w_ul, w_ur, ub, w_dl, w_dr)
    out_s, gr2, part3, ddl, ddr, dul, dur, sums2, d_ub = call(
        ffn_bwd_kernel,
        [low(rows, width), wide(rows, width), low(rows, width)] + [low(width, n)] * 4 + [wide(5, width), wide(1, ff)],
        [low(rows, width), low(rows, ff)],
        n1, row(first_gain), row(first_shift), part2, swap(part2), seg_sc, row(down_bias), row(second_gain), row(second_shift), cot_s, nlow,
        hidden, slope, w_ul, w_ur, w_dl, w_dr)
    other_out = lax.ppermute(out_s, "mp", [(0, 1), (1, 0)])
    layer_out = jnp.where(mine, out_s, other_out)[None]
    own, send, dqk, dvo, sums1, d_qkvb = call(
        attn_bwd_plain_kernel,
        [wide(rows, half), low(rows, half), low(width, 2 * half), low(width, 2 * half), wide(3, width), wide(1, 3 * half)], sh["back_scratch"],
        gr2, part3, swap(part3), n1, r1, row(first_gain), seg_sc, seg_sr, ctx, qkv, lse, mlow, w_qk, w_vo)
    gm_half = turned((own + swap(send).astype(F32)).astype(BF16))
    d_conv, input_grad, d_cb, d_me = call(
        conv_bwd_kernel,
        [low(blocks, half, TAPS * CG), wide(rows, half), wide(1, half), wide(1, half)],
        [low(rows, spread_width), low(half, spread_width), low(blocks * CG, spread_width), wide(half, spread_width)],
        seg_c, xq, conv_full, conv_slope, gm_half, mask_c)

    d_wall = jnp.concatenate([dqk, dvo, dul, dur, ddl, ddr], axis=1)
    d_wall = turned(lax.psum_scatter(d_wall, BOTH, scatter_dimension=0, tiled=True, axis_index_groups=core_groups)).astype(F32)
    d_conv = lax.psum_scatter(d_conv.swapaxes(1, 2).reshape(blocks * TAPS * CG, half), "dp", scatter_dimension=0, tiled=True).astype(F32)
    once = (jnp.arange(width) // half == core).astype(F32)[None]
    put = lambda v, which: lax.dynamic_update_slice(jnp.zeros((1, 2 * v.shape[1]), F32), v, (0, which * v.shape[1]))
    full = jnp.concatenate([sums2, sums1, stat_attn], axis=0) * once
    pieces = [put(d_me, part), put(d_cb, part), put(d_qkvb[:, :half], core), put(d_qkvb[:, 2 * half:], core), put(d_ub, core)]
    stats = jnp.stack([jnp.sum(stat_conv) * 0.5, jnp.sum(full[8]), jnp.sum(full[0]), jnp.sum(full[1]), jnp.sum((seg_c != 0).astype(F32)) * 0.5])
    flat = jnp.concatenate([jnp.concatenate(pieces, axis=1)[0], full[2:8].reshape(-1), stats])
    flat = lax.psum(flat, BOTH)
    at = 0
    sections = []
    for size in (width, width, width, width, 2 * ff) + (width,) * 6 + (5,):
        sections.append(flat[at:at + size])
        at += size
    me, cb, dqb, dvb, dub, g2, s2, db, g1, s1, ob, st = sections
    half_of = lambda v: lax.dynamic_slice_in_dim(v, part * (v.shape[0] // 2), v.shape[0] // 2, 0)
    stream_rms = jnp.sqrt(st[:4] / (st[4] * width))
    q_, k_, v_, o_, u_, d_ = jnp.split(d_wall, [half, 2 * half, 3 * half, 4 * half, 4 * half + ff], axis=1)
    return (layer_out, input_grad[None], half_of(me), d_conv, half_of(cb), q_, k_, v_, half_of(dqb), half_of(dvb), o_.T, ob, g1, s1,
            u_, half_of(dub), d_.T, db, g2, s2, stream_rms)


def solution(mesh):
    split, half, turn = P("dp", "mp"), P("mp"), P("mp", "dp")
    whole = P()
    rows = P("dp", None, None)
    return jax.shard_map(
        local_close if mesh.shape["dp"] == 16 else functools.partial(local_any, mesh.shape["dp"]),
        mesh=mesh,
        in_specs=(rows, P("dp", None), P("dp", None), whole, split, half, split, split, split, half, half, turn, whole, whole, whole,
                  split, half, turn, whole, whole, whole, rows),
        out_specs=(rows, P("dp", None, "mp"), half, split, half, split, split, split, half, half, turn, whole, whole, whole,
                   split, half, turn, whole, whole, whole, whole),
        check_vma=False,
    )
```
